512 devices in a mesh: dp: 64 (over z, y), tensor: 8 (over x, core).
Axes of the slice: x: 4, y: 8, z: 8, core: 2. Of those that a mesh axis runs over, the one named last changes fastest.
Arguments:
- activations: bfloat16 [106496, 2560], P(('dp', 'tensor')), may hold values from -6 to 6
- key_grad: bfloat16 [106496, 1024], P('dp', 'tensor'), may hold values from -0.15625 to 0.15625
- momentum: float32 [64, 2560, 1024], P('dp', None, 'tensor'), may hold values from -6 to 6
- block_ids: int32 [64, 40, 16, 6], P('dp', None, 'tensor'), may hold values from 0 to 31, all different within a row
- counts: int32 [64], P('dp'), may hold values from 1 to 6, 192 in all
Outputs:
- new_momentum: float32 [64, 2560, 1024], P('dp', None, 'tensor')
- update: bfloat16 [2560, 1024], P(None, 'tensor')
The draws below stay inside these ranges and needn't reach their ends.
Inputs may be any that keep to these rules, and one draw needn't show every extreme that they name: Within one list block_ids[r, a, b, :] all numbers differ; every block number appears somewhere. `counts`: some replica sends 6 blocks for every span.
All inputs are finite; a program needn't handle non-finite values.
Results may differ from the reference program's by a relative error of at most 0.005.
Values may be sent and summed in bfloat16 or wider, within the bound.
No kernel may reach another device: no remote copies, remote signals or barrier semaphores. Data moves between devices by JAX's collectives and lax.ppermute only.
A program may use at most 64 MiB of HBM per device.

```python
import math
import jax
import jax.numpy as jnp
import numpy as np
from jax import lax

DW = 2560
KMAX = 6
BLK = 32
TOK_REP = 1664
REPLICAS = 64
SEQ_ALL = 106496
KCOL = 1024


def shard_levels(key, dims, shards, least, top_value):
    def one(dim, shards_of):
        heights = jax.random.uniform(jax.random.fold_in(jax.random.fold_in(key, 6), dim), (shards_of,), jnp.float32, least / len(shards), top_value / len(shards))
        return jnp.repeat(jnp.exp(heights), dims[dim] // shards_of).reshape((-1,) + (1,) * (len(dims) - dim - 1))

    level = one(*shards[0])
    for cut in shards[1:]:
        level = level * one(*cut)
    return level


def distinct(key, rows, count, top, lift):
    order = jax.random.permutation(jax.random.fold_in(key, 1), count)
    pull = order
    for power in range(3):
        pull = pull * pull // count
    pull = pull * lift // count
    tickets = jax.random.randint(jax.random.fold_in(key, 2), (rows, count), 0, 4096) + pull
    sure = jax.random.permutation(jax.random.fold_in(key, 3), rows)[jnp.arange(count) % rows]
    tickets = jnp.where(jnp.arange(rows)[:, None] == sure[None, :], 1 << 14, tickets)
    score = tickets * count + jnp.arange(count)
    return lax.top_k(score.astype(jnp.int32), top)[1].astype(jnp.int32)


def split_up(amount, total, most, skew):
    portions = [(1 << 20) // math.isqrt(standing ** skew) + 1 for standing in range(2, amount + 1)]
    surplus, holding = total - most - (amount - 1), [1] * (amount - 1)
    while surplus > 0:
        movable = [i for i in range(amount - 1) if holding[i] < most]
        pool, left = sum([portions[i] for i in movable]), surplus
        for i in movable:
            more = min(most - holding[i], max(1, left * portions[i] // pool), surplus)
            holding[i] = holding[i] + more
            surplus = surplus - more
    return np.array([most] + holding)


def uneven(key, number_of, total, limit, slope):
    if number_of == 2:
        one = jax.random.randint(key, (), max(1, total - limit), min(limit, total - 1) + 1)
        return jnp.stack([one, total - one])
    tallies = jnp.asarray(split_up(number_of, total, limit, slope), jnp.int32)
    twos = (number_of - 1) // 2
    donor, sink = tallies[1:1 + 2 * twos:2], tallies[2:2 + 2 * twos:2]
    slack = jnp.minimum(donor - 1, limit - sink)
    shifted = jax.random.randint(jax.random.fold_in(key, 1), (twos,), 0, 1 << 20) % (slack + 1)
    tallies = tallies.at[1:1 + 2 * twos:2].set(donor - shifted).at[2:2 + 2 * twos:2].set(sink + shifted)
    return tallies[jax.random.permutation(jax.random.fold_in(key, 2), number_of)]


def noise(own_key, extent, spread, reach, split=(), held_as=jnp.bfloat16):
    drawn = jax.random.normal(own_key, extent, jnp.float32) * spread
    if len(split) > 0:
        drawn = shard_levels(own_key, extent, split, -0.22, 0.18) * drawn
    return jnp.clip(drawn, min=-reach, max=reach).astype(held_as)


def setup_inputs(seed: int = 0) -> dict:
    keys = jax.random.split(jax.random.key(seed), 6)
    return {
        "activations": noise(keys[0], (SEQ_ALL, DW), 1.0, 6.0, ((0, 512),)),
        "key_grad": noise(keys[1], (SEQ_ALL, KCOL), TOK_REP ** -0.5, 0.15625, ((0, 64), (1, 8))),
        "momentum": noise(keys[2], (REPLICAS, DW, KCOL), 1.0, 6.0, ((0, 64), (2, 8)), jnp.float32),
        "block_ids": distinct(keys[3], REPLICAS * (DW // 64) * (KCOL // 64), BLK, KMAX, 0).reshape((REPLICAS, DW // 64, KCOL // 64, KMAX)),
        "counts": uneven(keys[4], REPLICAS, REPLICAS * KMAX // 2, KMAX, 2).astype(jnp.int32),
    }


def cosine_table():
    positions = jnp.arange(64, dtype=jnp.float32)
    freq = positions[:, None]
    angles = jnp.pi * (2.0 * positions[None, :] + 1.0) * freq / 128.0
    matrix = jnp.cos(angles) * jnp.sqrt(2.0 / 64.0)
    return jnp.where(freq == 0.0, matrix * jnp.sqrt(0.5), matrix)

def forward(cosines, matrix):
    return jnp.einsum('ij,ajbc,lc->aibl', cosines, matrix, cosines, precision=lax.Precision.HIGHEST)

def inverse(cosines, spectrum):
    return jnp.einsum('ij,aibl,lc->ajbc', cosines, spectrum, cosines, precision=lax.Precision.HIGHEST)

def reference(activations, key_grad, momentum, block_ids, counts):
    cosines = cosine_table()
    row_spans = DW // 64
    col_spans = KCOL // 64
    numbers = jnp.arange(BLK, dtype=jnp.int32)

    def replica_step(running, replica):
        token_rows = lax.dynamic_slice_in_dim(activations, (replica * TOK_REP).astype(jnp.int32), TOK_REP, 0)
        key_rows = lax.dynamic_slice_in_dim(key_grad, (replica * TOK_REP).astype(jnp.int32), TOK_REP, 0)
        gradient = lax.dot_general(token_rows, key_rows, (((0,), (0,)), ((), ())), preferred_element_type=jnp.float32)
        advanced = 0.999 * momentum[replica] + gradient
        spectrum = forward(cosines, advanced.reshape(row_spans, 64, col_spans, 64))
        blocks = spectrum.reshape(row_spans, BLK, 2, col_spans, 64)
        active = (jnp.arange(KMAX, dtype=jnp.int32) < counts[replica]).astype(jnp.float32)
        onehot = (block_ids[replica][..., None] == numbers).astype(jnp.float32) * active[:, None]
        outgoing = jnp.einsum('abkj,ajrbc->abkrc', onehot, blocks, precision=lax.Precision.HIGHEST).astype(jnp.bfloat16)
        chosen = lax.optimization_barrier(jnp.sum(onehot, axis=2))
        kept_out = blocks * jnp.transpose(chosen, (0, 2, 1))[:, :, None, :, None]
        removed = inverse(cosines, kept_out.reshape(row_spans, 64, col_spans, 64))
        momentum_next = advanced - removed.reshape(DW, KCOL)
        contribution = jnp.einsum('abkj,abkrc->ajrbc', onehot, outgoing.astype(jnp.float32), precision=lax.Precision.HIGHEST)
        return (running + contribution, momentum_next)
    start = jnp.zeros((row_spans, BLK, 2, col_spans, 64), jnp.float32)
    summed, new_momentum = lax.scan(replica_step, start, jnp.arange(REPLICAS, dtype=jnp.int32))
    update = inverse(cosines, summed.reshape(row_spans, 64, col_spans, 64)).reshape(DW, KCOL).astype(jnp.bfloat16)
    return (new_momentum, update)
```

```python
import functools

import jax
import jax.numpy as jnp
import ml_dtypes
import numpy as np
from jax import lax
from jax.experimental import pallas as pl
from jax.experimental.pallas import tpu as pltpu
from jax.sharding import PartitionSpec as P

BLK = 32
CHUNK = 256


def cosine_parts():
    n = np.arange(64, dtype=np.float64)
    c = np.cos(np.pi * (2.0 * n[None, :] + 1.0) * n[:, None] / 128.0) * np.sqrt(2.0 / 64.0)
    c[0] *= np.sqrt(0.5)
    table = np.kron(np.eye(CHUNK // 64), c)
    high = table.astype(ml_dtypes.bfloat16)
    low = (table - high.astype(np.float64)).astype(ml_dtypes.bfloat16)
    return high, low


def dot(a, b):
    return jnp.dot(a, b, preferred_element_type=jnp.float32)


def split(x):
    high = x.astype(jnp.bfloat16)
    return high, (x - high.astype(jnp.float32)).astype(jnp.bfloat16)


def step_kernel(grad, other, momentum, mask, ch, cl, th, tl, sent, kept):
    def body(i, _):
        rows = pl.ds(pl.multiple_of(i * CHUNK, CHUNK), CHUNK)
        x = 0.999 * momentum[rows, :] + grad[rows, :] + other[rows, :].astype(jnp.float32)
        xh, xl = split(x)
        s = (dot(ch[...], xh) + (dot(ch[...], xl) + dot(cl[...], xh))) * mask[rows, :]
        sh, sl = split(s)
        sent[rows, :] = sh
        kept[rows, :] = x - (dot(th[...], sh) + (dot(th[...], sl) + dot(tl[...], sh)))
        return 0

    lax.fori_loop(0, grad.shape[0] // CHUNK, body, 0, unroll=True)


def inverse_kernel(summed, th, tl, update):
    def body(i, _):
        rows = pl.ds(pl.multiple_of(i * CHUNK, CHUNK), CHUNK)
        s = summed[rows, :]
        update[rows, :] = (dot(th[...], s) + dot(tl[...], s)).astype(jnp.bfloat16)
        return 0

    lax.fori_loop(0, update.shape[0] // CHUNK, body, 0, unroll=True)


def gram(a, k):
    return lax.dot_general(a, k, (((0,), (0,)), ((), ())), preferred_element_type=jnp.float32)


def shards(activations, key_grad, momentum, block_ids, counts, *, replicas, group):
    tokens, features = activations.shape
    cols = key_grad.shape[1]
    chips = group // 2
    spot = lax.axis_index("tensor")
    chip, core = spot // 2, spot % 2

    def along(x, step):
        return lax.ppermute(x, "tensor", [(i, (i + 2 * step) % group) for i in range(group)])

    def swap(x):
        return lax.ppermute(x, "tensor", [(i, i ^ 1) for i in range(group)])

    ch, cl = cosine_parts()
    th, tl = jnp.asarray(ch.T), jnp.asarray(cl.T)
    ch, cl = jnp.asarray(ch), jnp.asarray(cl)

    by_core = key_grad.reshape(chips, 2, tokens, cols)
    own = lax.dynamic_index_in_dim(by_core, core, 1, keepdims=False)
    theirs = swap(lax.dynamic_index_in_dim(by_core, 1 - core, 1, keepdims=False))
    keys = jnp.concatenate([own, theirs], axis=2)

    def keys_of(step):
        return lax.dynamic_index_in_dim(keys, (chip + step) % chips, 0, keepdims=False)

    cut = tokens // 2 // 16 * 16
    left = along(activations, 1)
    right = along(activations, -1)
    far_a = along(left[:cut], 1)
    far_b = along(right[cut:], -1)
    total = gram(activations, keys_of(0)) + gram(left, keys_of(-1)) + gram(right, keys_of(1))
    far_keys = keys_of(2)
    total = total + gram(far_a, far_keys[:cut]) + gram(far_b, far_keys[cut:])
    other = swap(total[:, cols:].astype(jnp.bfloat16))

    active = jnp.arange(block_ids.shape[3], dtype=jnp.int32) < counts[0]
    hit = (block_ids[0][..., None] == jnp.arange(BLK, dtype=jnp.int32)) & active[:, None]
    chosen = jnp.transpose(jnp.any(hit, axis=2), (0, 2, 1)).astype(jnp.float32)
    mask = jnp.broadcast_to(
        chosen[:, :, None, :, None], (features // 64, BLK, 2, cols // 64, 64)
    ).reshape(features, cols)

    vmem = pl.BlockSpec(memory_space=pltpu.VMEM)
    sent, kept = pl.pallas_call(
        step_kernel,
        out_shape=(
            jax.ShapeDtypeStruct((features, cols), jnp.bfloat16),
            jax.ShapeDtypeStruct((features, cols), jnp.float32),
        ),
        in_specs=[vmem] * 8,
        out_specs=(vmem, vmem),
        compiler_params=pltpu.CompilerParams(vmem_limit_bytes=32 << 20),
        name="step",
    )(total[:, :cols], other, momentum[0], mask, ch, cl, th, tl)

    pieces = lax.all_to_all(
        sent.reshape(replicas, features // replicas, cols), "dp", 0, 0, tiled=True
    )
    mine = jnp.sum(pieces.astype(jnp.float32), axis=0).astype(jnp.bfloat16)
    summed = lax.all_to_all(
        jnp.broadcast_to(mine[None], (replicas,) + mine.shape), "dp", 0, 0, tiled=True
    ).reshape(features, cols)
    update = pl.pallas_call(
        inverse_kernel,
        out_shape=jax.ShapeDtypeStruct((features, cols), jnp.bfloat16),
        in_specs=[vmem] * 3,
        out_specs=vmem,
        compiler_params=pltpu.CompilerParams(vmem_limit_bytes=32 << 20),
        name="inverse",
    )(summed, th, tl)
    return kept[None], update


def solution(mesh):
    in_specs = (
        P(("dp", "tensor"), None),
        P("dp", "tensor"),
        P("dp", None, "tensor"),
        P("dp", None, "tensor", None),
        P("dp"),
    )
    out_specs = (P("dp", None, "tensor"), P(None, "tensor"))
    body = functools.partial(shards, replicas=mesh.shape["dp"], group=mesh.shape["tensor"])
    return jax.shard_map(body, mesh=mesh, in_specs=in_specs, out_specs=out_specs, check_vma=False)
```

```python
import functools

import jax
import jax.numpy as jnp
import ml_dtypes
import numpy as np
from jax import lax
from jax.experimental import pallas as pl
from jax.experimental.pallas import tpu as pltpu
from jax.sharding import PartitionSpec as P

BLK = 32
SPAN = 64
WIDE = 4


def cosine_parts():
    n = np.arange(SPAN, dtype=np.float64)
    table = np.cos(np.pi * (2.0 * n[None, :] + 1.0) * n[:, None] / 128.0) * np.sqrt(2.0 / SPAN)
    table[0] *= np.sqrt(0.5)
    high = table.astype(ml_dtypes.bfloat16)
    low = (table - high.astype(np.float64)).astype(ml_dtypes.bfloat16)
    return high, low


def split(x):
    high = x.astype(jnp.bfloat16)
    return high, (x - high.astype(jnp.float32)).astype(jnp.bfloat16)


def spans_of(ref, i, count):
    first = i * count * SPAN
    return [ref[first + s * SPAN : first + (s + 1) * SPAN, :] for s in range(count)]


def beside(parts):
    return jnp.concatenate(parts, axis=1)


def product(table, parts):
    return jnp.dot(table[...], jnp.concatenate(parts, axis=0), preferred_element_type=jnp.float32)


def put(ref, i, count, value):
    cols = ref.shape[1]
    for s in range(count):
        first = (i * count + s) * SPAN
        ref[first : first + SPAN, :] = value[:, s * cols : (s + 1) * cols].astype(ref.dtype)


def spectrum_kernel(grad, other, momentum, mask, forward, advanced, sent, rows):
    for i in range(grad.shape[0] // (SPAN * WIDE)):
        x = beside(
            [
                0.999 * m + g + o.astype(jnp.float32)
                for m, g, o in zip(
                    spans_of(momentum, i, WIDE),
                    spans_of(grad, i, WIDE),
                    spans_of(other, i, WIDE),
                )
            ]
        )
        high, low = split(x)
        s = product(forward, [high, low, high]) * beside(spans_of(mask, i, WIDE))
        put(sent, i, WIDE, s)
        put(advanced, i, WIDE, x)
        put(rows, i, WIDE, s)


def kept_kernel(advanced, rows, backward, kept):
    for i in range(kept.shape[0] // (SPAN * WIDE)):
        high, low = split(beside(spans_of(rows, i, WIDE)))
        x = beside(spans_of(advanced, i, WIDE))
        put(kept, i, WIDE, x - product(backward, [high, low, high]))


def total_kernel(pieces, totals):
    total = pieces[0].astype(jnp.float32)
    for r in range(1, pieces.shape[0]):
        total = total + pieces[r].astype(jnp.float32)
    total = total.astype(totals.dtype)
    for r in range(totals.shape[0]):
        totals[r] = total


def inverse_kernel(summed, backward, update):
    for i in range(update.shape[0] // (SPAN * WIDE)):
        s = beside(spans_of(summed, i, WIDE))
        put(update, i, WIDE, product(backward, [s, s]))


def gram(a, k):
    return lax.dot_general(a, k, (((0,), (0,)), ((), ())), preferred_element_type=jnp.float32)


def call(kernel, name, out_shape, *args):
    vmem = pl.BlockSpec(memory_space=pltpu.VMEM)
    outs = out_shape if isinstance(out_shape, tuple) else (out_shape,)
    moved = sum(x.size * x.dtype.itemsize for x in args + outs)
    return pl.pallas_call(
        kernel,
        out_shape=out_shape,
        in_specs=[vmem] * len(args),
        out_specs=jax.tree.map(lambda _: vmem, out_shape),
        compiler_params=pltpu.CompilerParams(vmem_limit_bytes=40 << 20),
        cost_estimate=pl.CostEstimate(
            flops=6 * 2 * SPAN * outs[0].size, bytes_accessed=moved, transcendentals=0
        ),
        name=name,
    )(*args)


def shards(activations, key_grad, momentum, block_ids, counts, *, replicas, group):
    tokens, features = activations.shape
    cols = key_grad.shape[1]
    chips = group // 2
    spot = lax.axis_index("tensor")
    chip, core = lax.shift_right_logical(spot, 1), lax.bitwise_and(spot, 1)

    def along(x, step):
        return lax.ppermute(x, "tensor", [(i, (i + 2 * step) % group) for i in range(group)])

    def swap(x):
        return lax.ppermute(x, "tensor", [(i, i ^ 1) for i in range(group)])

    cut = tokens // 2 // 16 * 16
    head, tail = activations[:cut], activations[cut:]
    left_head, right_tail = along(head, 1), along(tail, -1)

    by_core = key_grad.reshape(chips, 2, tokens, cols)
    own_keys = lax.dynamic_index_in_dim(by_core, core, 1, keepdims=False)
    their_keys = swap(lax.dynamic_index_in_dim(by_core, 1 - core, 1, keepdims=False))

    head, tail, their_keys = lax.optimization_barrier((head, tail, their_keys))
    left_tail, right_head = along(tail, 1), along(head, -1)
    far_head, far_tail = along(left_head, 1), along(right_tail, -1)

    def block(keys, step):
        return lax.dynamic_index_in_dim(
            keys, lax.bitwise_and(chip + step, chips - 1), 0, keepdims=False
        )

    def near(keys):
        total = gram(activations, block(keys, 0))
        before, after = block(keys, chips - 1), block(keys, 1)
        return (
            total
            + gram(left_head, before[:cut])
            + gram(right_tail, after[cut:])
            + gram(left_tail, before[cut:])
            + gram(right_head, after[:cut])
        )

    def whole(total, keys):
        far = block(keys, 2)
        return total + gram(far_head, far[:cut]) + gram(far_tail, far[cut:])

    active = jnp.arange(block_ids.shape[3], dtype=jnp.int32) < counts[0]
    hit = (block_ids[0][..., None] == jnp.arange(BLK, dtype=jnp.int32)) & active[:, None]
    chosen = jnp.transpose(jnp.any(hit, axis=2), (0, 2, 1)).astype(jnp.float32)
    mask = jnp.broadcast_to(
        chosen[:, :, None, :, None], (features // SPAN, BLK, 2, cols // SPAN, SPAN)
    ).reshape(features, cols)

    their_near, own_near = near(their_keys), near(own_keys)
    their_near, own_near, mask, far_head, far_tail = lax.optimization_barrier(
        (their_near, own_near, mask, far_head, far_tail)
    )
    other = swap(whole(their_near, their_keys).astype(jnp.bfloat16))
    grad = whole(own_near, own_keys)

    high, low = cosine_parts()
    forward = jnp.asarray(np.concatenate([high, high, low], axis=1))
    backward = jnp.asarray(np.concatenate([high.T, high.T, low.T], axis=1))
    backward_once = jnp.asarray(np.concatenate([high.T, low.T], axis=1))

    flat = jax.ShapeDtypeStruct((features, cols), jnp.float32)
    flat_half = jax.ShapeDtypeStruct((features, cols), jnp.bfloat16)
    advanced, sent, rows = call(
        spectrum_kernel,
        "spectrum",
        (flat, flat_half, flat),
        grad,
        other,
        momentum[0],
        mask,
        forward,
    )
    pieces = lax.all_to_all(
        sent.reshape(replicas, features // replicas, cols), "dp", 0, 0, tiled=True
    )
    kept = call(kept_kernel, "kept", flat, advanced, rows, backward)
    totals = call(
        total_kernel, "total", jax.ShapeDtypeStruct(pieces.shape, jnp.bfloat16), pieces
    )
    summed = lax.all_to_all(totals, "dp", 0, 0, tiled=True).reshape(features, cols)
    update = call(inverse_kernel, "inverse", flat_half, summed, backward_once)
    return kept[None], update


def solution(mesh):
    in_specs = (
        P(("dp", "tensor"), None),
        P("dp", "tensor"),
        P("dp", None, "tensor"),
        P("dp", None, "tensor", None),
        P("dp"),
    )
    out_specs = (P("dp", None, "tensor"), P(None, "tensor"))
    body = functools.partial(shards, replicas=mesh.shape["dp"], group=mesh.shape["tensor"])
    return jax.shard_map(body, mesh=mesh, in_specs=in_specs, out_specs=out_specs, check_vma=False)
```

```python
import functools

import jax
import jax.numpy as jnp
import ml_dtypes
import numpy as np
from jax import lax
from jax.experimental import pallas as pl
from jax.experimental.pallas import tpu as pltpu
from jax.sharding import PartitionSpec as P

BLK = 32
SPAN = 64
WIDE = 4


def cosine_parts():
    n = np.arange(SPAN, dtype=np.float64)
    table = np.cos(np.pi * (2.0 * n[None, :] + 1.0) * n[:, None] / 128.0) * np.sqrt(2.0 / SPAN)
    table[0] *= np.sqrt(0.5)
    high = table.astype(ml_dtypes.bfloat16)
    low = (table - high.astype(np.float64)).astype(ml_dtypes.bfloat16)
    return high, low


def split(x):
    high = x.astype(jnp.bfloat16)
    return high, (x - high.astype(jnp.float32)).astype(jnp.bfloat16)


def spans_of(ref, i, count):
    first = i * count * SPAN
    return [ref[first + s * SPAN : first + (s + 1) * SPAN, :] for s in range(count)]


def beside(parts):
    return jnp.concatenate(parts, axis=1)


def product(table, parts):
    return jnp.dot(table[...], jnp.concatenate(parts, axis=0), preferred_element_type=jnp.float32)


def put(ref, i, count, value):
    cols = ref.shape[1]
    for s in range(count):
        first = (i * count + s) * SPAN
        ref[first : first + SPAN, :] = value[:, s * cols : (s + 1) * cols].astype(ref.dtype)


def spectrum_kernel(part, other, mask, forward, advanced, sent, rows):
    for i in range(part.shape[0] // (SPAN * WIDE)):
        x = beside(
            [
                p + o.astype(jnp.float32)
                for p, o in zip(spans_of(part, i, WIDE), spans_of(other, i, WIDE))
            ]
        )
        high, low = split(x)
        s = product(forward, [high, low, high]) * beside(spans_of(mask, i, WIDE))
        put(sent, i, WIDE, s)
        put(advanced, i, WIDE, x)
        put(rows, i, WIDE, s)


def kept_kernel(advanced, rows, backward, kept):
    for i in range(kept.shape[0] // (SPAN * WIDE)):
        high, low = split(beside(spans_of(rows, i, WIDE)))
        x = beside(spans_of(advanced, i, WIDE))
        put(kept, i, WIDE, x - product(backward, [high, low, high]))


def total_kernel(pieces, totals):
    total = pieces[0].astype(jnp.float32)
    for r in range(1, pieces.shape[0]):
        total = total + pieces[r].astype(jnp.float32)
    total = total.astype(totals.dtype)
    for r in range(totals.shape[0]):
        totals[r] = total


def inverse_kernel(summed, backward, update):
    for i in range(update.shape[0] // (SPAN * WIDE)):
        s = beside(spans_of(summed, i, WIDE))
        put(update, i, WIDE, product(backward, [s, s]))


def gram(a, k):
    return lax.dot_general(a, k, (((0,), (0,)), ((), ())), preferred_element_type=jnp.float32)


def call(kernel, name, out_shape, *args):
    vmem = pl.BlockSpec(memory_space=pltpu.VMEM)
    outs = out_shape if isinstance(out_shape, tuple) else (out_shape,)
    moved = sum(x.size * x.dtype.itemsize for x in args + outs)
    return pl.pallas_call(
        kernel,
        out_shape=out_shape,
        in_specs=[vmem] * len(args),
        out_specs=jax.tree.map(lambda _: vmem, out_shape),
        compiler_params=pltpu.CompilerParams(vmem_limit_bytes=10 << 20),
        cost_estimate=pl.CostEstimate(
            flops=6 * 2 * SPAN * outs[0].size, bytes_accessed=moved, transcendentals=0
        ),
        name=name,
    )(*args)


def shards(activations, key_grad, momentum, block_ids, counts, *, replicas, group):
    tokens, features = activations.shape
    cols = key_grad.shape[1]
    chips = group // 2
    spot = lax.axis_index("tensor")
    chip, core = lax.shift_right_logical(spot, 1), lax.bitwise_and(spot, 1)

    def along(x, step):
        return lax.ppermute(x, "tensor", [(i, (i + 2 * step) % group) for i in range(group)])

    def swap(x):
        return lax.ppermute(x, "tensor", [(i, i ^ 1) for i in range(group)])

    cut = tokens // 2 // 16 * 16
    head, tail = activations[:cut], activations[cut:]
    left_head, right_tail = along(head, 1), along(tail, -1)

    by_core = key_grad.reshape(chips, 2, tokens, cols)

    def keys_for(which):
        rows = lax.dynamic_index_in_dim(by_core, which, 1, keepdims=False)
        return lax.dynamic_slice_in_dim(jnp.concatenate([rows, rows]), chip, chips, 0)

    their_keys = swap(keys_for(1 - core))

    base = momentum[0]
    head, tail, their_keys, key_grad, block_ids, counts, base, block = lax.optimization_barrier(
        (head, tail, their_keys, key_grad, block_ids, counts, base, activations)
    )
    left_tail, right_head = along(tail, 1), along(head, -1)
    far_head, far_tail = along(left_head, 1), along(right_tail, -1)

    by_core = key_grad.reshape(chips, 2, tokens, cols)
    own_keys = lax.optimization_barrier(keys_for(core))

    def near(keys, total):
        before, after = keys[chips - 1], keys[1]
        return (
            total
            + gram(block, keys[0])
            + gram(left_head, before[:cut])
            + gram(right_tail, after[cut:])
            + gram(left_tail, before[cut:])
            + gram(right_head, after[:cut])
        )

    def whole(total, keys):
        return total + gram(far_head, keys[2][:cut]) + gram(far_tail, keys[2][cut:])

    active = jnp.arange(block_ids.shape[3], dtype=jnp.int32) < counts[0]
    hit = (block_ids[0][..., None] == jnp.arange(BLK, dtype=jnp.int32)) & active[:, None]
    chosen = jnp.transpose(jnp.any(hit, axis=2), (0, 2, 1)).astype(jnp.float32)
    mask = jnp.broadcast_to(
        chosen[:, :, None, :, None], (features // SPAN, BLK, 2, cols // SPAN, SPAN)
    ).reshape(features, cols)

    their_near, own_near = near(their_keys, 0.0), near(own_keys, 0.999 * base)
    their_near, own_near, mask, far_head, far_tail = lax.optimization_barrier(
        (their_near, own_near, mask, far_head, far_tail)
    )
    other = swap(whole(their_near, their_keys).astype(jnp.bfloat16))
    part = whole(own_near, own_keys)

    high, low = cosine_parts()
    forward = jnp.asarray(np.concatenate([high, high, low], axis=1))
    backward = jnp.asarray(np.concatenate([high.T, high.T, low.T], axis=1))
    backward_once = jnp.asarray(np.concatenate([high.T, low.T], axis=1))

    flat = jax.ShapeDtypeStruct((features, cols), jnp.float32)
    flat_half = jax.ShapeDtypeStruct((features, cols), jnp.bfloat16)
    advanced, sent, rows = call(
        spectrum_kernel,
        "spectrum",
        (flat, flat_half, flat),
        part,
        other,
        mask,
        forward,
    )
    pieces = lax.all_to_all(
        sent.reshape(replicas, features // replicas, cols), "dp", 0, 0, tiled=True
    )
    kept = call(kept_kernel, "kept", flat, advanced, rows, backward)
    totals = call(
        total_kernel, "total", jax.ShapeDtypeStruct(pieces.shape, jnp.bfloat16), pieces
    )
    summed = lax.all_to_all(totals, "dp", 0, 0, tiled=True).reshape(features, cols)
    update = call(inverse_kernel, "inverse", flat_half, summed, backward_once)
    return kept[None], update


def solution(mesh):
    in_specs = (
        P(("dp", "tensor"), None),
        P("dp", "tensor"),
        P("dp", None, "tensor"),
        P("dp", None, "tensor", None),
        P("dp"),
    )
    out_specs = (P("dp", None, "tensor"), P(None, "tensor"))
    body = functools.partial(shards, replicas=mesh.shape["dp"], group=mesh.shape["tensor"])
    return jax.shard_map(body, mesh=mesh, in_specs=in_specs, out_specs=out_specs, check_vma=False)
```

```python
import functools

import jax
import jax.numpy as jnp
import ml_dtypes
import numpy as np
from jax import lax
from jax.experimental import pallas as pl
from jax.experimental.pallas import tpu as pltpu
from jax.sharding import PartitionSpec as P

BLK = 32
SPAN = 64
WIDE = 4


def cosine_parts():
    n = np.arange(SPAN, dtype=np.float64)
    table = np.cos(np.pi * (2.0 * n[None, :] + 1.0) * n[:, None] / 128.0) * np.sqrt(2.0 / SPAN)
    table[0] *= np.sqrt(0.5)
    high = table.astype(ml_dtypes.bfloat16)
    low = (table - high.astype(np.float64)).astype(ml_dtypes.bfloat16)
    return high, low


def split(x):
    high = x.astype(jnp.bfloat16)
    return high, (x - high.astype(jnp.float32)).astype(jnp.bfloat16)


def spans_of(ref, i, count):
    first = i * count * SPAN
    return [ref[first + s * SPAN : first + (s + 1) * SPAN, :] for s in range(count)]


def beside(parts):
    return jnp.concatenate(parts, axis=1)


def product(table, parts):
    return jnp.dot(table[...], jnp.concatenate(parts, axis=0), preferred_element_type=jnp.float32)


def put(ref, i, count, value):
    cols = ref.shape[1]
    for s in range(count):
        first = (i * count + s) * SPAN
        ref[first : first + SPAN, :] = value[:, s * cols : (s + 1) * cols].astype(ref.dtype)


def mask_kernel(ids, count, mask):
    shape = (SPAN, mask.shape[1])
    block = lax.shift_right_logical(lax.broadcasted_iota(jnp.int32, shape, 0), 1)
    first = lax.broadcasted_iota(jnp.int32, shape, 1) < SPAN
    most = ids.shape[0] * SPAN // (2 * mask.shape[0])

    def body(a, _):
        hit = jnp.zeros(shape, jnp.bool_)
        for k in range(most):
            active = k < count[0]
            one = jnp.where(active, ids[2 * most * a + k], -1)
            two = jnp.where(active, ids[2 * most * a + most + k], -1)
            hit = hit | (jnp.where(first, one, two) == block)
        rows = pl.ds(pl.multiple_of(a * SPAN, SPAN), SPAN)
        mask[rows, :] = hit.astype(jnp.float32).astype(mask.dtype)
        return 0

    lax.fori_loop(0, mask.shape[0] // SPAN, body, 0)


def chosen_rows(x, mask, forward, i):
    high, low = split(x)
    keep = beside(spans_of(mask, i, WIDE)).astype(jnp.float32)
    return product(forward, [high, low, high]) * keep


def spectrum_kernel(part, other, mask, forward, advanced, sent, held, done):
    copies = []
    for i in range(part.shape[0] // (SPAN * WIDE)):
        x = beside(
            [
                p + o.astype(jnp.float32)
                for p, o in zip(spans_of(part, i, WIDE), spans_of(other, i, WIDE))
            ]
        )
        put(held, i, WIDE, x)
        rows = pl.ds(i * WIDE * SPAN, WIDE * SPAN)
        copies.append(pltpu.make_async_copy(held.at[rows], advanced.at[rows], done.at[i]))
        copies[-1].start()
        put(sent, i, WIDE, chosen_rows(x, mask, forward, i))
    for copy in copies:
        copy.wait()


def kept_kernel(advanced, mask, forward, backward, kept):
    for i in range(kept.shape[0] // (SPAN * WIDE)):
        x = beside(spans_of(advanced, i, WIDE))
        high, low = split(chosen_rows(x, mask, forward, i))
        put(kept, i, WIDE, x - product(backward, [high, low, high]))


def total_kernel(pieces, totals):
    total = pieces[0].astype(jnp.float32)
    for r in range(1, pieces.shape[0]):
        total = total + pieces[r].astype(jnp.float32)
    total = total.astype(totals.dtype)
    for r in range(totals.shape[0]):
        totals[r] = total


def inverse_kernel(summed, backward, update):
    for i in range(update.shape[0] // (SPAN * WIDE)):
        s = beside(spans_of(summed, i, WIDE))
        put(update, i, WIDE, product(backward, [s, s]))


def gram(a, k):
    return lax.dot_general(a, k, (((0,), (0,)), ((), ())), preferred_element_type=jnp.float32)


VMEM, SMEM, ANY = (
    pl.BlockSpec(memory_space=space) for space in (pltpu.VMEM, pltpu.SMEM, pl.ANY)
)


def call(kernel, name, outs, *args, places=None, out_places=None, scratch=()):
    moved = sum(x.size * x.dtype.itemsize for x in args + outs)
    return pl.pallas_call(
        kernel,
        out_shape=outs,
        in_specs=places or [VMEM] * len(args),
        out_specs=out_places or (VMEM,) * len(outs),
        scratch_shapes=scratch,
        compiler_params=pltpu.CompilerParams(vmem_limit_bytes=10 << 20),
        cost_estimate=pl.CostEstimate(
            flops=6 * 2 * SPAN * outs[0].size, bytes_accessed=moved, transcendentals=0
        ),
        name=name,
    )(*args)


def shards(activations, key_grad, momentum, block_ids, counts, *, replicas, group):
    tokens, features = activations.shape
    cols = key_grad.shape[1]
    chips = group // 2
    spot = lax.axis_index("tensor")
    chip, core = lax.shift_right_logical(spot, 1), lax.bitwise_and(spot, 1)

    def along(x, step):
        return lax.ppermute(x, "tensor", [(i, (i + 2 * step) % group) for i in range(group)])

    def swap(x):
        return lax.ppermute(x, "tensor", [(i, i ^ 1) for i in range(group)])

    cut = tokens // 2 // 16 * 16
    head, tail = activations[:cut], activations[cut:]
    left_head, right_tail = along(head, 1), along(tail, -1)

    by_core = key_grad.reshape(chips, 2, tokens, cols)

    def keys_for(which):
        rows = lax.dynamic_index_in_dim(by_core, which, 1, keepdims=False)
        return lax.dynamic_slice_in_dim(jnp.concatenate([rows, rows]), chip, chips, 0)

    their_keys = swap(keys_for(1 - core))

    head, tail, their_keys = lax.optimization_barrier((head, tail, their_keys))
    left_tail, right_head = along(tail, 1), along(head, -1)

    (left_head, right_tail, block, key_grad, block_ids, counts, momentum) = (
        lax.optimization_barrier(
            (left_head, right_tail, activations, key_grad, block_ids, counts, momentum)
        )
    )
    far_head, far_tail = along(left_head, 1), along(right_tail, -1)

    by_core = key_grad.reshape(chips, 2, tokens, cols)
    own_keys = keys_for(core)
    keys = lax.optimization_barrier(jnp.concatenate([own_keys, their_keys], axis=2))
    before, after = keys[chips - 1], keys[1]
    near = (
        gram(block, keys[0])
        + gram(left_head, before[:cut])
        + gram(right_tail, after[cut:])
        + gram(left_tail, before[cut:])
        + gram(right_head, after[:cut])
    )
    own_near = near[:, :cols] + 0.999 * momentum[0]
    their_near = near[:, cols:]
    own_far, their_far = own_keys[2], their_keys[2]

    def whole(total, far):
        return total + gram(far_head, far[:cut]) + gram(far_tail, far[cut:])

    flat = jax.ShapeDtypeStruct((features, cols), jnp.float32)
    flat_half = jax.ShapeDtypeStruct((features, cols), jnp.bfloat16)
    (mask,) = call(
        mask_kernel, "mask", (flat_half,), block_ids.reshape(-1), counts, places=[SMEM, SMEM]
    )

    (own_near, their_near, own_far, their_far, mask, far_head, far_tail) = (
        lax.optimization_barrier(
            (own_near, their_near, own_far, their_far, mask, far_head, far_tail)
        )
    )
    other = swap(whole(their_near, their_far).astype(jnp.bfloat16))
    part = whole(own_near, own_far)

    high, low = cosine_parts()
    forward = jnp.asarray(np.concatenate([high, high, low], axis=1))
    backward = jnp.asarray(np.concatenate([high.T, high.T, low.T], axis=1))
    backward_once = jnp.asarray(np.concatenate([high.T, low.T], axis=1))

    advanced, sent = call(
        spectrum_kernel,
        "spectrum",
        (flat, flat_half),
        part,
        other,
        mask,
        forward,
        out_places=(ANY, VMEM),
        scratch=(
            pltpu.VMEM(flat.shape, jnp.float32),
            pltpu.SemaphoreType.DMA((features // (SPAN * WIDE),)),
        ),
    )
    pieces = lax.all_to_all(
        sent.reshape(replicas, features // replicas, cols), "dp", 0, 0, tiled=True
    )
    (kept,) = call(kept_kernel, "kept", (flat,), advanced, mask, forward, backward)
    (totals,) = call(
        total_kernel, "total", (jax.ShapeDtypeStruct(pieces.shape, jnp.bfloat16),), pieces
    )
    summed = lax.all_to_all(totals, "dp", 0, 0, tiled=True).reshape(features, cols)
    (update,) = call(inverse_kernel, "inverse", (flat_half,), summed, backward_once)
    return kept[None], update


def solution(mesh):
    in_specs = (
        P(("dp", "tensor"), None),
        P("dp", "tensor"),
        P("dp", None, "tensor"),
        P("dp", None, "tensor", None),
        P("dp"),
    )
    out_specs = (P("dp", None, "tensor"), P(None, "tensor"))
    body = functools.partial(shards, replicas=mesh.shape["dp"], group=mesh.shape["tensor"])
    return jax.shard_map(body, mesh=mesh, in_specs=in_specs, out_specs=out_specs, check_vma=False)
```

```python
import functools

import jax
import jax.numpy as jnp
import ml_dtypes
import numpy as np
from jax import lax
from jax.experimental import pallas as pl
from jax.experimental.pallas import tpu as pltpu
from jax.sharding import PartitionSpec as P

BLK = 32
SPAN = 64
WIDE = 4


def cosine_parts():
    n = np.arange(SPAN, dtype=np.float64)
    table = np.cos(np.pi * (2.0 * n[None, :] + 1.0) * n[:, None] / 128.0) * np.sqrt(2.0 / SPAN)
    table[0] *= np.sqrt(0.5)
    high = table.astype(ml_dtypes.bfloat16)
    low = (table - high.astype(np.float64)).astype(ml_dtypes.bfloat16)
    return high, low


def split(x):
    high = x.astype(jnp.bfloat16)
    return high, (x - high.astype(jnp.float32)).astype(jnp.bfloat16)


def spans_of(ref, i, count):
    first = i * count * SPAN
    return [ref[first + s * SPAN : first + (s + 1) * SPAN, :] for s in range(count)]


def beside(parts):
    return jnp.concatenate(parts, axis=1)


def product(table, parts):
    return jnp.dot(table[...], jnp.concatenate(parts, axis=0), preferred_element_type=jnp.float32)


def put(ref, i, count, value):
    cols = ref.shape[1]
    for s in range(count):
        first = (i * count + s) * SPAN
        ref[first : first + SPAN, :] = value[:, s * cols : (s + 1) * cols].astype(ref.dtype)


def mask_kernel(ids, count, mask):
    shape = (SPAN, mask.shape[1])
    block = lax.shift_right_logical(lax.broadcasted_iota(jnp.int32, shape, 0), 1)
    first = lax.broadcasted_iota(jnp.int32, shape, 1) < SPAN
    most = ids.shape[0] * SPAN // (2 * mask.shape[0])

    def body(a, _):
        hit = jnp.zeros(shape, jnp.bool_)
        for k in range(most):
            active = k < count[0]
            one = jnp.where(active, ids[2 * most * a + k], -1)
            two = jnp.where(active, ids[2 * most * a + most + k], -1)
            hit = hit | (jnp.where(first, one, two) == block)
        rows = pl.ds(pl.multiple_of(a * SPAN, SPAN), SPAN)
        mask[rows, :] = hit.astype(jnp.float32).astype(mask.dtype)
        return 0

    lax.fori_loop(0, mask.shape[0] // SPAN, body, 0)


def chosen_rows(x, mask, forward, i):
    high, low = split(x)
    keep = beside(spans_of(mask, i, WIDE)).astype(jnp.float32)
    return product(forward, [high, low, high]) * keep


def spectrum_kernel(part, other, mask, forward, advanced, sent):
    for i in range(part.shape[0] // (SPAN * WIDE)):
        x = beside(
            [
                p + o.astype(jnp.float32)
                for p, o in zip(spans_of(part, i, WIDE), spans_of(other, i, WIDE))
            ]
        )
        put(advanced, i, WIDE, x)
        put(sent, i, WIDE, chosen_rows(x, mask, forward, i))


def kept_kernel(advanced, mask, forward, backward, kept):
    for i in range(kept.shape[0] // (SPAN * WIDE)):
        x = beside(spans_of(advanced, i, WIDE))
        high, low = split(chosen_rows(x, mask, forward, i))
        put(kept, i, WIDE, x - product(backward, [high, low, high]))


def total_kernel(pieces, totals):
    total = pieces[0].astype(jnp.float32)
    for r in range(1, pieces.shape[0]):
        total = total + pieces[r].astype(jnp.float32)
    total = total.astype(totals.dtype)
    for r in range(totals.shape[0]):
        totals[r] = total


def inverse_kernel(summed, backward, update):
    for i in range(update.shape[0] // (SPAN * WIDE)):
        s = beside(spans_of(summed, i, WIDE))
        put(update, i, WIDE, product(backward, [s, s]))


def gram(a, k):
    return lax.dot_general(a, k, (((0,), (0,)), ((), ())), preferred_element_type=jnp.float32)


VMEM, SMEM = (pl.BlockSpec(memory_space=space) for space in (pltpu.VMEM, pltpu.SMEM))


def call(kernel, name, outs, *args, places=None):
    moved = sum(x.size * x.dtype.itemsize for x in args + outs)
    return pl.pallas_call(
        kernel,
        out_shape=outs,
        in_specs=places or [VMEM] * len(args),
        out_specs=(VMEM,) * len(outs),
        compiler_params=pltpu.CompilerParams(vmem_limit_bytes=10 << 20),
        cost_estimate=pl.CostEstimate(
            flops=6 * 2 * SPAN * outs[0].size, bytes_accessed=moved, transcendentals=0
        ),
        name=name,
    )(*args)


def shards(activations, key_grad, momentum, block_ids, counts, *, replicas, group):
    tokens, features = activations.shape
    cols = key_grad.shape[1]
    chips = group // 2
    spot = lax.axis_index("tensor")
    chip, core = lax.shift_right_logical(spot, 1), lax.bitwise_and(spot, 1)

    def along(x, step):
        return lax.ppermute(x, "tensor", [(i, (i + 2 * step) % group) for i in range(group)])

    def swap(x):
        return lax.ppermute(x, "tensor", [(i, i ^ 1) for i in range(group)])

    cut = tokens * 9 // 16 // 16 * 16
    head, tail = activations[:cut], activations[cut:]
    left, right_tail = along(activations, 1), along(tail, -1)

    by_core = key_grad.reshape(chips, 2, tokens, cols)

    def keys_for(which):
        rows = lax.dynamic_index_in_dim(by_core, which, 1, keepdims=False)
        return lax.dynamic_slice_in_dim(jnp.concatenate([rows, rows]), chip, chips, 0)

    their_keys = swap(keys_for(1 - core))

    head, their_keys, block_ids, counts = lax.optimization_barrier(
        (head, their_keys, block_ids, counts)
    )
    right_head = along(head, -1)

    left, right_tail, block, key_grad, momentum = lax.optimization_barrier(
        (left, right_tail, activations, key_grad, momentum)
    )
    far_head, far_tail = along(left[:cut], 1), along(right_tail, -1)
    by_core = key_grad.reshape(chips, 2, tokens, cols)
    own_keys = keys_for(core)
    keys = lax.optimization_barrier(jnp.concatenate([own_keys, their_keys], axis=2))
    before, after = keys[chips - 1], keys[1]
    near = (
        gram(block, keys[0])
        + gram(left, before)
        + gram(right_tail, after[cut:])
        + gram(right_head, after[:cut])
    )
    own_near = near[:, :cols] + 0.999 * momentum[0]
    their_near = near[:, cols:]
    own_far, their_far = own_keys[2], their_keys[2]

    def whole(total, far):
        return total + gram(far_head, far[:cut]) + gram(far_tail, far[cut:])

    flat = jax.ShapeDtypeStruct((features, cols), jnp.float32)
    flat_half = jax.ShapeDtypeStruct((features, cols), jnp.bfloat16)
    (mask,) = call(
        mask_kernel, "mask", (flat_half,), block_ids.reshape(-1), counts, places=[SMEM, SMEM]
    )

    (own_near, their_near, own_far, their_far, mask, far_head, far_tail) = (
        lax.optimization_barrier(
            (own_near, their_near, own_far, their_far, mask, far_head, far_tail)
        )
    )
    other = swap(whole(their_near, their_far).astype(jnp.bfloat16))
    part = whole(own_near, own_far)

    high, low = cosine_parts()
    forward = jnp.asarray(np.concatenate([high, high, low], axis=1))
    backward = jnp.asarray(np.concatenate([high.T, high.T, low.T], axis=1))
    backward_once = jnp.asarray(np.concatenate([high.T, low.T], axis=1))

    advanced, sent = call(
        spectrum_kernel,
        "spectrum",
        (flat, flat_half),
        part,
        other,
        mask,
        forward,
    )
    pieces = lax.all_to_all(
        sent.reshape(replicas, features // replicas, cols), "dp", 0, 0, tiled=True
    )
    (kept,) = call(kept_kernel, "kept", (flat,), advanced, mask, forward, backward)
    (totals,) = call(
        total_kernel, "total", (jax.ShapeDtypeStruct(pieces.shape, jnp.bfloat16),), pieces
    )
    summed = lax.all_to_all(totals, "dp", 0, 0, tiled=True).reshape(features, cols)
    (update,) = call(inverse_kernel, "inverse", (flat_half,), summed, backward_once)
    return kept[None], update


def solution(mesh):
    in_specs = (
        P(("dp", "tensor"), None),
        P("dp", "tensor"),
        P("dp", None, "tensor"),
        P("dp", None, "tensor", None),
        P("dp"),
    )
    out_specs = (P("dp", None, "tensor"), P(None, "tensor"))
    body = functools.partial(shards, replicas=mesh.shape["dp"], group=mesh.shape["tensor"])
    return jax.shard_map(body, mesh=mesh, in_specs=in_specs, out_specs=out_specs, check_vma=False)
```

```python
import functools

import jax
import jax.numpy as jnp
import ml_dtypes
import numpy as np
from jax import lax
from jax.experimental import pallas as pl
from jax.experimental.pallas import tpu as pltpu
from jax.sharding import PartitionSpec as P

BLK = 32
SPAN = 64
WIDE = 4


def cosine_parts():
    n = np.arange(SPAN, dtype=np.float64)
    table = np.cos(np.pi * (2.0 * n[None, :] + 1.0) * n[:, None] / 128.0) * np.sqrt(2.0 / SPAN)
    table[0] *= np.sqrt(0.5)
    high = table.astype(ml_dtypes.bfloat16)
    low = (table - high.astype(np.float64)).astype(ml_dtypes.bfloat16)
    return high, low


def split(x):
    high = x.astype(jnp.bfloat16)
    return high, (x - high.astype(jnp.float32)).astype(jnp.bfloat16)


def spans_of(ref, i, count):
    first = i * count * SPAN
    return [ref[first + s * SPAN : first + (s + 1) * SPAN, :] for s in range(count)]


def beside(parts):
    return jnp.concatenate(parts, axis=1)


def product(table, parts):
    return jnp.dot(table[...], jnp.concatenate(parts, axis=0), preferred_element_type=jnp.float32)


def put(ref, i, count, value):
    cols = ref.shape[1]
    for s in range(count):
        first = (i * count + s) * SPAN
        ref[first : first + SPAN, :] = value[:, s * cols : (s + 1) * cols].astype(ref.dtype)


def mask_kernel(ids, count, mask):
    shape = (SPAN, mask.shape[1])
    block = lax.shift_right_logical(lax.broadcasted_iota(jnp.int32, shape, 0), 1)
    first = lax.broadcasted_iota(jnp.int32, shape, 1) < SPAN
    most = ids.shape[0] * SPAN // (2 * mask.shape[0])

    def body(a, _):
        hit = jnp.zeros(shape, jnp.bool_)
        for k in range(most):
            active = k < count[0]
            one = jnp.where(active, ids[2 * most * a + k], -1)
            two = jnp.where(active, ids[2 * most * a + most + k], -1)
            hit = hit | (jnp.where(first, one, two) == block)
        rows = pl.ds(pl.multiple_of(a * SPAN, SPAN), SPAN)
        mask[rows, :] = hit.astype(jnp.float32).astype(mask.dtype)
        return 0

    lax.fori_loop(0, mask.shape[0] // SPAN, body, 0)


def chosen_rows(x, mask, forward, i):
    high, low = split(x)
    keep = beside(spans_of(mask, i, WIDE)).astype(jnp.float32)
    return product(forward, [high, low, high]) * keep


def spectrum_kernel(part, other, mask, forward, advanced, sent):
    for i in range(part.shape[0] // (SPAN * WIDE)):
        x = beside(
            [
                p + o.astype(jnp.float32)
                for p, o in zip(spans_of(part, i, WIDE), spans_of(other, i, WIDE))
            ]
        )
        put(advanced, i, WIDE, x)
        put(sent, i, WIDE, chosen_rows(x, mask, forward, i))


def kept_kernel(advanced, mask, forward, backward, kept):
    for i in range(kept.shape[0] // (SPAN * WIDE)):
        x = beside(spans_of(advanced, i, WIDE))
        high, low = split(chosen_rows(x, mask, forward, i))
        put(kept, i, WIDE, x - product(backward, [high, low, high]))


def total_kernel(pieces, totals):
    total = pieces[0].astype(jnp.float32)
    for r in range(1, pieces.shape[0]):
        total = total + pieces[r].astype(jnp.float32)
    total = total.astype(totals.dtype)
    for r in range(totals.shape[0]):
        totals[r] = total


def inverse_kernel(summed, backward, update):
    for i in range(update.shape[0] // (SPAN * WIDE)):
        s = beside(spans_of(summed, i, WIDE))
        put(update, i, WIDE, product(backward, [s, s]))


def gram(a, k):
    return lax.dot_general(a, k, (((0,), (0,)), ((), ())), preferred_element_type=jnp.float32)


VMEM, SMEM = (pl.BlockSpec(memory_space=space) for space in (pltpu.VMEM, pltpu.SMEM))


def call(kernel, name, outs, *args, places=None):
    moved = sum(x.size * x.dtype.itemsize for x in args + outs)
    return pl.pallas_call(
        kernel,
        out_shape=outs,
        in_specs=places or [VMEM] * len(args),
        out_specs=(VMEM,) * len(outs),
        compiler_params=pltpu.CompilerParams(vmem_limit_bytes=10 << 20),
        cost_estimate=pl.CostEstimate(
            flops=6 * 2 * SPAN * outs[0].size, bytes_accessed=moved, transcendentals=0
        ),
        name=name,
    )(*args)


def shards(activations, key_grad, momentum, block_ids, counts, *, replicas, group):
    tokens, features = activations.shape
    cols = key_grad.shape[1]
    chips = group // 2
    spot = lax.axis_index("tensor")
    chip, core = lax.shift_right_logical(spot, 1), lax.bitwise_and(spot, 1)

    def along(x, step):
        return lax.ppermute(x, "tensor", [(i, (i + 2 * step) % group) for i in range(group)])

    def swap(x):
        return lax.ppermute(x, "tensor", [(i, i ^ 1) for i in range(group)])

    cut = tokens * 9 // 16 // 16 * 16
    head, tail = activations[:cut], activations[cut:]
    left, right_tail = along(activations, 1), along(tail, -1)

    by_core = key_grad.reshape(chips, 2, tokens, cols)

    def keys_for(which):
        rows = lax.dynamic_index_in_dim(by_core, which, 1, keepdims=False)
        return lax.dynamic_slice_in_dim(jnp.concatenate([rows, rows]), chip, chips, 0)

    their_keys = swap(keys_for(1 - core))

    head, their_keys, block_ids, counts = lax.optimization_barrier(
        (head, their_keys, block_ids, counts)
    )
    right_head = along(head, -1)
    far_tail = along(right_tail, -1)

    left, right_tail, block, key_grad, momentum = lax.optimization_barrier(
        (left, right_tail, activations, key_grad, momentum)
    )
    far_head = along(left[:cut], 1)
    by_core = key_grad.reshape(chips, 2, tokens, cols)
    own_keys = keys_for(core)
    keys = lax.optimization_barrier(jnp.concatenate([own_keys, their_keys], axis=2))
    before, after = keys[chips - 1], keys[1]
    near = (
        gram(block, keys[0])
        + gram(left, before)
        + gram(right_tail, after[cut:])
        + gram(right_head, after[:cut])
    )
    own_near = near[:, :cols] + 0.999 * momentum[0]
    their_near = near[:, cols:]
    own_far, their_far = own_keys[2], their_keys[2]

    def whole(total, far):
        return total + gram(far_head, far[:cut]) + gram(far_tail, far[cut:])

    flat = jax.ShapeDtypeStruct((features, cols), jnp.float32)
    flat_half = jax.ShapeDtypeStruct((features, cols), jnp.bfloat16)
    (mask,) = call(
        mask_kernel, "mask", (flat_half,), block_ids.reshape(-1), counts, places=[SMEM, SMEM]
    )

    (own_near, their_near, own_far, their_far, mask, far_head, far_tail) = (
        lax.optimization_barrier(
            (own_near, their_near, own_far, their_far, mask, far_head, far_tail)
        )
    )
    other = swap(whole(their_near, their_far).astype(jnp.bfloat16))
    part = whole(own_near, own_far)

    high, low = cosine_parts()
    forward = jnp.asarray(np.concatenate([high, high, low], axis=1))
    backward = jnp.asarray(np.concatenate([high.T, high.T, low.T], axis=1))
    backward_once = jnp.asarray(np.concatenate([high.T, low.T], axis=1))

    advanced, sent = call(
        spectrum_kernel,
        "spectrum",
        (flat, flat_half),
        part,
        other,
        mask,
        forward,
    )
    pieces = lax.all_to_all(
        sent.reshape(replicas, features // replicas, cols), "dp", 0, 0, tiled=True
    )
    (kept,) = call(kept_kernel, "kept", (flat,), advanced, mask, forward, backward)
    (totals,) = call(
        total_kernel, "total", (jax.ShapeDtypeStruct(pieces.shape, jnp.bfloat16),), pieces
    )
    summed = lax.all_to_all(totals, "dp", 0, 0, tiled=True).reshape(features, cols)
    (update,) = call(inverse_kernel, "inverse", (flat_half,), summed, backward_once)
    return kept[None], update


def solution(mesh):
    in_specs = (
        P(("dp", "tensor"), None),
        P("dp", "tensor"),
        P("dp", None, "tensor"),
        P("dp", None, "tensor", None),
        P("dp"),
    )
    out_specs = (P("dp", None, "tensor"), P(None, "tensor"))
    body = functools.partial(shards, replicas=mesh.shape["dp"], group=mesh.shape["tensor"])
    return jax.shard_map(body, mesh=mesh, in_specs=in_specs, out_specs=out_specs, check_vma=False)
```

```python
import functools

import jax
import jax.numpy as jnp
import ml_dtypes
import numpy as np
from jax import lax
from jax.experimental import pallas as pl
from jax.experimental.pallas import tpu as pltpu
from jax.sharding import PartitionSpec as P

BLK = 32
SPAN = 64
WIDE = 4


def cosine_parts():
    n = np.arange(SPAN, dtype=np.float64)
    table = np.cos(np.pi * (2.0 * n[None, :] + 1.0) * n[:, None] / 128.0) * np.sqrt(2.0 / SPAN)
    table[0] *= np.sqrt(0.5)
    high = table.astype(ml_dtypes.bfloat16)
    low = (table - high.astype(np.float64)).astype(ml_dtypes.bfloat16)
    return high, low


def split(x):
    high = x.astype(jnp.bfloat16)
    return high, (x - high.astype(jnp.float32)).astype(jnp.bfloat16)


def spans_of(ref, i, count):
    first = i * count * SPAN
    return [ref[first + s * SPAN : first + (s + 1) * SPAN, :] for s in range(count)]


def beside(parts):
    return jnp.concatenate(parts, axis=1)


def product(table, parts):
    return jnp.dot(table[...], jnp.concatenate(parts, axis=0), preferred_element_type=jnp.float32)


def put(ref, i, count, value):
    cols = ref.shape[1]
    for s in range(count):
        first = (i * count + s) * SPAN
        ref[first : first + SPAN, :] = value[:, s * cols : (s + 1) * cols].astype(ref.dtype)


def mask_kernel(ids, count, mask):
    shape = (SPAN, mask.shape[1])
    block = lax.shift_right_logical(lax.broadcasted_iota(jnp.int32, shape, 0), 1)
    first = lax.broadcasted_iota(jnp.int32, shape, 1) < SPAN
    most = ids.shape[0] * SPAN // (2 * mask.shape[0])

    def body(a, _):
        hit = jnp.zeros(shape, jnp.bool_)
        for k in range(most):
            active = k < count[0]
            one = jnp.where(active, ids[2 * most * a + k], -1)
            two = jnp.where(active, ids[2 * most * a + most + k], -1)
            hit = hit | (jnp.where(first, one, two) == block)
        rows = pl.ds(pl.multiple_of(a * SPAN, SPAN), SPAN)
        mask[rows, :] = hit.astype(jnp.float32).astype(mask.dtype)
        return 0

    lax.fori_loop(0, mask.shape[0] // SPAN, body, 0)


def chosen_rows(x, mask, forward, i):
    high, low = split(x)
    keep = beside(spans_of(mask, i, WIDE)).astype(jnp.float32)
    return product(forward, [high, low, high]) * keep


def spectrum_kernel(part, other, mask, forward, advanced, sent):
    for i in range(part.shape[0] // (SPAN * WIDE)):
        x = beside(
            [
                p + o.astype(jnp.float32)
                for p, o in zip(spans_of(part, i, WIDE), spans_of(other, i, WIDE))
            ]
        )
        put(advanced, i, WIDE, x)
        put(sent, i, WIDE, chosen_rows(x, mask, forward, i))


def kept_kernel(advanced, mask, forward, backward, kept):
    for i in range(kept.shape[0] // (SPAN * WIDE)):
        x = beside(spans_of(advanced, i, WIDE))
        high, low = split(chosen_rows(x, mask, forward, i))
        put(kept, i, WIDE, x - product(backward, [high, low, high]))


def total_kernel(pieces, totals):
    total = pieces[0].astype(jnp.float32)
    for r in range(1, pieces.shape[0]):
        total = total + pieces[r].astype(jnp.float32)
    total = total.astype(totals.dtype)
    for r in range(totals.shape[0]):
        totals[r] = total


def inverse_kernel(summed, backward, update):
    for i in range(update.shape[0] // (SPAN * WIDE)):
        s = beside(spans_of(summed, i, WIDE))
        put(update, i, WIDE, product(backward, [s, s]))


def gram(a, k):
    return lax.dot_general(a, k, (((0,), (0,)), ((), ())), preferred_element_type=jnp.float32)


VMEM, SMEM = (pl.BlockSpec(memory_space=space) for space in (pltpu.VMEM, pltpu.SMEM))


def call(kernel, name, outs, *args, places=None):
    moved = sum(x.size * x.dtype.itemsize for x in args + outs)
    return pl.pallas_call(
        kernel,
        out_shape=outs,
        in_specs=places or [VMEM] * len(args),
        out_specs=(VMEM,) * len(outs),
        compiler_params=pltpu.CompilerParams(vmem_limit_bytes=10 << 20),
        cost_estimate=pl.CostEstimate(
            flops=6 * 2 * SPAN * outs[0].size, bytes_accessed=moved, transcendentals=0
        ),
        name=name,
    )(*args)


def shards(activations, key_grad, momentum, block_ids, counts, *, replicas, group):
    tokens, features = activations.shape
    cols = key_grad.shape[1]
    chips = group // 2
    spot = lax.axis_index("tensor")
    chip, core = lax.shift_right_logical(spot, 1), lax.bitwise_and(spot, 1)

    def along(x, step):
        return lax.ppermute(x, "tensor", [(i, (i + 2 * step) % group) for i in range(group)])

    def swap(x):
        return lax.ppermute(x, "tensor", [(i, i ^ 1) for i in range(group)])

    cut = tokens * 2 // 5 // 16 * 16
    head, tail = activations[:cut], activations[cut:]
    left_head, right_tail = along(head, 1), along(tail, -1)
    left_tail, right_head = along(tail, 1), along(head, -1)

    left_head, right_tail, block, key_grad, momentum = lax.optimization_barrier(
        (left_head, right_tail, activations, key_grad, momentum)
    )
    far_head, far_tail = along(left_head, 1), along(right_tail, -1)

    by_core = key_grad.reshape(chips, 2, tokens, cols)

    def keys_for(which):
        rows = lax.dynamic_index_in_dim(by_core, which, 1, keepdims=False)
        return lax.dynamic_slice_in_dim(jnp.concatenate([rows, rows]), chip, chips, 0)

    own_keys, their_keys = keys_for(core), swap(keys_for(1 - core))
    keys = lax.optimization_barrier(jnp.concatenate([own_keys, their_keys], axis=2))
    before, after = keys[chips - 1], keys[1]
    near = (
        gram(block, keys[0])
        + gram(left_head, before[:cut])
        + gram(left_tail, before[cut:])
        + gram(right_tail, after[cut:])
        + gram(right_head, after[:cut])
    )
    own_near = near[:, :cols] + 0.999 * momentum[0]
    their_near = near[:, cols:]
    own_far, their_far = own_keys[2], their_keys[2]

    def whole(total, far):
        return total + gram(far_head, far[:cut]) + gram(far_tail, far[cut:])

    flat = jax.ShapeDtypeStruct((features, cols), jnp.float32)
    flat_half = jax.ShapeDtypeStruct((features, cols), jnp.bfloat16)
    (mask,) = call(
        mask_kernel, "mask", (flat_half,), block_ids.reshape(-1), counts, places=[SMEM, SMEM]
    )

    (own_near, their_near, own_far, their_far, mask, far_head, far_tail) = (
        lax.optimization_barrier(
            (own_near, their_near, own_far, their_far, mask, far_head, far_tail)
        )
    )
    other = swap(whole(their_near, their_far).astype(jnp.bfloat16))
    part = whole(own_near, own_far)

    high, low = cosine_parts()
    forward = jnp.asarray(np.concatenate([high, high, low], axis=1))
    backward = jnp.asarray(np.concatenate([high.T, high.T, low.T], axis=1))
    backward_once = jnp.asarray(np.concatenate([high.T, low.T], axis=1))

    advanced, sent = call(
        spectrum_kernel,
        "spectrum",
        (flat, flat_half),
        part,
        other,
        mask,
        forward,
    )
    pieces = lax.all_to_all(
        sent.reshape(replicas, features // replicas, cols), "dp", 0, 0, tiled=True
    )
    (kept,) = call(kept_kernel, "kept", (flat,), advanced, mask, forward, backward)
    (totals,) = call(
        total_kernel, "total", (jax.ShapeDtypeStruct(pieces.shape, jnp.bfloat16),), pieces
    )
    summed = lax.all_to_all(totals, "dp", 0, 0, tiled=True).reshape(features, cols)
    (update,) = call(inverse_kernel, "inverse", (flat_half,), summed, backward_once)
    return kept[None], update


def solution(mesh):
    in_specs = (
        P(("dp", "tensor"), None),
        P("dp", "tensor"),
        P("dp", None, "tensor"),
        P("dp", None, "tensor", None),
        P("dp"),
    )
    out_specs = (P("dp", None, "tensor"), P(None, "tensor"))
    body = functools.partial(shards, replicas=mesh.shape["dp"], group=mesh.shape["tensor"])
    return jax.shard_map(body, mesh=mesh, in_specs=in_specs, out_specs=out_specs, check_vma=False)
```

```python
import functools

import jax
import jax.numpy as jnp
import ml_dtypes
import numpy as np
from jax import lax
from jax.experimental import pallas as pl
from jax.experimental.pallas import tpu as pltpu
from jax.sharding import PartitionSpec as P

BLK = 32
SPAN = 64
WIDE = 4
ROW_GROUPS = 4
OWN_COLS = 8


def cosine_parts():
    n = np.arange(SPAN, dtype=np.float64)
    table = np.cos(np.pi * (2.0 * n[None, :] + 1.0) * n[:, None] / 128.0) * np.sqrt(2.0 / SPAN)
    table[0] *= np.sqrt(0.5)
    high = table.astype(ml_dtypes.bfloat16)
    low = (table - high.astype(np.float64)).astype(ml_dtypes.bfloat16)
    return high, low


def split(x):
    high = x.astype(jnp.bfloat16)
    return high, (x - high.astype(jnp.float32)).astype(jnp.bfloat16)


def spans_of(ref, i, count):
    first = i * count * SPAN
    return [ref[first + s * SPAN : first + (s + 1) * SPAN, :] for s in range(count)]


def beside(parts):
    return jnp.concatenate(parts, axis=1)


def product(table, parts):
    return jnp.dot(table[...], jnp.concatenate(parts, axis=0), preferred_element_type=jnp.float32)


def put(ref, i, count, value):
    cols = ref.shape[1]
    for s in range(count):
        first = (i * count + s) * SPAN
        ref[first : first + SPAN, :] = value[:, s * cols : (s + 1) * cols].astype(ref.dtype)


def routes_kernel(ids, count, base, mask, picks, numbers):
    cols = mask.shape[1]
    spans = mask.shape[0] // SPAN
    most = ids.shape[0] // (2 * spans)
    each = spans // ROW_GROUPS

    def number(a, b, k):
        return jnp.where(k < count[0], ids[(2 * a + b) * most + k], -1)

    block = lax.shift_right_logical(lax.broadcasted_iota(jnp.int32, (SPAN, cols), 0), 1)
    first = lax.broadcasted_iota(jnp.int32, (SPAN, cols), 1) < SPAN

    def body(a, _):
        hit = jnp.zeros((SPAN, cols), jnp.bool_)
        for k in range(most):
            hit = hit | (jnp.where(first, number(a, 0, k), number(a, 1, k)) == block)
        rows = pl.ds(pl.multiple_of(a * SPAN, SPAN), SPAN)
        mask[rows, :] = hit.astype(jnp.float32).astype(mask.dtype)
        return 0

    lax.fori_loop(0, spans, body, 0)

    lane = lax.broadcasted_iota(jnp.int32, (SPAN, cols), 1)
    square = (cols, cols)
    column = lax.broadcasted_iota(jnp.int32, square, 1)
    slot = lax.shift_right_logical(lax.broadcasted_iota(jnp.int32, square, 0), 1)
    double = (column == slot).astype(jnp.float32).astype(jnp.bfloat16)
    place = column.astype(jnp.float32)
    for g in range(ROW_GROUPS):
        halves = []
        for b in range(2):
            line = jnp.full((SPAN, cols), -1, jnp.int32)
            for a in range(each):
                for k in range(most):
                    line = jnp.where(lane == a * most + k, number(g * each + a, b, k), line)
            halves.append(line)
        tile = jnp.concatenate(halves, axis=0).astype(jnp.float32)
        numbers[g * cols : (g + 1) * cols, :] = tile.astype(numbers.dtype)
        twice = jnp.dot(
            double, tile.T.astype(jnp.bfloat16), preferred_element_type=jnp.float32
        )
        for b in range(2):
            own = jnp.broadcast_to(twice[:, b * SPAN : b * SPAN + 1], square)
            target = jnp.where(own < 0.0, -1.0, base[...] + 2.0 * own)
            for i in range(picks.shape[1] // cols):
                picks[(2 * g + b) * cols : (2 * g + b + 1) * cols, i * cols : (i + 1) * cols] = (
                    (target == place + float(i * cols)).astype(jnp.float32).astype(picks.dtype)
                )


def chosen_rows(x, mask, forward, i):
    high, low = split(x)
    keep = beside(spans_of(mask, i, WIDE)).astype(jnp.float32)
    return product(forward, [high, low, high]) * keep


def spectrum_kernel(part, other, picks, numbers, forward, advanced, sent, rows):
    for i in range(part.shape[0] // (SPAN * WIDE)):
        x = beside(
            [
                p + o.astype(jnp.float32)
                for p, o in zip(spans_of(part, i, WIDE), spans_of(other, i, WIDE))
            ]
        )
        put(advanced, i, WIDE, x)
        high, low = split(x)
        put(rows, i, WIDE, product(forward, [high, low, high]))
    cols = part.shape[1]
    height = picks.shape[1]
    first = lax.broadcasted_iota(jnp.int32, (cols, cols), 1) < SPAN
    for g in range(ROW_GROUPS):
        band = rows[g * height : (g + 1) * height, :]
        one, two = (
            jnp.dot(
                picks[(2 * g + b) * cols : (2 * g + b + 1) * cols, :],
                band,
                preferred_element_type=jnp.float32,
            )
            for b in range(2)
        )
        message = slice(g * cols, (g + 1) * cols)
        sent[message, :cols] = jnp.where(first, one, two).T.astype(sent.dtype)
        sent[message, cols:] = numbers[message, :]


def kept_kernel(advanced, mask, forward, backward, kept):
    for i in range(kept.shape[0] // (SPAN * WIDE)):
        x = beside(spans_of(advanced, i, WIDE))
        high, low = split(chosen_rows(x, mask, forward, i))
        put(kept, i, WIDE, x - product(backward, [high, low, high]))


def total_kernel(pieces, backward, totals, placed):
    wide = pieces.shape[1] // 2
    spans = totals.shape[1] // SPAN
    lane = lax.broadcasted_iota(jnp.int32, (BLK, wide), 0).astype(jnp.float32)
    for t in range(pieces.shape[0] // wide):
        values = pieces[t * wide : (t + 1) * wide, :wide].astype(jnp.float32).T
        numbers = pieces[t * wide : (t + 1) * wide, wide:].astype(jnp.float32).T
        most = wide // (2 * spans)
        for a in range(spans):
            upper = jnp.zeros((BLK, wide), jnp.float32)
            lower = upper
            for k in range(most):
                at = a * most + k
                here = numbers[at : at + 1, :] == lane
                upper = jnp.where(here, values[2 * at : 2 * at + 1, :], upper)
                lower = jnp.where(here, values[2 * at + 1 : 2 * at + 2, :], lower)
            both = jnp.concatenate([upper, lower], axis=0)
            placed[a * SPAN : (a + 1) * SPAN, t * wide : (t + 1) * wide] = both.astype(placed.dtype)
    shape = (2 * OWN_COLS, placed.shape[1])
    column = lax.broadcasted_iota(jnp.int32, shape, 1) & (OWN_COLS - 1)
    row = lax.broadcasted_iota(jnp.int32, shape, 0) & (OWN_COLS - 1)
    total = lax.dot_general(
        (column == row).astype(jnp.float32).astype(placed.dtype),
        placed[...],
        (((1,), (1,)), ((), ())),
        preferred_element_type=jnp.float32,
    )
    pair = 2 * SPAN
    for i in range(totals.shape[1] // pair):
        high, low = split(total[:, i * pair : (i + 1) * pair])
        done = jnp.dot(
            jnp.concatenate([high, low, high], axis=1),
            backward[...],
            preferred_element_type=jnp.float32,
        ).astype(totals.dtype)
        for r in range(totals.shape[0] // shape[0]):
            totals[r * shape[0] : (r + 1) * shape[0], i * pair : (i + 1) * pair] = done


def turn_kernel(turned, update):
    cols, height = update.shape[1], turned.shape[1]
    square = (cols, cols)
    same = lax.broadcasted_iota(jnp.int32, square, 0) == lax.broadcasted_iota(
        jnp.int32, square, 1
    )
    same = same.astype(jnp.float32).astype(turned.dtype)
    for g in range(ROW_GROUPS):
        for i in range(height // cols):
            rows = g * height + i * cols
            update[rows : rows + cols, :] = lax.dot_general(
                same,
                turned[g * cols : (g + 1) * cols, i * cols : (i + 1) * cols],
                (((1,), (1,)), ((), ())),
                preferred_element_type=jnp.float32,
            ).astype(update.dtype)


def gram(a, k):
    return lax.dot_general(a, k, (((0,), (0,)), ((), ())), preferred_element_type=jnp.float32)


VMEM, SMEM = (pl.BlockSpec(memory_space=space) for space in (pltpu.VMEM, pltpu.SMEM))


def call(kernel, name, outs, *args, places=None, scratch=()):
    moved = sum(x.size * x.dtype.itemsize for x in args + outs)
    return pl.pallas_call(
        kernel,
        out_shape=outs,
        in_specs=places or [VMEM] * len(args),
        out_specs=(VMEM,) * len(outs),
        scratch_shapes=scratch,
        compiler_params=pltpu.CompilerParams(vmem_limit_bytes=10 << 20),
        cost_estimate=pl.CostEstimate(
            flops=6 * 2 * SPAN * outs[0].size, bytes_accessed=moved, transcendentals=0
        ),
        name=name,
    )(*args)


def shards(activations, key_grad, momentum, block_ids, counts, *, replicas, group):
    tokens, features = activations.shape
    cols = key_grad.shape[1]
    chips = group // 2
    spot = lax.axis_index("tensor")
    chip, core = lax.shift_right_logical(spot, 1), lax.bitwise_and(spot, 1)

    def along(x, step):
        return lax.ppermute(x, "tensor", [(i, (i + 2 * step) % group) for i in range(group)])

    def swap(x):
        return lax.ppermute(x, "tensor", [(i, i ^ 1) for i in range(group)])

    cut = tokens * 2 // 5 // 16 * 16
    head, tail = activations[:cut], activations[cut:]
    left_head, right_tail = along(head, 1), along(tail, -1)
    left_tail, right_head = along(tail, 1), along(head, -1)

    left_head, right_tail, block, key_grad, momentum = lax.optimization_barrier(
        (left_head, right_tail, activations, key_grad, momentum)
    )
    far_head, far_tail = along(left_head, 1), along(right_tail, -1)

    by_core = key_grad.reshape(chips, 2, tokens, cols)

    def keys_for(which):
        rows = lax.dynamic_index_in_dim(by_core, which, 1, keepdims=False)
        return lax.dynamic_slice_in_dim(jnp.concatenate([rows, rows]), chip, chips, 0)

    own_keys, their_keys = keys_for(core), swap(keys_for(1 - core))
    keys = lax.optimization_barrier(jnp.concatenate([own_keys, their_keys], axis=2))
    before, after = keys[chips - 1], keys[1]
    near = (
        gram(block, keys[0])
        + gram(left_head, before[:cut])
        + gram(left_tail, before[cut:])
        + gram(right_tail, after[cut:])
        + gram(right_head, after[:cut])
    )
    own_near = near[:, :cols] + 0.999 * momentum[0]
    their_near = near[:, cols:]
    own_far, their_far = own_keys[2], their_keys[2]

    def whole(total, far):
        return total + gram(far_head, far[:cut]) + gram(far_tail, far[cut:])

    flat = jax.ShapeDtypeStruct((features, cols), jnp.float32)
    flat_half = jax.ShapeDtypeStruct((features, cols), jnp.bfloat16)
    height = features // ROW_GROUPS
    lines = np.arange(cols)
    base = SPAN * (lines // (2 * block_ids.shape[3])) + lines % 2
    mask, picks, numbers = call(
        routes_kernel,
        "routes",
        (
            flat_half,
            jax.ShapeDtypeStruct((2 * ROW_GROUPS * cols, height), jnp.bfloat16),
            jax.ShapeDtypeStruct((ROW_GROUPS * cols, cols), jnp.bfloat16),
        ),
        block_ids.reshape(-1),
        counts,
        jnp.asarray(np.repeat(base[:, None], cols, axis=1).astype(np.float32)),
        places=[SMEM, SMEM, VMEM],
    )

    (own_near, their_near, own_far, their_far, mask, picks, numbers, far_head, far_tail) = (
        lax.optimization_barrier(
            (own_near, their_near, own_far, their_far, mask, picks, numbers, far_head, far_tail)
        )
    )
    other = swap(whole(their_near, their_far).astype(jnp.bfloat16))
    part = whole(own_near, own_far)

    high, low = cosine_parts()
    forward = jnp.asarray(np.concatenate([high, high, low], axis=1))
    backward = jnp.asarray(np.concatenate([high.T, high.T, low.T], axis=1))
    order = np.concatenate([np.arange(0, SPAN, 2), np.arange(1, SPAN, 2)])
    both_high, both_low = (np.kron(np.eye(2, dtype=p.dtype), p[order]) for p in (high, low))
    backward_pair = jnp.asarray(np.concatenate([both_high, both_high, both_low], axis=0))

    message = jax.ShapeDtypeStruct((ROW_GROUPS * cols, 2 * cols), jnp.bfloat16)
    advanced, sent = call(
        spectrum_kernel,
        "spectrum",
        (flat, message),
        part,
        other,
        picks,
        numbers,
        forward,
        scratch=(pltpu.VMEM((features, cols), jnp.bfloat16),),
    )

    def exchange(x):
        return lax.all_to_all(
            x.reshape(replicas, OWN_COLS, x.shape[1]), "dp", 0, 0, tiled=True
        ).reshape(x.shape)

    pieces = exchange(sent)
    (kept,) = call(kept_kernel, "kept", (flat,), advanced, mask, forward, backward)
    (totals,) = call(
        total_kernel,
        "total",
        (jax.ShapeDtypeStruct((replicas * OWN_COLS, height), jnp.bfloat16),),
        pieces,
        backward_pair,
        scratch=(pltpu.VMEM((height, replicas * OWN_COLS), jnp.bfloat16),),
    )
    (update,) = call(turn_kernel, "turn", (flat_half,), exchange(totals))
    return kept[None], update


def solution(mesh):
    in_specs = (
        P(("dp", "tensor"), None),
        P("dp", "tensor"),
        P("dp", None, "tensor"),
        P("dp", None, "tensor", None),
        P("dp"),
    )
    out_specs = (P("dp", None, "tensor"), P(None, "tensor"))
    body = functools.partial(shards, replicas=mesh.shape["dp"], group=mesh.shape["tensor"])
    return jax.shard_map(body, mesh=mesh, in_specs=in_specs, out_specs=out_specs, check_vma=False)
```

```python
import functools

import jax
import jax.numpy as jnp
import ml_dtypes
import numpy as np
from jax import lax
from jax.experimental import pallas as pl
from jax.experimental.pallas import tpu as pltpu
from jax.sharding import PartitionSpec as P

BLK = 32
SPAN = 64
WIDE = 4
ROW_GROUPS = 4
OWN_COLS = 8


def cosine_parts():
    n = np.arange(SPAN, dtype=np.float64)
    table = np.cos(np.pi * (2.0 * n[None, :] + 1.0) * n[:, None] / 128.0) * np.sqrt(2.0 / SPAN)
    table[0] *= np.sqrt(0.5)
    high = table.astype(ml_dtypes.bfloat16)
    low = (table - high.astype(np.float64)).astype(ml_dtypes.bfloat16)
    return high, low


def split(x):
    high = x.astype(jnp.bfloat16)
    return high, (x - high.astype(jnp.float32)).astype(jnp.bfloat16)


def spans_of(ref, i, count):
    first = i * count * SPAN
    return [ref[first + s * SPAN : first + (s + 1) * SPAN, :] for s in range(count)]


def beside(parts):
    return jnp.concatenate(parts, axis=1)


def product(table, parts):
    return jnp.dot(table[...], jnp.concatenate(parts, axis=0), preferred_element_type=jnp.float32)


def put(ref, i, count, value):
    cols = ref.shape[1]
    for s in range(count):
        first = (i * count + s) * SPAN
        ref[first : first + SPAN, :] = value[:, s * cols : (s + 1) * cols].astype(ref.dtype)


def keys_kernel(chips, tokens, keys, own, partner):
    spot = lax.axis_index("tensor")
    chip, core = lax.shift_right_logical(spot, 1), lax.bitwise_and(spot, 1)
    for step in range(chips):
        pair = 2 * lax.bitwise_and(chip + step, chips - 1)
        here = slice(step * tokens, (step + 1) * tokens)
        own[here, :] = keys[pl.ds(pl.multiple_of((pair + core) * tokens, 16), tokens), :]
        partner[here, :] = keys[pl.ds(pl.multiple_of((pair + 1 - core) * tokens, 16), tokens), :]


def routes_kernel(ids, count, base, mask, picks, numbers):
    cols = mask.shape[1]
    spans = mask.shape[0] // SPAN
    most = ids.shape[0]
    each = spans // ROW_GROUPS

    def number(a, b, k):
        return jnp.where(k < count[0], ids[k, b, a], -1)

    block = lax.shift_right_logical(lax.broadcasted_iota(jnp.int32, (SPAN, cols), 0), 1)
    first = lax.broadcasted_iota(jnp.int32, (SPAN, cols), 1) < SPAN

    def body(a, _):
        hit = jnp.zeros((SPAN, cols), jnp.bool_)
        for k in range(most):
            hit = hit | (jnp.where(first, number(a, 0, k), number(a, 1, k)) == block)
        rows = pl.ds(pl.multiple_of(a * SPAN, SPAN), SPAN)
        mask[rows, :] = hit.astype(jnp.float32).astype(mask.dtype)
        return 0

    lax.fori_loop(0, spans, body, 0)

    lane = lax.broadcasted_iota(jnp.int32, (SPAN, cols), 1)
    square = (cols, cols)
    column = lax.broadcasted_iota(jnp.int32, square, 1)
    slot = lax.shift_right_logical(lax.broadcasted_iota(jnp.int32, square, 0), 1)
    double = (column == slot).astype(jnp.float32).astype(jnp.bfloat16)
    place = column.astype(jnp.float32)
    for g in range(ROW_GROUPS):
        halves = []
        for b in range(2):
            line = jnp.full((SPAN, cols), -1, jnp.int32)
            for a in range(each):
                for k in range(most):
                    line = jnp.where(lane == a * most + k, number(g * each + a, b, k), line)
            halves.append(line)
        tile = jnp.concatenate(halves, axis=0).astype(jnp.float32)
        numbers[g * cols : (g + 1) * cols, :] = tile.astype(numbers.dtype)
        twice = jnp.dot(
            double, tile.T.astype(jnp.bfloat16), preferred_element_type=jnp.float32
        )
        for b in range(2):
            own = jnp.broadcast_to(twice[:, b * SPAN : b * SPAN + 1], square)
            target = jnp.where(own < 0.0, -1.0, base[...] + 2.0 * own)
            for i in range(picks.shape[1] // cols):
                picks[(2 * g + b) * cols : (2 * g + b + 1) * cols, i * cols : (i + 1) * cols] = (
                    (target == place + float(i * cols)).astype(jnp.float32).astype(picks.dtype)
                )


def chosen_rows(x, mask, forward, i):
    high, low = split(x)
    keep = beside(spans_of(mask, i, WIDE)).astype(jnp.float32)
    return product(forward, [high, low, high]) * keep


def spectrum_kernel(part, other, picks, numbers, forward, advanced, sent, rows):
    for i in range(part.shape[0] // (SPAN * WIDE)):
        x = beside(
            [
                p + o.astype(jnp.float32)
                for p, o in zip(spans_of(part, i, WIDE), spans_of(other, i, WIDE))
            ]
        )
        put(advanced, i, WIDE, x)
        high, low = split(x)
        put(rows, i, WIDE, product(forward, [high, low, high]))
    cols = part.shape[1]
    height = picks.shape[1]
    first = lax.broadcasted_iota(jnp.int32, (cols, cols), 1) < SPAN
    for g in range(ROW_GROUPS):
        band = rows[g * height : (g + 1) * height, :]
        one, two = (
            jnp.dot(
                picks[(2 * g + b) * cols : (2 * g + b + 1) * cols, :],
                band,
                preferred_element_type=jnp.float32,
            )
            for b in range(2)
        )
        message = slice(g * cols, (g + 1) * cols)
        sent[message, :cols] = jnp.where(first, one, two).T.astype(sent.dtype)
        sent[message, cols:] = numbers[message, :]


def kept_kernel(advanced, mask, forward, backward, kept):
    for i in range(kept.shape[0] // (SPAN * WIDE)):
        x = beside(spans_of(advanced, i, WIDE))
        high, low = split(chosen_rows(x, mask, forward, i))
        put(kept, i, WIDE, x - product(backward, [high, low, high]))


def total_kernel(pieces, backward, totals, placed):
    wide = pieces.shape[1] // 2
    spans = totals.shape[1] // SPAN
    lane = lax.broadcasted_iota(jnp.int32, (BLK, wide), 0).astype(jnp.float32)
    for t in range(pieces.shape[0] // wide):
        values = pieces[t * wide : (t + 1) * wide, :wide].astype(jnp.float32).T
        numbers = pieces[t * wide : (t + 1) * wide, wide:].astype(jnp.float32).T
        most = wide // (2 * spans)
        for a in range(spans):
            upper = jnp.zeros((BLK, wide), jnp.float32)
            lower = upper
            for k in range(most):
                at = a * most + k
                here = numbers[at : at + 1, :] == lane
                upper = jnp.where(here, values[2 * at : 2 * at + 1, :], upper)
                lower = jnp.where(here, values[2 * at + 1 : 2 * at + 2, :], lower)
            both = jnp.concatenate([upper, lower], axis=0)
            placed[a * SPAN : (a + 1) * SPAN, t * wide : (t + 1) * wide] = both.astype(placed.dtype)
    shape = (2 * OWN_COLS, placed.shape[1])
    column = lax.broadcasted_iota(jnp.int32, shape, 1) & (OWN_COLS - 1)
    row = lax.broadcasted_iota(jnp.int32, shape, 0) & (OWN_COLS - 1)
    total = lax.dot_general(
        (column == row).astype(jnp.float32).astype(placed.dtype),
        placed[...],
        (((1,), (1,)), ((), ())),
        preferred_element_type=jnp.float32,
    )
    pair = 2 * SPAN
    for i in range(totals.shape[1] // pair):
        high, low = split(total[:, i * pair : (i + 1) * pair])
        done = jnp.dot(
            jnp.concatenate([high, low, high], axis=1),
            backward[...],
            preferred_element_type=jnp.float32,
        ).astype(totals.dtype)
        for r in range(totals.shape[0] // shape[0]):
            totals[r * shape[0] : (r + 1) * shape[0], i * pair : (i + 1) * pair] = done


def turn_kernel(turned, update):
    cols, height = update.shape[1], turned.shape[1]
    square = (cols, cols)
    same = lax.broadcasted_iota(jnp.int32, square, 0) == lax.broadcasted_iota(
        jnp.int32, square, 1
    )
    same = same.astype(jnp.float32).astype(turned.dtype)
    for g in range(ROW_GROUPS):
        for i in range(height // cols):
            rows = g * height + i * cols
            update[rows : rows + cols, :] = lax.dot_general(
                same,
                turned[g * cols : (g + 1) * cols, i * cols : (i + 1) * cols],
                (((1,), (1,)), ((), ())),
                preferred_element_type=jnp.float32,
            ).astype(update.dtype)


def gram(a, k):
    return lax.dot_general(a, k, (((0,), (0,)), ((), ())), preferred_element_type=jnp.float32)


VMEM, SMEM = (pl.BlockSpec(memory_space=space) for space in (pltpu.VMEM, pltpu.SMEM))


def call(kernel, name, outs, *args, places=None, scratch=()):
    return pl.pallas_call(
        kernel,
        out_shape=outs,
        in_specs=places or [VMEM] * len(args),
        out_specs=(VMEM,) * len(outs),
        scratch_shapes=scratch,
        compiler_params=pltpu.CompilerParams(vmem_limit_bytes=10 << 20),
        cost_estimate=pl.CostEstimate(flops=0, bytes_accessed=0, transcendentals=0),
        name=name,
    )(*args)


def shards(activations, key_grad, momentum, block_ids, counts, *, replicas, group):
    tokens, features = activations.shape
    cols = key_grad.shape[1]
    chips = group // 2

    def along(x, step):
        return lax.ppermute(x, "tensor", [(i, (i + 2 * step) % group) for i in range(group)])

    def swap(x):
        return lax.ppermute(x, "tensor", [(i, i ^ 1) for i in range(group)])

    cut = tokens * 2 // 5 // 16 * 16
    head, tail = activations[:cut], activations[cut:]
    left_head, right_tail = along(head, 1), along(tail, -1)

    rows = jax.ShapeDtypeStruct((chips * tokens, cols), jnp.bfloat16)
    own_keys, sent_keys = call(
        functools.partial(keys_kernel, chips, tokens), "keys", (rows, rows), key_grad
    )

    head, tail, own_keys, sent_keys, block_ids, counts = lax.optimization_barrier(
        (head, tail, own_keys, sent_keys, block_ids, counts)
    )
    left_tail, right_head = along(tail, 1), along(head, -1)
    their_keys = swap(sent_keys)

    left_head, right_tail, block, own_keys, momentum = lax.optimization_barrier(
        (left_head, right_tail, activations, own_keys, momentum)
    )
    far_head, far_tail = along(left_head, 1), along(right_tail, -1)
    own_keys = own_keys.reshape(chips, tokens, cols)
    their_keys = their_keys.reshape(chips, tokens, cols)
    keys = lax.optimization_barrier(jnp.concatenate([own_keys, their_keys], axis=2))
    before, after = keys[chips - 1], keys[1]
    near = (
        gram(block, keys[0])
        + gram(left_head, before[:cut])
        + gram(left_tail, before[cut:])
        + gram(right_tail, after[cut:])
        + gram(right_head, after[:cut])
    )
    own_near = near[:, :cols] + 0.999 * momentum[0]
    their_near = near[:, cols:]
    own_far, their_far = own_keys[2], their_keys[2]

    def whole(total, far):
        return total + gram(far_head, far[:cut]) + gram(far_tail, far[cut:])

    flat = jax.ShapeDtypeStruct((features, cols), jnp.float32)
    flat_half = jax.ShapeDtypeStruct((features, cols), jnp.bfloat16)
    height = features // ROW_GROUPS
    lines = np.arange(cols)
    base = SPAN * (lines // (2 * block_ids.shape[3])) + lines % 2
    mask, picks, numbers = call(
        routes_kernel,
        "routes",
        (
            flat_half,
            jax.ShapeDtypeStruct((2 * ROW_GROUPS * cols, height), jnp.bfloat16),
            jax.ShapeDtypeStruct((ROW_GROUPS * cols, cols), jnp.bfloat16),
        ),
        jnp.transpose(block_ids[0], (2, 1, 0)),
        counts,
        jnp.asarray(np.repeat(base[:, None], cols, axis=1).astype(np.float32)),
        places=[SMEM, SMEM, VMEM],
    )

    (own_near, their_near, own_far, their_far, mask, picks, numbers, far_head, far_tail) = (
        lax.optimization_barrier(
            (own_near, their_near, own_far, their_far, mask, picks, numbers, far_head, far_tail)
        )
    )
    other = swap(whole(their_near, their_far).astype(jnp.bfloat16))
    part = whole(own_near, own_far)

    high, low = cosine_parts()
    forward = jnp.asarray(np.concatenate([high, high, low], axis=1))
    backward = jnp.asarray(np.concatenate([high.T, high.T, low.T], axis=1))
    order = np.concatenate([np.arange(0, SPAN, 2), np.arange(1, SPAN, 2)])
    both_high, both_low = (np.kron(np.eye(2, dtype=p.dtype), p[order]) for p in (high, low))
    backward_pair = jnp.asarray(np.concatenate([both_high, both_high, both_low], axis=0))

    message = jax.ShapeDtypeStruct((ROW_GROUPS * cols, 2 * cols), jnp.bfloat16)
    advanced, sent = call(
        spectrum_kernel,
        "spectrum",
        (flat, message),
        part,
        other,
        picks,
        numbers,
        forward,
        scratch=(pltpu.VMEM((features, cols), jnp.bfloat16),),
    )

    def exchange(x):
        return lax.all_to_all(
            x.reshape(replicas, OWN_COLS, x.shape[1]), "dp", 0, 0, tiled=True
        ).reshape(x.shape)

    pieces = exchange(sent)
    (kept,) = call(kept_kernel, "kept", (flat,), advanced, mask, forward, backward)
    (totals,) = call(
        total_kernel,
        "total",
        (jax.ShapeDtypeStruct((replicas * OWN_COLS, height), jnp.bfloat16),),
        pieces,
        backward_pair,
        scratch=(pltpu.VMEM((height, replicas * OWN_COLS), jnp.bfloat16),),
    )
    (update,) = call(turn_kernel, "turn", (flat_half,), exchange(totals))
    return kept[None], update


def solution(mesh):
    in_specs = (
        P(("dp", "tensor"), None),
        P("dp", "tensor"),
        P("dp", None, "tensor"),
        P("dp", None, "tensor", None),
        P("dp"),
    )
    out_specs = (P("dp", None, "tensor"), P(None, "tensor"))
    body = functools.partial(shards, replicas=mesh.shape["dp"], group=mesh.shape["tensor"])
    return jax.shard_map(body, mesh=mesh, in_specs=in_specs, out_specs=out_specs, check_vma=False)
```

```python
import functools

import jax
import jax.numpy as jnp
import ml_dtypes
import numpy as np
from jax import lax
from jax.experimental import pallas as pl
from jax.experimental.pallas import tpu as pltpu
from jax.sharding import PartitionSpec as P

BLK = 32
SPAN = 64
WIDE = 4
ROW_GROUPS = 4
OWN_COLS = 8


def cosine_parts():
    n = np.arange(SPAN, dtype=np.float64)
    table = np.cos(np.pi * (2.0 * n[None, :] + 1.0) * n[:, None] / 128.0) * np.sqrt(2.0 / SPAN)
    table[0] *= np.sqrt(0.5)
    high = table.astype(ml_dtypes.bfloat16)
    low = (table - high.astype(np.float64)).astype(ml_dtypes.bfloat16)
    return high, low


def split(x):
    high = x.astype(jnp.bfloat16)
    return high, (x - high.astype(jnp.float32)).astype(jnp.bfloat16)


def spans_of(ref, i, count):
    first = i * count * SPAN
    return [ref[first + s * SPAN : first + (s + 1) * SPAN, :] for s in range(count)]


def beside(parts):
    return jnp.concatenate(parts, axis=1)


def product(table, parts):
    return jnp.dot(table[...], jnp.concatenate(parts, axis=0), preferred_element_type=jnp.float32)


def put(ref, i, count, value):
    cols = ref.shape[1]
    for s in range(count):
        first = (i * count + s) * SPAN
        ref[first : first + SPAN, :] = value[:, s * cols : (s + 1) * cols].astype(ref.dtype)


def keys_kernel(chips, tokens, keys, own, partner):
    spot = lax.axis_index("tensor")
    chip, core = lax.shift_right_logical(spot, 1), lax.bitwise_and(spot, 1)
    for step in range(chips):
        pair = 2 * lax.bitwise_and(chip + step, chips - 1)
        here = slice(step * tokens, (step + 1) * tokens)
        own[here, :] = keys[pl.ds(pl.multiple_of((pair + core) * tokens, 16), tokens), :]
        partner[here, :] = keys[pl.ds(pl.multiple_of((pair + 1 - core) * tokens, 16), tokens), :]


def routes_kernel(ids, count, base, mask, picks, numbers):
    cols = mask.shape[1]
    spans = mask.shape[0] // SPAN
    most = ids.shape[0]
    each = spans // ROW_GROUPS

    def number(a, b, k):
        return jnp.where(k < count[0], ids[k, b, a], -1)

    block = lax.shift_right_logical(lax.broadcasted_iota(jnp.int32, (SPAN, cols), 0), 1)
    first = lax.broadcasted_iota(jnp.int32, (SPAN, cols), 1) < SPAN

    def body(a, _):
        hit = jnp.zeros((SPAN, cols), jnp.bool_)
        for k in range(most):
            hit = hit | (jnp.where(first, number(a, 0, k), number(a, 1, k)) == block)
        rows = pl.ds(pl.multiple_of(a * SPAN, SPAN), SPAN)
        mask[rows, :] = hit.astype(jnp.float32).astype(mask.dtype)
        return 0

    lax.fori_loop(0, spans, body, 0)

    lane = lax.broadcasted_iota(jnp.int32, (SPAN, cols), 1)
    square = (cols, cols)
    column = lax.broadcasted_iota(jnp.int32, square, 1)
    slot = lax.shift_right_logical(lax.broadcasted_iota(jnp.int32, square, 0), 1)
    double = (column == slot).astype(jnp.float32).astype(jnp.bfloat16)
    place = column.astype(jnp.float32)
    for g in range(ROW_GROUPS):
        halves = []
        for b in range(2):
            line = jnp.full((SPAN, cols), -1, jnp.int32)
            for a in range(each):
                for k in range(most):
                    line = jnp.where(lane == a * most + k, number(g * each + a, b, k), line)
            halves.append(line)
        tile = jnp.concatenate(halves, axis=0).astype(jnp.float32)
        numbers[g * cols : (g + 1) * cols, :] = tile.astype(numbers.dtype)
        twice = jnp.dot(
            double, tile.T.astype(jnp.bfloat16), preferred_element_type=jnp.float32
        )
        for b in range(2):
            own = jnp.broadcast_to(twice[:, b * SPAN : b * SPAN + 1], square)
            target = jnp.where(own < 0.0, -1.0, base[...] + 2.0 * own)
            for i in range(picks.shape[1] // cols):
                picks[(2 * g + b) * cols : (2 * g + b + 1) * cols, i * cols : (i + 1) * cols] = (
                    (target == place + float(i * cols)).astype(jnp.float32).astype(picks.dtype)
                )


def chosen_rows(x, mask, forward, i):
    high, low = split(x)
    keep = beside(spans_of(mask, i, WIDE)).astype(jnp.float32)
    return product(forward, [high, low, high]) * keep


def spectrum_kernel(part, other, picks, numbers, forward, advanced, sent, rows):
    for i in range(part.shape[0] // (SPAN * WIDE)):
        x = beside(
            [
                p + o.astype(jnp.float32)
                for p, o in zip(spans_of(part, i, WIDE), spans_of(other, i, WIDE))
            ]
        )
        put(advanced, i, WIDE, x)
        high, low = split(x)
        put(rows, i, WIDE, product(forward, [high, low, high]))
    cols = part.shape[1]
    height = picks.shape[1]
    first = lax.broadcasted_iota(jnp.int32, (cols, cols), 1) < SPAN
    for g in range(ROW_GROUPS):
        band = rows[g * height : (g + 1) * height, :]
        one, two = (
            jnp.dot(
                picks[(2 * g + b) * cols : (2 * g + b + 1) * cols, :],
                band,
                preferred_element_type=jnp.float32,
            )
            for b in range(2)
        )
        message = slice(g * cols, (g + 1) * cols)
        sent[message, :cols] = jnp.where(first, one, two).T.astype(sent.dtype)
        sent[message, cols:] = numbers[message, :]


def kept_kernel(advanced, mask, forward, backward, kept):
    for i in range(kept.shape[0] // (SPAN * WIDE)):
        x = beside(spans_of(advanced, i, WIDE))
        high, low = split(chosen_rows(x, mask, forward, i))
        put(kept, i, WIDE, x - product(backward, [high, low, high]))


def total_kernel(pieces, backward, totals, placed):
    wide = pieces.shape[1] // 2
    spans = totals.shape[1] // SPAN
    lane = lax.broadcasted_iota(jnp.int32, (BLK, wide), 0).astype(jnp.float32)
    for t in range(pieces.shape[0] // wide):
        values = pieces[t * wide : (t + 1) * wide, :wide].astype(jnp.float32).T
        numbers = pieces[t * wide : (t + 1) * wide, wide:].astype(jnp.float32).T
        most = wide // (2 * spans)
        for a in range(spans):
            upper = jnp.zeros((BLK, wide), jnp.float32)
            lower = upper
            for k in range(most):
                at = a * most + k
                here = numbers[at : at + 1, :] == lane
                upper = jnp.where(here, values[2 * at : 2 * at + 1, :], upper)
                lower = jnp.where(here, values[2 * at + 1 : 2 * at + 2, :], lower)
            both = jnp.concatenate([upper, lower], axis=0)
            placed[a * SPAN : (a + 1) * SPAN, t * wide : (t + 1) * wide] = both.astype(placed.dtype)
    shape = (2 * OWN_COLS, placed.shape[1])
    column = lax.broadcasted_iota(jnp.int32, shape, 1) & (OWN_COLS - 1)
    row = lax.broadcasted_iota(jnp.int32, shape, 0) & (OWN_COLS - 1)
    total = lax.dot_general(
        (column == row).astype(jnp.float32).astype(placed.dtype),
        placed[...],
        (((1,), (1,)), ((), ())),
        preferred_element_type=jnp.float32,
    )
    pair = 2 * SPAN
    for i in range(totals.shape[1] // pair):
        high, low = split(total[:, i * pair : (i + 1) * pair])
        done = jnp.dot(
            jnp.concatenate([high, low, high], axis=1),
            backward[...],
            preferred_element_type=jnp.float32,
        ).astype(totals.dtype)
        for r in range(totals.shape[0] // shape[0]):
            totals[r * shape[0] : (r + 1) * shape[0], i * pair : (i + 1) * pair] = done


def turn_kernel(turned, update):
    cols, height = update.shape[1], turned.shape[1]
    square = (cols, cols)
    same = lax.broadcasted_iota(jnp.int32, square, 0) == lax.broadcasted_iota(
        jnp.int32, square, 1
    )
    same = same.astype(jnp.float32).astype(turned.dtype)
    for g in range(ROW_GROUPS):
        for i in range(height // cols):
            rows = g * height + i * cols
            update[rows : rows + cols, :] = lax.dot_general(
                same,
                turned[g * cols : (g + 1) * cols, i * cols : (i + 1) * cols],
                (((1,), (1,)), ((), ())),
                preferred_element_type=jnp.float32,
            ).astype(update.dtype)


def gram(a, k):
    return lax.dot_general(a, k, (((0,), (0,)), ((), ())), preferred_element_type=jnp.float32)


VMEM, SMEM = (pl.BlockSpec(memory_space=space) for space in (pltpu.VMEM, pltpu.SMEM))


def call(kernel, name, outs, *args, places=None, scratch=()):
    return pl.pallas_call(
        kernel,
        out_shape=outs,
        in_specs=places or [VMEM] * len(args),
        out_specs=(VMEM,) * len(outs),
        scratch_shapes=scratch,
        compiler_params=pltpu.CompilerParams(vmem_limit_bytes=10 << 20),
        cost_estimate=pl.CostEstimate(flops=0, bytes_accessed=0, transcendentals=0),
        name=name,
    )(*args)


def shards(activations, key_grad, momentum, block_ids, counts, *, replicas, group):
    tokens, features = activations.shape
    cols = key_grad.shape[1]
    chips = group // 2

    def along(x, step):
        return lax.ppermute(x, "tensor", [(i, (i + 2 * step) % group) for i in range(group)])

    def swap(x):
        return lax.ppermute(x, "tensor", [(i, i ^ 1) for i in range(group)])

    cut = tokens * 9 // 16 // 16 * 16
    head, tail = activations[:cut], activations[cut:]
    left, right_tail = along(activations, 1), along(tail, -1)

    rows = jax.ShapeDtypeStruct((chips * tokens, cols), jnp.bfloat16)
    own_keys, sent_keys = call(
        functools.partial(keys_kernel, chips, tokens), "keys", (rows, rows), key_grad
    )

    head, own_keys, sent_keys, block_ids, counts = lax.optimization_barrier(
        (head, own_keys, sent_keys, block_ids, counts)
    )
    right_head = along(head, -1)
    their_keys = swap(sent_keys)
    far_tail = along(right_tail, -1)

    left, right_tail, block, own_keys, momentum = lax.optimization_barrier(
        (left, right_tail, activations, own_keys, momentum)
    )
    far_head = along(left[:cut], 1)
    own_keys = own_keys.reshape(chips, tokens, cols)
    their_keys = their_keys.reshape(chips, tokens, cols)
    keys = lax.optimization_barrier(jnp.concatenate([own_keys, their_keys], axis=2))
    before, after = keys[chips - 1], keys[1]
    near = (
        gram(block, keys[0])
        + gram(left, before)
        + gram(right_tail, after[cut:])
        + gram(right_head, after[:cut])
    )
    own_near = near[:, :cols] + 0.999 * momentum[0]
    their_near = near[:, cols:]
    own_far, their_far = own_keys[2], their_keys[2]

    def whole(total, far):
        return total + gram(far_head, far[:cut]) + gram(far_tail, far[cut:])

    flat = jax.ShapeDtypeStruct((features, cols), jnp.float32)
    flat_half = jax.ShapeDtypeStruct((features, cols), jnp.bfloat16)
    height = features // ROW_GROUPS
    lines = np.arange(cols)
    base = SPAN * (lines // (2 * block_ids.shape[3])) + lines % 2
    mask, picks, numbers = call(
        routes_kernel,
        "routes",
        (
            flat_half,
            jax.ShapeDtypeStruct((2 * ROW_GROUPS * cols, height), jnp.bfloat16),
            jax.ShapeDtypeStruct((ROW_GROUPS * cols, cols), jnp.bfloat16),
        ),
        jnp.transpose(block_ids[0], (2, 1, 0)),
        counts,
        jnp.asarray(np.repeat(base[:, None], cols, axis=1).astype(np.float32)),
        places=[SMEM, SMEM, VMEM],
    )

    own_near, their_near, own_far, their_far, picks, numbers = lax.optimization_barrier(
        (own_near, their_near, own_far, their_far, picks, numbers)
    )
    other = swap(whole(their_near, their_far).astype(jnp.bfloat16))
    part = whole(own_near, own_far)

    high, low = cosine_parts()
    forward = jnp.asarray(np.concatenate([high, high, low], axis=1))
    backward = jnp.asarray(np.concatenate([high.T, high.T, low.T], axis=1))
    order = np.concatenate([np.arange(0, SPAN, 2), np.arange(1, SPAN, 2)])
    both_high, both_low = (np.kron(np.eye(2, dtype=p.dtype), p[order]) for p in (high, low))
    backward_pair = jnp.asarray(np.concatenate([both_high, both_high, both_low], axis=0))

    message = jax.ShapeDtypeStruct((ROW_GROUPS * cols, 2 * cols), jnp.bfloat16)
    advanced, sent = call(
        spectrum_kernel,
        "spectrum",
        (flat, message),
        part,
        other,
        picks,
        numbers,
        forward,
        scratch=(pltpu.VMEM((features, cols), jnp.bfloat16),),
    )

    def exchange(x):
        return lax.all_to_all(
            x.reshape(replicas, OWN_COLS, x.shape[1]), "dp", 0, 0, tiled=True
        ).reshape(x.shape)

    pieces = exchange(sent)
    (kept,) = call(kept_kernel, "kept", (flat,), advanced, mask, forward, backward)
    (totals,) = call(
        total_kernel,
        "total",
        (jax.ShapeDtypeStruct((replicas * OWN_COLS, height), jnp.bfloat16),),
        pieces,
        backward_pair,
        scratch=(pltpu.VMEM((height, replicas * OWN_COLS), jnp.bfloat16),),
    )
    (update,) = call(turn_kernel, "turn", (flat_half,), exchange(totals))
    return kept[None], update


def solution(mesh):
    in_specs = (
        P(("dp", "tensor"), None),
        P("dp", "tensor"),
        P("dp", None, "tensor"),
        P("dp", None, "tensor", None),
        P("dp"),
    )
    out_specs = (P("dp", None, "tensor"), P(None, "tensor"))
    body = functools.partial(shards, replicas=mesh.shape["dp"], group=mesh.shape["tensor"])
    return jax.shard_map(body, mesh=mesh, in_specs=in_specs, out_specs=out_specs, check_vma=False)
```

```python
import functools

import jax
import jax.numpy as jnp
import ml_dtypes
import numpy as np
from jax import lax
from jax.experimental import pallas as pl
from jax.experimental.pallas import tpu as pltpu
from jax.sharding import PartitionSpec as P

BLK = 32
SPAN = 64
WIDE = 4
ROW_GROUPS = 4
OWN_COLS = 8
NEAR = (0, 1, 3)
FAR = 2


def cosine_parts():
    n = np.arange(SPAN, dtype=np.float64)
    table = np.cos(np.pi * (2.0 * n[None, :] + 1.0) * n[:, None] / 128.0) * np.sqrt(2.0 / SPAN)
    table[0] *= np.sqrt(0.5)
    high = table.astype(ml_dtypes.bfloat16)
    low = (table - high.astype(np.float64)).astype(ml_dtypes.bfloat16)
    return high, low


def split(x):
    high = x.astype(jnp.bfloat16)
    return high, (x - high.astype(jnp.float32)).astype(jnp.bfloat16)


def spans_of(ref, i, count):
    first = i * count * SPAN
    return [ref[first + s * SPAN : first + (s + 1) * SPAN, :] for s in range(count)]


def beside(parts):
    return jnp.concatenate(parts, axis=1)


def product(table, parts):
    return jnp.dot(table[...], jnp.concatenate(parts, axis=0), preferred_element_type=jnp.float32)


def put(ref, i, count, value):
    cols = ref.shape[1]
    for s in range(count):
        first = (i * count + s) * SPAN
        ref[first : first + SPAN, :] = value[:, s * cols : (s + 1) * cols].astype(ref.dtype)


def keys_kernel(chips, tokens, keys, ids, own, partner, far_own, far_partner):
    spot = lax.axis_index("tensor")
    chip, core = lax.shift_right_logical(spot, 1), lax.bitwise_and(spot, 1)

    def block(step, which):
        first = (2 * lax.bitwise_and(chip + step, chips - 1) + which) * tokens
        return keys[pl.ds(pl.multiple_of(first, 16), tokens), :]

    for place, step in enumerate(NEAR):
        here = slice(place * tokens, (place + 1) * tokens)
        own[here, :] = block(step, core)
        partner[here, :] = block(step, 1 - core)
    far_own[:tokens, :] = block(FAR, core)
    far_partner[...] = block(FAR, 1 - core)
    most, halves, spans = ids.shape
    rows = [ids[k].astype(jnp.float32) for k in range(most)]
    rows.append(jnp.zeros((16 - most * halves, spans), jnp.float32))
    rows = jnp.concatenate(rows, axis=0)
    rows = jnp.concatenate([rows, jnp.zeros((16, far_own.shape[1] - spans), jnp.float32)], axis=1)
    far_own[tokens:, :] = rows.astype(far_own.dtype)


def routes_kernel(ids, count, base, mask, picks, numbers):
    cols = mask.shape[1]
    spans = mask.shape[0] // SPAN
    most = ids.shape[0]
    each = spans // ROW_GROUPS

    def number(a, b, k):
        return jnp.where(k < count[0], ids[k, b, a], -1)

    block = lax.shift_right_logical(lax.broadcasted_iota(jnp.int32, (SPAN, cols), 0), 1)
    first = lax.broadcasted_iota(jnp.int32, (SPAN, cols), 1) < SPAN

    def body(a, _):
        hit = jnp.zeros((SPAN, cols), jnp.bool_)
        for k in range(most):
            hit = hit | (jnp.where(first, number(a, 0, k), number(a, 1, k)) == block)
        rows = pl.ds(pl.multiple_of(a * SPAN, SPAN), SPAN)
        mask[rows, :] = hit.astype(jnp.float32).astype(mask.dtype)
        return 0

    lax.fori_loop(0, spans, body, 0)

    lane = lax.broadcasted_iota(jnp.int32, (SPAN, cols), 1)
    square = (cols, cols)
    column = lax.broadcasted_iota(jnp.int32, square, 1)
    slot = lax.shift_right_logical(lax.broadcasted_iota(jnp.int32, square, 0), 1)
    double = (column == slot).astype(jnp.float32).astype(jnp.bfloat16)
    place = column.astype(jnp.float32)
    for g in range(ROW_GROUPS):
        halves = []
        for b in range(2):
            line = jnp.full((SPAN, cols), -1, jnp.int32)
            for a in range(each):
                for k in range(most):
                    line = jnp.where(lane == a * most + k, number(g * each + a, b, k), line)
            halves.append(line)
        tile = jnp.concatenate(halves, axis=0).astype(jnp.float32)
        numbers[g * cols : (g + 1) * cols, :] = tile.astype(numbers.dtype)
        twice = jnp.dot(
            double, tile.T.astype(jnp.bfloat16), preferred_element_type=jnp.float32
        )
        for b in range(2):
            own = jnp.broadcast_to(twice[:, b * SPAN : b * SPAN + 1], square)
            target = jnp.where(own < 0.0, -1.0, base[...] + 2.0 * own)
            for i in range(picks.shape[1] // cols):
                picks[(2 * g + b) * cols : (2 * g + b + 1) * cols, i * cols : (i + 1) * cols] = (
                    (target == place + float(i * cols)).astype(jnp.float32).astype(picks.dtype)
                )


def chosen_rows(x, mask, forward, i):
    high, low = split(x)
    keep = beside(spans_of(mask, i, WIDE)).astype(jnp.float32)
    return product(forward, [high, low, high]) * keep


def chosen(picks, rows, group, first):
    cols = rows.shape[1]
    height = picks.shape[1]
    band = rows[group * height : (group + 1) * height, :]
    one, two = (
        jnp.dot(
            picks[(2 * group + b) * cols : (2 * group + b + 1) * cols, :],
            band,
            preferred_element_type=jnp.float32,
        )
        for b in range(2)
    )
    return jnp.where(first, one, two)


def left_half(cols):
    return lax.broadcasted_iota(jnp.int32, (cols, cols), 1) < SPAN


def far_kernel(
    numbers, count, spans, slots, base, part, other, forward, whole, sent, picks, rows
):
    cols = part.shape[1]
    height = picks.shape[1]
    square = (cols, cols)
    known = numbers[...].astype(jnp.float32)
    known = jnp.concatenate(
        [known, jnp.zeros((cols - known.shape[0], cols), jnp.float32)], axis=0
    ).T.astype(jnp.bfloat16)
    place = lax.broadcasted_iota(jnp.int32, square, 1).astype(jnp.float32)
    ones = jnp.ones(square, jnp.bfloat16)
    slot = slots[...]
    active = slot < count[0].astype(jnp.float32)
    for g in range(ROW_GROUPS):
        by_span = jnp.dot(
            spans[g * cols : (g + 1) * cols, :], known, preferred_element_type=jnp.float32
        )
        for b in range(2):
            single = jnp.where(place == 2.0 * slot + float(b), by_span, 0.0)
            own = jnp.dot(
                single.astype(jnp.bfloat16), ones, preferred_element_type=jnp.float32
            )
            target = jnp.where(active, base[...] + 2.0 * own, -1.0)
            for i in range(height // cols):
                picks[(2 * g + b) * cols : (2 * g + b + 1) * cols, i * cols : (i + 1) * cols] = (
                    (target == place + float(i * cols)).astype(jnp.float32).astype(picks.dtype)
                )
    for i in range(part.shape[0] // (SPAN * WIDE)):
        x = beside(
            [
                p + o.astype(jnp.float32)
                for p, o in zip(spans_of(part, i, WIDE), spans_of(other, i, WIDE))
            ]
        )
        put(whole, i, WIDE, x)
        high, low = split(x)
        put(rows, i, WIDE, product(forward, [high, low, high]))
    first = left_half(cols)
    for g in range(ROW_GROUPS):
        sent[g * cols : (g + 1) * cols, :] = chosen(picks, rows, g, first).astype(sent.dtype)


def spectrum_kernel(part, other, far, picks, numbers, forward, advanced, sent, rows):
    for i in range(part.shape[0] // (SPAN * WIDE)):
        x = beside(
            [
                p + o.astype(jnp.float32)
                for p, o in zip(spans_of(part, i, WIDE), spans_of(other, i, WIDE))
            ]
        )
        put(advanced, i, WIDE, x)
        high, low = split(x)
        put(rows, i, WIDE, product(forward, [high, low, high]))
    cols = part.shape[1]
    first = left_half(cols)
    for g in range(ROW_GROUPS):
        message = slice(g * cols, (g + 1) * cols)
        total = chosen(picks, rows, g, first) + far[message, :].astype(jnp.float32)
        sent[message, :cols] = total.T.astype(sent.dtype)
        sent[message, cols:] = numbers[message, :]


def kept_kernel(advanced, far, mask, forward, backward, kept):
    for i in range(kept.shape[0] // (SPAN * WIDE)):
        x = beside(
            [
                n + f.astype(jnp.float32)
                for n, f in zip(spans_of(advanced, i, WIDE), spans_of(far, i, WIDE))
            ]
        )
        high, low = split(chosen_rows(x, mask, forward, i))
        put(kept, i, WIDE, x - product(backward, [high, low, high]))


def total_kernel(pieces, backward, totals, placed):
    wide = pieces.shape[1] // 2
    spans = totals.shape[1] // SPAN
    lane = lax.broadcasted_iota(jnp.int32, (BLK, wide), 0).astype(jnp.float32)
    for t in range(pieces.shape[0] // wide):
        values = pieces[t * wide : (t + 1) * wide, :wide].astype(jnp.float32).T
        numbers = pieces[t * wide : (t + 1) * wide, wide:].astype(jnp.float32).T
        most = wide // (2 * spans)
        for a in range(spans):
            upper = jnp.zeros((BLK, wide), jnp.float32)
            lower = upper
            for k in range(most):
                at = a * most + k
                here = numbers[at : at + 1, :] == lane
                upper = jnp.where(here, values[2 * at : 2 * at + 1, :], upper)
                lower = jnp.where(here, values[2 * at + 1 : 2 * at + 2, :], lower)
            both = jnp.concatenate([upper, lower], axis=0)
            placed[a * SPAN : (a + 1) * SPAN, t * wide : (t + 1) * wide] = both.astype(placed.dtype)
    shape = (2 * OWN_COLS, placed.shape[1])
    column = lax.broadcasted_iota(jnp.int32, shape, 1) & (OWN_COLS - 1)
    row = lax.broadcasted_iota(jnp.int32, shape, 0) & (OWN_COLS - 1)
    total = lax.dot_general(
        (column == row).astype(jnp.float32).astype(placed.dtype),
        placed[...],
        (((1,), (1,)), ((), ())),
        preferred_element_type=jnp.float32,
    )
    pair = 2 * SPAN
    for i in range(totals.shape[1] // pair):
        high, low = split(total[:, i * pair : (i + 1) * pair])
        done = jnp.dot(
            jnp.concatenate([high, low, high], axis=1),
            backward[...],
            preferred_element_type=jnp.float32,
        ).astype(totals.dtype)
        for r in range(totals.shape[0] // shape[0]):
            totals[r * shape[0] : (r + 1) * shape[0], i * pair : (i + 1) * pair] = done


def turn_kernel(turned, update):
    cols, height = update.shape[1], turned.shape[1]
    for g in range(ROW_GROUPS):
        for i in range(height // cols):
            rows = g * height + i * cols
            block = turned[g * cols : (g + 1) * cols, i * cols : (i + 1) * cols]
            update[rows : rows + cols, :] = block.astype(jnp.float32).T.astype(update.dtype)


def gram(a, k):
    return lax.dot_general(a, k, (((0,), (0,)), ((), ())), preferred_element_type=jnp.float32)


VMEM, SMEM = (pl.BlockSpec(memory_space=space) for space in (pltpu.VMEM, pltpu.SMEM))


def call(kernel, name, outs, *args, places=None, scratch=()):
    return pl.pallas_call(
        kernel,
        out_shape=outs,
        in_specs=places or [VMEM] * len(args),
        out_specs=(VMEM,) * len(outs),
        scratch_shapes=scratch,
        compiler_params=pltpu.CompilerParams(vmem_limit_bytes=10 << 20),
        cost_estimate=pl.CostEstimate(flops=0, bytes_accessed=0, transcendentals=0),
        name=name,
    )(*args)


def shards(activations, key_grad, momentum, block_ids, counts, *, replicas, group):
    tokens, features = activations.shape
    cols = key_grad.shape[1]
    chips = group // 2

    def along(x, step, across=False):
        pairs = [(i, ((i + 2 * step) % group) ^ int(across)) for i in range(group)]
        return lax.ppermute(x, "tensor", pairs)

    def swap(x):
        return lax.ppermute(x, "tensor", [(i, i ^ 1) for i in range(group)])

    near_rows = jax.ShapeDtypeStruct((len(NEAR) * tokens, cols), jnp.bfloat16)
    ids = jnp.transpose(block_ids[0], (2, 1, 0))
    own_keys, partner_keys, far_own, far_partner = call(
        functools.partial(keys_kernel, chips, tokens),
        "keys",
        (
            near_rows,
            near_rows,
            jax.ShapeDtypeStruct((tokens + 16, cols), jnp.bfloat16),
            jax.ShapeDtypeStruct((tokens, cols), jnp.bfloat16),
        ),
        key_grad,
        ids,
    )
    far_own, far_partner = along(far_own, FAR), along(far_partner, FAR, across=True)
    left, right = along(activations, 1), along(activations, -1)

    far_other = swap(gram(activations, far_partner).astype(jnp.bfloat16))
    far_part = gram(activations, far_own[:tokens])
    their_keys = swap(partner_keys)

    flat = jax.ShapeDtypeStruct((features, cols), jnp.float32)
    flat_half = jax.ShapeDtypeStruct((features, cols), jnp.bfloat16)
    high, low = cosine_parts()
    forward = jnp.asarray(np.concatenate([high, high, low], axis=1))
    backward = jnp.asarray(np.concatenate([high.T, high.T, low.T], axis=1))
    height = features // ROW_GROUPS
    lines = np.arange(cols)
    base = SPAN * (lines // (2 * block_ids.shape[3])) + lines % 2
    base = jnp.asarray(np.repeat(base[:, None], cols, axis=1).astype(np.float32))
    picks_shape = (2 * ROW_GROUPS * cols, height)
    mask, picks, numbers = call(
        routes_kernel,
        "routes",
        (
            flat_half,
            jax.ShapeDtypeStruct(picks_shape, jnp.bfloat16),
            jax.ShapeDtypeStruct((ROW_GROUPS * cols, cols), jnp.bfloat16),
        ),
        ids,
        counts,
        base,
        places=[SMEM, SMEM, VMEM],
    )

    most = block_ids.shape[3]
    span = lines // (2 * most)
    each = features // SPAN // ROW_GROUPS
    span_table = np.concatenate(
        [(span[:, None] + g * each == lines) & (span[:, None] < each) for g in range(ROW_GROUPS)]
    )
    slot_table = np.where(span < each, lines % (2 * most) // 2, most)
    slot_table = np.repeat(slot_table[:, None], cols, axis=1)
    far_whole, far_sent = call(
        far_kernel,
        "far",
        (flat_half, jax.ShapeDtypeStruct((ROW_GROUPS * cols, cols), jnp.bfloat16)),
        far_own[tokens:],
        counts,
        jnp.asarray(span_table.astype(np.float32).astype(ml_dtypes.bfloat16)),
        jnp.asarray(slot_table.astype(np.float32)),
        base,
        far_part,
        far_other,
        forward,
        places=[VMEM, SMEM] + [VMEM] * 6,
        scratch=(
            pltpu.VMEM(picks_shape, jnp.bfloat16),
            pltpu.VMEM((features, cols), jnp.bfloat16),
        ),
    )
    far_sent = along(far_sent, FAR)

    keys = jnp.concatenate([own_keys, their_keys], axis=1)
    keys = lax.optimization_barrier(keys.reshape(len(NEAR), tokens, 2 * cols))
    left, right, far_whole = lax.optimization_barrier((left, right, far_whole))
    far_whole = along(far_whole, FAR)
    near = gram(activations, keys[0]) + gram(right, keys[1]) + gram(left, keys[2])
    other = swap(near[:, cols:].astype(jnp.bfloat16))
    part = near[:, :cols] + 0.999 * momentum[0]

    order = np.concatenate([np.arange(0, SPAN, 2), np.arange(1, SPAN, 2)])
    both_high, both_low = (np.kron(np.eye(2, dtype=p.dtype), p[order]) for p in (high, low))
    backward_pair = jnp.asarray(np.concatenate([both_high, both_high, both_low], axis=0))

    message = jax.ShapeDtypeStruct((ROW_GROUPS * cols, 2 * cols), jnp.bfloat16)
    advanced, sent = call(
        spectrum_kernel,
        "spectrum",
        (flat, message),
        part,
        other,
        far_sent,
        picks,
        numbers,
        forward,
        scratch=(pltpu.VMEM((features, cols), jnp.bfloat16),),
    )

    def exchange(x):
        return lax.all_to_all(
            x.reshape(replicas, OWN_COLS, x.shape[1]), "dp", 0, 0, tiled=True
        ).reshape(x.shape)

    pieces = exchange(sent)
    (kept,) = call(kept_kernel, "kept", (flat,), advanced, far_whole, mask, forward, backward)
    (totals,) = call(
        total_kernel,
        "total",
        (jax.ShapeDtypeStruct((replicas * OWN_COLS, height), jnp.bfloat16),),
        pieces,
        backward_pair,
        scratch=(pltpu.VMEM((height, replicas * OWN_COLS), jnp.bfloat16),),
    )
    (update,) = call(turn_kernel, "turn", (flat_half,), exchange(totals))
    return kept[None], update


def solution(mesh):
    in_specs = (
        P(("dp", "tensor"), None),
        P("dp", "tensor"),
        P("dp", None, "tensor"),
        P("dp", None, "tensor", None),
        P("dp"),
    )
    out_specs = (P("dp", None, "tensor"), P(None, "tensor"))
    body = functools.partial(shards, replicas=mesh.shape["dp"], group=mesh.shape["tensor"])
    return jax.shard_map(body, mesh=mesh, in_specs=in_specs, out_specs=out_specs, check_vma=False)
```

```python
import functools

import jax
import jax.numpy as jnp
import ml_dtypes
import numpy as np
from jax import lax
from jax.experimental import pallas as pl
from jax.experimental.pallas import tpu as pltpu
from jax.sharding import PartitionSpec as P

BLK = 32
SPAN = 64
WIDE = 4
ROW_GROUPS = 4
OWN_COLS = 8
NEAR = (0, 1, 3)
FAR = 2


def cosine_parts():
    n = np.arange(SPAN, dtype=np.float64)
    table = np.cos(np.pi * (2.0 * n[None, :] + 1.0) * n[:, None] / 128.0) * np.sqrt(2.0 / SPAN)
    table[0] *= np.sqrt(0.5)
    high = table.astype(ml_dtypes.bfloat16)
    low = (table - high.astype(np.float64)).astype(ml_dtypes.bfloat16)
    return high, low


def split(x):
    high = x.astype(jnp.bfloat16)
    return high, (x - high.astype(jnp.float32)).astype(jnp.bfloat16)


def spans_of(ref, i, count):
    first = i * count * SPAN
    return [ref[first + s * SPAN : first + (s + 1) * SPAN, :] for s in range(count)]


def beside(parts):
    return jnp.concatenate(parts, axis=1)


def product(table, parts):
    return jnp.dot(table[...], jnp.concatenate(parts, axis=0), preferred_element_type=jnp.float32)


def put(ref, i, count, value):
    cols = ref.shape[1]
    for s in range(count):
        first = (i * count + s) * SPAN
        ref[first : first + SPAN, :] = value[:, s * cols : (s + 1) * cols].astype(ref.dtype)


def keys_kernel(chips, tokens, keys, ids, own, partner, far):
    spot = lax.axis_index("tensor")
    chip, core = lax.shift_right_logical(spot, 1), lax.bitwise_and(spot, 1)

    def first(step, which):
        block = 2 * lax.bitwise_and(chip + step, chips - 1) + which
        return pl.multiple_of(block * tokens, 16)

    for place, step in enumerate(NEAR):
        here = slice(place * tokens, (place + 1) * tokens)
        own[here, :] = keys[pl.ds(first(step, core), tokens), :]
        partner[here, :] = keys[pl.ds(first(step, 1 - core), tokens), :]
    far[: 2 * tokens, :] = keys[pl.ds(first(FAR, 0), 2 * tokens), :]
    most, halves, spans = ids.shape
    wide = far.shape[1]
    rows = [ids[k].astype(jnp.float32) for k in range(most)]
    rows.append(jnp.zeros((16 - most * halves, spans), jnp.float32))
    rows = jnp.concatenate(rows, axis=0)
    rows = jnp.concatenate([rows, jnp.zeros((16, wide - spans), jnp.float32)], axis=1)
    far[2 * tokens :, :] = rows.astype(far.dtype)


def pair_kernel(tokens, far, mine, theirs):
    core = lax.bitwise_and(lax.axis_index("tensor"), 1)
    mine[...] = far[pl.ds(pl.multiple_of(core * tokens, 16), tokens), :]
    theirs[...] = far[pl.ds(pl.multiple_of((1 - core) * tokens, 16), tokens), :]


def routes_kernel(ids, count, base, mask, picks, numbers):
    cols = mask.shape[1]
    spans = mask.shape[0] // SPAN
    most = ids.shape[0]
    each = spans // ROW_GROUPS

    def number(a, b, k):
        return jnp.where(k < count[0], ids[k, b, a], -1)

    block = lax.shift_right_logical(lax.broadcasted_iota(jnp.int32, (SPAN, cols), 0), 1)
    first = lax.broadcasted_iota(jnp.int32, (SPAN, cols), 1) < SPAN

    def body(a, _):
        hit = jnp.zeros((SPAN, cols), jnp.bool_)
        for k in range(most):
            hit = hit | (jnp.where(first, number(a, 0, k), number(a, 1, k)) == block)
        rows = pl.ds(pl.multiple_of(a * SPAN, SPAN), SPAN)
        mask[rows, :] = hit.astype(jnp.float32).astype(mask.dtype)
        return 0

    lax.fori_loop(0, spans, body, 0)

    lane = lax.broadcasted_iota(jnp.int32, (SPAN, cols), 1)
    square = (cols, cols)
    column = lax.broadcasted_iota(jnp.int32, square, 1)
    slot = lax.shift_right_logical(lax.broadcasted_iota(jnp.int32, square, 0), 1)
    double = (column == slot).astype(jnp.float32).astype(jnp.bfloat16)
    place = column.astype(jnp.float32)
    for g in range(ROW_GROUPS):
        halves = []
        for b in range(2):
            line = jnp.full((SPAN, cols), -1, jnp.int32)
            for a in range(each):
                for k in range(most):
                    line = jnp.where(lane == a * most + k, number(g * each + a, b, k), line)
            halves.append(line)
        tile = jnp.concatenate(halves, axis=0).astype(jnp.float32)
        numbers[g * cols : (g + 1) * cols, :] = tile.astype(numbers.dtype)
        twice = jnp.dot(
            double, tile.T.astype(jnp.bfloat16), preferred_element_type=jnp.float32
        )
        for b in range(2):
            own = jnp.broadcast_to(twice[:, b * SPAN : b * SPAN + 1], square)
            target = jnp.where(own < 0.0, -1.0, base[...] + 2.0 * own)
            for i in range(picks.shape[1] // cols):
                picks[(2 * g + b) * cols : (2 * g + b + 1) * cols, i * cols : (i + 1) * cols] = (
                    (target == place + float(i * cols)).astype(jnp.float32).astype(picks.dtype)
                )


def chosen_rows(x, mask, forward, i):
    high, low = split(x)
    keep = beside(spans_of(mask, i, WIDE)).astype(jnp.float32)
    return product(forward, [high, low, high]) * keep


def chosen(picks, rows, group, first):
    cols = rows.shape[1]
    height = picks.shape[1]
    band = rows[group * height : (group + 1) * height, :]
    one, two = (
        jnp.dot(
            picks[(2 * group + b) * cols : (2 * group + b + 1) * cols, :],
            band,
            preferred_element_type=jnp.float32,
        )
        for b in range(2)
    )
    return jnp.where(first, one, two)


def left_half(cols):
    return lax.broadcasted_iota(jnp.int32, (cols, cols), 1) < SPAN


def far_kernel(
    numbers, count, spans, slots, base, part, other, forward, whole, sent, picks, rows
):
    cols = part.shape[1]
    height = picks.shape[1]
    square = (cols, cols)
    known = numbers[...].astype(jnp.float32)
    known = jnp.concatenate(
        [known, jnp.zeros((cols - known.shape[0], cols), jnp.float32)], axis=0
    ).T.astype(jnp.bfloat16)
    place = lax.broadcasted_iota(jnp.int32, square, 1).astype(jnp.float32)
    ones = jnp.ones(square, jnp.bfloat16)
    slot = slots[...]
    active = slot < count[0].astype(jnp.float32)
    for g in range(ROW_GROUPS):
        by_span = jnp.dot(
            spans[g * cols : (g + 1) * cols, :], known, preferred_element_type=jnp.float32
        )
        for b in range(2):
            single = jnp.where(place == 2.0 * slot + float(b), by_span, 0.0)
            own = jnp.dot(
                single.astype(jnp.bfloat16), ones, preferred_element_type=jnp.float32
            )
            target = jnp.where(active, base[...] + 2.0 * own, -1.0)
            for i in range(height // cols):
                picks[(2 * g + b) * cols : (2 * g + b + 1) * cols, i * cols : (i + 1) * cols] = (
                    (target == place + float(i * cols)).astype(jnp.float32).astype(picks.dtype)
                )
    for i in range(part.shape[0] // (SPAN * WIDE)):
        x = beside(
            [
                p + o.astype(jnp.float32)
                for p, o in zip(spans_of(part, i, WIDE), spans_of(other, i, WIDE))
            ]
        )
        put(whole, i, WIDE, x)
        high, low = split(x)
        put(rows, i, WIDE, product(forward, [high, low, high]))
    first = left_half(cols)
    for g in range(ROW_GROUPS):
        sent[g * cols : (g + 1) * cols, :] = chosen(picks, rows, g, first).astype(sent.dtype)


def spectrum_kernel(part, other, far, picks, numbers, forward, advanced, sent, rows):
    for i in range(part.shape[0] // (SPAN * WIDE)):
        x = beside(
            [
                p + o.astype(jnp.float32)
                for p, o in zip(spans_of(part, i, WIDE), spans_of(other, i, WIDE))
            ]
        )
        put(advanced, i, WIDE, x)
        high, low = split(x)
        put(rows, i, WIDE, product(forward, [high, low, high]))
    cols = part.shape[1]
    first = left_half(cols)
    for g in range(ROW_GROUPS):
        message = slice(g * cols, (g + 1) * cols)
        total = chosen(picks, rows, g, first) + far[message, :].astype(jnp.float32)
        sent[message, :cols] = total.T.astype(sent.dtype)
        sent[message, cols:] = numbers[message, :]


def kept_kernel(advanced, far, mask, forward, backward, kept):
    for i in range(kept.shape[0] // (SPAN * WIDE)):
        x = beside(
            [
                n + f.astype(jnp.float32)
                for n, f in zip(spans_of(advanced, i, WIDE), spans_of(far, i, WIDE))
            ]
        )
        high, low = split(chosen_rows(x, mask, forward, i))
        put(kept, i, WIDE, x - product(backward, [high, low, high]))


def total_kernel(pieces, backward, totals, placed):
    wide = pieces.shape[1] // 2
    spans = totals.shape[1] // SPAN
    lane = lax.broadcasted_iota(jnp.int32, (BLK, wide), 0).astype(jnp.float32)
    for t in range(pieces.shape[0] // wide):
        values = pieces[t * wide : (t + 1) * wide, :wide].astype(jnp.float32).T
        numbers = pieces[t * wide : (t + 1) * wide, wide:].astype(jnp.float32).T
        most = wide // (2 * spans)
        for a in range(spans):
            upper = jnp.zeros((BLK, wide), jnp.float32)
            lower = upper
            for k in range(most):
                at = a * most + k
                here = numbers[at : at + 1, :] == lane
                upper = jnp.where(here, values[2 * at : 2 * at + 1, :], upper)
                lower = jnp.where(here, values[2 * at + 1 : 2 * at + 2, :], lower)
            both = jnp.concatenate([upper, lower], axis=0)
            placed[a * SPAN : (a + 1) * SPAN, t * wide : (t + 1) * wide] = both.astype(placed.dtype)
    shape = (2 * OWN_COLS, placed.shape[1])
    column = lax.broadcasted_iota(jnp.int32, shape, 1) & (OWN_COLS - 1)
    row = lax.broadcasted_iota(jnp.int32, shape, 0) & (OWN_COLS - 1)
    total = lax.dot_general(
        (column == row).astype(jnp.float32).astype(placed.dtype),
        placed[...],
        (((1,), (1,)), ((), ())),
        preferred_element_type=jnp.float32,
    )
    pair = 2 * SPAN
    for i in range(totals.shape[1] // pair):
        high, low = split(total[:, i * pair : (i + 1) * pair])
        done = jnp.dot(
            jnp.concatenate([high, low, high], axis=1),
            backward[...],
            preferred_element_type=jnp.float32,
        ).astype(totals.dtype)
        for r in range(totals.shape[0] // shape[0]):
            totals[r * shape[0] : (r + 1) * shape[0], i * pair : (i + 1) * pair] = done


def turn_kernel(turned, update):
    cols, height = update.shape[1], turned.shape[1]
    for g in range(ROW_GROUPS):
        for i in range(height // cols):
            rows = g * height + i * cols
            block = turned[g * cols : (g + 1) * cols, i * cols : (i + 1) * cols]
            update[rows : rows + cols, :] = block.astype(jnp.float32).T.astype(update.dtype)


def gram(a, k):
    return lax.dot_general(a, k, (((0,), (0,)), ((), ())), preferred_element_type=jnp.float32)


VMEM, SMEM = (pl.BlockSpec(memory_space=space) for space in (pltpu.VMEM, pltpu.SMEM))


def call(kernel, name, outs, *args, places=None, scratch=()):
    return pl.pallas_call(
        kernel,
        out_shape=outs,
        in_specs=places or [VMEM] * len(args),
        out_specs=(VMEM,) * len(outs),
        scratch_shapes=scratch,
        compiler_params=pltpu.CompilerParams(vmem_limit_bytes=10 << 20),
        cost_estimate=pl.CostEstimate(flops=0, bytes_accessed=0, transcendentals=0),
        name=name,
    )(*args)


def shards(activations, key_grad, momentum, block_ids, counts, *, replicas, group):
    tokens, features = activations.shape
    cols = key_grad.shape[1]
    chips = group // 2

    def along(x, step):
        return lax.ppermute(x, "tensor", [(i, (i + 2 * step) % group) for i in range(group)])

    def swap(x):
        return lax.ppermute(x, "tensor", [(i, i ^ 1) for i in range(group)])

    near_rows = jax.ShapeDtypeStruct((len(NEAR) * tokens, cols), jnp.bfloat16)
    far_rows = jax.ShapeDtypeStruct((2 * tokens + 16, cols), jnp.bfloat16)
    ids = jnp.transpose(block_ids[0], (2, 1, 0))
    own_keys, partner_keys, far_keys = call(
        functools.partial(keys_kernel, chips, tokens),
        "keys",
        (near_rows, near_rows, far_rows),
        key_grad,
        ids,
    )
    far_keys = along(far_keys, FAR)
    activations, own_keys, partner_keys = lax.optimization_barrier(
        (activations, own_keys, partner_keys)
    )
    left, right = along(activations, 1), along(activations, -1)

    block_rows = jax.ShapeDtypeStruct((tokens, cols), jnp.bfloat16)
    far_own, far_theirs = call(
        functools.partial(pair_kernel, tokens), "pair", (block_rows, block_rows), far_keys
    )
    far_theirs = swap(far_theirs)
    far_other = swap(gram(activations, far_theirs).astype(jnp.bfloat16))
    far_part = gram(activations, far_own)
    their_keys = swap(partner_keys)

    flat = jax.ShapeDtypeStruct((features, cols), jnp.float32)
    flat_half = jax.ShapeDtypeStruct((features, cols), jnp.bfloat16)
    high, low = cosine_parts()
    forward = jnp.asarray(np.concatenate([high, high, low], axis=1))
    backward = jnp.asarray(np.concatenate([high.T, high.T, low.T], axis=1))
    height = features // ROW_GROUPS
    lines = np.arange(cols)
    base = SPAN * (lines // (2 * block_ids.shape[3])) + lines % 2
    base = jnp.asarray(np.repeat(base[:, None], cols, axis=1).astype(np.float32))
    picks_shape = (2 * ROW_GROUPS * cols, height)
    mask, picks, numbers = call(
        routes_kernel,
        "routes",
        (
            flat_half,
            jax.ShapeDtypeStruct(picks_shape, jnp.bfloat16),
            jax.ShapeDtypeStruct((ROW_GROUPS * cols, cols), jnp.bfloat16),
        ),
        ids,
        counts,
        base,
        places=[SMEM, SMEM, VMEM],
    )

    most = block_ids.shape[3]
    span = lines // (2 * most)
    each = features // SPAN // ROW_GROUPS
    span_table = np.concatenate(
        [(span[:, None] + g * each == lines) & (span[:, None] < each) for g in range(ROW_GROUPS)]
    )
    slot_table = np.where(span < each, lines % (2 * most) // 2, most)
    slot_table = np.repeat(slot_table[:, None], cols, axis=1)
    far_whole, far_sent = call(
        far_kernel,
        "far",
        (flat_half, jax.ShapeDtypeStruct((ROW_GROUPS * cols, cols), jnp.bfloat16)),
        far_keys[2 * tokens :],
        counts,
        jnp.asarray(span_table.astype(np.float32).astype(ml_dtypes.bfloat16)),
        jnp.asarray(slot_table.astype(np.float32)),
        base,
        far_part,
        far_other,
        forward,
        places=[VMEM, SMEM] + [VMEM] * 6,
        scratch=(
            pltpu.VMEM(picks_shape, jnp.bfloat16),
            pltpu.VMEM((features, cols), jnp.bfloat16),
        ),
    )
    far_sent = along(far_sent, FAR)

    keys = jnp.concatenate([own_keys, their_keys], axis=1)
    keys = lax.optimization_barrier(keys.reshape(len(NEAR), tokens, 2 * cols))
    left, right, far_whole = lax.optimization_barrier((left, right, far_whole))
    far_whole = along(far_whole, FAR)
    near = gram(activations, keys[0]) + gram(right, keys[1]) + gram(left, keys[2])
    other = swap(near[:, cols:].astype(jnp.bfloat16))
    part = near[:, :cols] + 0.999 * momentum[0]

    order = np.concatenate([np.arange(0, SPAN, 2), np.arange(1, SPAN, 2)])
    both_high, both_low = (np.kron(np.eye(2, dtype=p.dtype), p[order]) for p in (high, low))
    backward_pair = jnp.asarray(np.concatenate([both_high, both_high, both_low], axis=0))

    message = jax.ShapeDtypeStruct((ROW_GROUPS * cols, 2 * cols), jnp.bfloat16)
    advanced, sent = call(
        spectrum_kernel,
        "spectrum",
        (flat, message),
        part,
        other,
        far_sent,
        picks,
        numbers,
        forward,
        scratch=(pltpu.VMEM((features, cols), jnp.bfloat16),),
    )

    def exchange(x):
        return lax.all_to_all(
            x.reshape(replicas, OWN_COLS, x.shape[1]), "dp", 0, 0, tiled=True
        ).reshape(x.shape)

    pieces, far_whole = lax.optimization_barrier((exchange(sent), far_whole))
    (kept,) = call(kept_kernel, "kept", (flat,), advanced, far_whole, mask, forward, backward)
    (totals,) = call(
        total_kernel,
        "total",
        (jax.ShapeDtypeStruct((replicas * OWN_COLS, height), jnp.bfloat16),),
        pieces,
        backward_pair,
        scratch=(pltpu.VMEM((height, replicas * OWN_COLS), jnp.bfloat16),),
    )
    (update,) = call(turn_kernel, "turn", (flat_half,), exchange(totals))
    return kept[None], update


def solution(mesh):
    in_specs = (
        P(("dp", "tensor"), None),
        P("dp", "tensor"),
        P("dp", None, "tensor"),
        P("dp", None, "tensor", None),
        P("dp"),
    )
    out_specs = (P("dp", None, "tensor"), P(None, "tensor"))
    body = functools.partial(shards, replicas=mesh.shape["dp"], group=mesh.shape["tensor"])
    return jax.shard_map(body, mesh=mesh, in_specs=in_specs, out_specs=out_specs, check_vma=False)
```

```python
import functools

import jax
import jax.numpy as jnp
import ml_dtypes
import numpy as np
from jax import lax
from jax.experimental import pallas as pl
from jax.experimental.pallas import tpu as pltpu
from jax.sharding import PartitionSpec as P

BLK = 32
SPAN = 64
WIDE = 4
ROW_GROUPS = 4
OWN_COLS = 8
NEAR = (0, 1, 3)
FAR = 2


def cosine_parts():
    n = np.arange(SPAN, dtype=np.float64)
    table = np.cos(np.pi * (2.0 * n[None, :] + 1.0) * n[:, None] / 128.0) * np.sqrt(2.0 / SPAN)
    table[0] *= np.sqrt(0.5)
    high = table.astype(ml_dtypes.bfloat16)
    low = (table - high.astype(np.float64)).astype(ml_dtypes.bfloat16)
    return high, low


def split(x):
    high = x.astype(jnp.bfloat16)
    return high, (x - high.astype(jnp.float32)).astype(jnp.bfloat16)


def spans_of(ref, i, count):
    first = i * count * SPAN
    return [ref[first + s * SPAN : first + (s + 1) * SPAN, :] for s in range(count)]


def beside(parts):
    return jnp.concatenate(parts, axis=1)


def product(table, parts):
    return jnp.dot(table[...], jnp.concatenate(parts, axis=0), preferred_element_type=jnp.float32)


def put(ref, i, count, value):
    cols = ref.shape[1]
    for s in range(count):
        first = (i * count + s) * SPAN
        ref[first : first + SPAN, :] = value[:, s * cols : (s + 1) * cols].astype(ref.dtype)


def keys_kernel(chips, tokens, keys, ids, own, partner, far):
    spot = lax.axis_index("tensor")
    chip, core = lax.shift_right_logical(spot, 1), lax.bitwise_and(spot, 1)

    def first(step, which):
        block = 2 * lax.bitwise_and(chip + step, chips - 1) + which
        return pl.multiple_of(block * tokens, 16)

    for place, step in enumerate(NEAR):
        here = slice(place * tokens, (place + 1) * tokens)
        own[here, :] = keys[pl.ds(first(step, core), tokens), :]
        partner[here, :] = keys[pl.ds(first(step, 1 - core), tokens), :]
    far[: 2 * tokens, :] = keys[pl.ds(first(FAR, 0), 2 * tokens), :]
    most, halves, spans = ids.shape
    wide = far.shape[1]
    rows = [ids[k].astype(jnp.float32) for k in range(most)]
    rows.append(jnp.zeros((16 - most * halves, spans), jnp.float32))
    rows = jnp.concatenate(rows, axis=0)
    rows = jnp.concatenate([rows, jnp.zeros((16, wide - spans), jnp.float32)], axis=1)
    far[2 * tokens :, :] = rows.astype(far.dtype)


def copy_kernel(x, y):
    y[...] = x[...]


def pair_kernel(tokens, far, mine, theirs):
    core = lax.bitwise_and(lax.axis_index("tensor"), 1)
    mine[...] = far[pl.ds(pl.multiple_of(core * tokens, 16), tokens), :]
    theirs[...] = far[pl.ds(pl.multiple_of((1 - core) * tokens, 16), tokens), :]


def routes_kernel(ids, count, base, mask, picks, numbers):
    cols = mask.shape[1]
    spans = mask.shape[0] // SPAN
    most = ids.shape[0]
    each = spans // ROW_GROUPS

    def number(a, b, k):
        return jnp.where(k < count[0], ids[k, b, a], -1)

    block = lax.shift_right_logical(lax.broadcasted_iota(jnp.int32, (SPAN, cols), 0), 1)
    first = lax.broadcasted_iota(jnp.int32, (SPAN, cols), 1) < SPAN

    def body(a, _):
        hit = jnp.zeros((SPAN, cols), jnp.bool_)
        for k in range(most):
            hit = hit | (jnp.where(first, number(a, 0, k), number(a, 1, k)) == block)
        rows = pl.ds(pl.multiple_of(a * SPAN, SPAN), SPAN)
        mask[rows, :] = hit.astype(jnp.float32).astype(mask.dtype)
        return 0

    lax.fori_loop(0, spans, body, 0)

    lane = lax.broadcasted_iota(jnp.int32, (SPAN, cols), 1)
    square = (cols, cols)
    column = lax.broadcasted_iota(jnp.int32, square, 1)
    slot = lax.shift_right_logical(lax.broadcasted_iota(jnp.int32, square, 0), 1)
    double = (column == slot).astype(jnp.float32).astype(jnp.bfloat16)
    place = column.astype(jnp.float32)
    for g in range(ROW_GROUPS):
        halves = []
        for b in range(2):
            line = jnp.full((SPAN, cols), -1, jnp.int32)
            for a in range(each):
                for k in range(most):
                    line = jnp.where(lane == a * most + k, number(g * each + a, b, k), line)
            halves.append(line)
        tile = jnp.concatenate(halves, axis=0).astype(jnp.float32)
        numbers[g * cols : (g + 1) * cols, :] = tile.astype(numbers.dtype)
        twice = jnp.dot(
            double, tile.T.astype(jnp.bfloat16), preferred_element_type=jnp.float32
        )
        for b in range(2):
            own = jnp.broadcast_to(twice[:, b * SPAN : b * SPAN + 1], square)
            target = jnp.where(own < 0.0, -1.0, base[...] + 2.0 * own)
            for i in range(picks.shape[1] // cols):
                picks[(2 * g + b) * cols : (2 * g + b + 1) * cols, i * cols : (i + 1) * cols] = (
                    (target == place + float(i * cols)).astype(jnp.float32).astype(picks.dtype)
                )


def chosen_rows(x, mask, forward, i):
    high, low = split(x)
    keep = beside(spans_of(mask, i, WIDE)).astype(jnp.float32)
    return product(forward, [high, low, high]) * keep


def chosen(picks, rows, group, first):
    cols = rows.shape[1]
    height = picks.shape[1]
    band = rows[group * height : (group + 1) * height, :]
    one, two = (
        jnp.dot(
            picks[(2 * group + b) * cols : (2 * group + b + 1) * cols, :],
            band,
            preferred_element_type=jnp.float32,
        )
        for b in range(2)
    )
    return jnp.where(first, one, two)


def left_half(cols):
    return lax.broadcasted_iota(jnp.int32, (cols, cols), 1) < SPAN


def far_kernel(
    numbers, count, spans, slots, base, part, other, forward, whole, sent, picks, rows
):
    cols = part.shape[1]
    height = picks.shape[1]
    square = (cols, cols)
    known = numbers[...].astype(jnp.float32)
    known = jnp.concatenate(
        [known, jnp.zeros((cols - known.shape[0], cols), jnp.float32)], axis=0
    ).T.astype(jnp.bfloat16)
    place = lax.broadcasted_iota(jnp.int32, square, 1).astype(jnp.float32)
    ones = jnp.ones(square, jnp.bfloat16)
    slot = slots[...]
    active = slot < count[0].astype(jnp.float32)
    for g in range(ROW_GROUPS):
        by_span = jnp.dot(
            spans[g * cols : (g + 1) * cols, :], known, preferred_element_type=jnp.float32
        )
        for b in range(2):
            single = jnp.where(place == 2.0 * slot + float(b), by_span, 0.0)
            own = jnp.dot(
                single.astype(jnp.bfloat16), ones, preferred_element_type=jnp.float32
            )
            target = jnp.where(active, base[...] + 2.0 * own, -1.0)
            for i in range(height // cols):
                picks[(2 * g + b) * cols : (2 * g + b + 1) * cols, i * cols : (i + 1) * cols] = (
                    (target == place + float(i * cols)).astype(jnp.float32).astype(picks.dtype)
                )
    for i in range(part.shape[0] // (SPAN * WIDE)):
        x = beside(
            [
                p + o.astype(jnp.float32)
                for p, o in zip(spans_of(part, i, WIDE), spans_of(other, i, WIDE))
            ]
        )
        put(whole, i, WIDE, x)
        high, low = split(x)
        put(rows, i, WIDE, product(forward, [high, low, high]))
    first = left_half(cols)
    for g in range(ROW_GROUPS):
        sent[g * cols : (g + 1) * cols, :] = chosen(picks, rows, g, first).astype(sent.dtype)


def spectrum_kernel(part, other, far, picks, numbers, forward, advanced, sent, rows):
    for i in range(part.shape[0] // (SPAN * WIDE)):
        x = beside(
            [
                p + o.astype(jnp.float32)
                for p, o in zip(spans_of(part, i, WIDE), spans_of(other, i, WIDE))
            ]
        )
        put(advanced, i, WIDE, x)
        high, low = split(x)
        put(rows, i, WIDE, product(forward, [high, low, high]))
    cols = part.shape[1]
    first = left_half(cols)
    for g in range(ROW_GROUPS):
        message = slice(g * cols, (g + 1) * cols)
        total = chosen(picks, rows, g, first) + far[message, :].astype(jnp.float32)
        sent[message, :cols] = total.T.astype(sent.dtype)
        sent[message, cols:] = numbers[message, :]


def kept_kernel(advanced, far, mask, forward, backward, kept):
    for i in range(kept.shape[0] // (SPAN * WIDE)):
        x = beside(
            [
                n + f.astype(jnp.float32)
                for n, f in zip(spans_of(advanced, i, WIDE), spans_of(far, i, WIDE))
            ]
        )
        high, low = split(chosen_rows(x, mask, forward, i))
        put(kept, i, WIDE, x - product(backward, [high, low, high]))


def total_kernel(pieces, backward, totals, placed):
    wide = pieces.shape[1] // 2
    spans = totals.shape[1] // SPAN
    lane = lax.broadcasted_iota(jnp.int32, (BLK, wide), 0).astype(jnp.float32)
    for t in range(pieces.shape[0] // wide):
        values = pieces[t * wide : (t + 1) * wide, :wide].astype(jnp.float32).T
        numbers = pieces[t * wide : (t + 1) * wide, wide:].astype(jnp.float32).T
        most = wide // (2 * spans)
        for a in range(spans):
            upper = jnp.zeros((BLK, wide), jnp.float32)
            lower = upper
            for k in range(most):
                at = a * most + k
                here = numbers[at : at + 1, :] == lane
                upper = jnp.where(here, values[2 * at : 2 * at + 1, :], upper)
                lower = jnp.where(here, values[2 * at + 1 : 2 * at + 2, :], lower)
            both = jnp.concatenate([upper, lower], axis=0)
            placed[a * SPAN : (a + 1) * SPAN, t * wide : (t + 1) * wide] = both.astype(placed.dtype)
    shape = (2 * OWN_COLS, placed.shape[1])
    column = lax.broadcasted_iota(jnp.int32, shape, 1) & (OWN_COLS - 1)
    row = lax.broadcasted_iota(jnp.int32, shape, 0) & (OWN_COLS - 1)
    total = lax.dot_general(
        (column == row).astype(jnp.float32).astype(placed.dtype),
        placed[...],
        (((1,), (1,)), ((), ())),
        preferred_element_type=jnp.float32,
    )
    pair = 2 * SPAN
    for i in range(totals.shape[1] // pair):
        high, low = split(total[:, i * pair : (i + 1) * pair])
        done = jnp.dot(
            jnp.concatenate([high, low, high], axis=1),
            backward[...],
            preferred_element_type=jnp.float32,
        ).astype(totals.dtype)
        for r in range(totals.shape[0] // shape[0]):
            totals[r * shape[0] : (r + 1) * shape[0], i * pair : (i + 1) * pair] = done


def turn_kernel(turned, update):
    cols, height = update.shape[1], turned.shape[1]
    for g in range(ROW_GROUPS):
        for i in range(height // cols):
            rows = g * height + i * cols
            block = turned[g * cols : (g + 1) * cols, i * cols : (i + 1) * cols]
            update[rows : rows + cols, :] = block.astype(jnp.float32).T.astype(update.dtype)


def gram(a, k):
    return lax.dot_general(a, k, (((0,), (0,)), ((), ())), preferred_element_type=jnp.float32)


VMEM, SMEM = (pl.BlockSpec(memory_space=space) for space in (pltpu.VMEM, pltpu.SMEM))


def call(kernel, name, outs, *args, places=None, scratch=()):
    return pl.pallas_call(
        kernel,
        out_shape=outs,
        in_specs=places or [VMEM] * len(args),
        out_specs=(VMEM,) * len(outs),
        scratch_shapes=scratch,
        compiler_params=pltpu.CompilerParams(vmem_limit_bytes=10 << 20),
        cost_estimate=pl.CostEstimate(flops=0, bytes_accessed=0, transcendentals=0),
        name=name,
    )(*args)


def shards(activations, key_grad, momentum, block_ids, counts, *, replicas, group):
    tokens, features = activations.shape
    cols = key_grad.shape[1]
    chips = group // 2

    def along(x, step):
        return lax.ppermute(x, "tensor", [(i, (i + 2 * step) % group) for i in range(group)])

    def swap(x):
        return lax.ppermute(x, "tensor", [(i, i ^ 1) for i in range(group)])

    near_rows = jax.ShapeDtypeStruct((len(NEAR) * tokens, cols), jnp.bfloat16)
    far_rows = jax.ShapeDtypeStruct((2 * tokens + 16, cols), jnp.bfloat16)
    ids = jnp.transpose(block_ids[0], (2, 1, 0))
    own_keys, partner_keys, far_keys = call(
        functools.partial(keys_kernel, chips, tokens),
        "keys",
        (near_rows, near_rows, far_rows),
        key_grad,
        ids,
    )
    far_keys = along(far_keys, FAR)
    (activations,) = call(
        copy_kernel,
        "copy",
        (jax.ShapeDtypeStruct(activations.shape, activations.dtype),),
        activations,
    )
    activations, own_keys, partner_keys = lax.optimization_barrier(
        (activations, own_keys, partner_keys)
    )
    left, right = along(activations, 1), along(activations, -1)

    block_rows = jax.ShapeDtypeStruct((tokens, cols), jnp.bfloat16)
    far_own, far_theirs = call(
        functools.partial(pair_kernel, tokens), "pair", (block_rows, block_rows), far_keys
    )
    far_theirs = swap(far_theirs)
    far_other = swap(gram(activations, far_theirs).astype(jnp.bfloat16))
    far_part = gram(activations, far_own)
    their_keys = swap(partner_keys)

    flat = jax.ShapeDtypeStruct((features, cols), jnp.float32)
    flat_half = jax.ShapeDtypeStruct((features, cols), jnp.bfloat16)
    high, low = cosine_parts()
    forward = jnp.asarray(np.concatenate([high, high, low], axis=1))
    backward = jnp.asarray(np.concatenate([high.T, high.T, low.T], axis=1))
    height = features // ROW_GROUPS
    lines = np.arange(cols)
    base = SPAN * (lines // (2 * block_ids.shape[3])) + lines % 2
    base = jnp.asarray(np.repeat(base[:, None], cols, axis=1).astype(np.float32))
    picks_shape = (2 * ROW_GROUPS * cols, height)
    mask, picks, numbers = call(
        routes_kernel,
        "routes",
        (
            flat_half,
            jax.ShapeDtypeStruct(picks_shape, jnp.bfloat16),
            jax.ShapeDtypeStruct((ROW_GROUPS * cols, cols), jnp.bfloat16),
        ),
        ids,
        counts,
        base,
        places=[SMEM, SMEM, VMEM],
    )

    most = block_ids.shape[3]
    span = lines // (2 * most)
    each = features // SPAN // ROW_GROUPS
    span_table = np.concatenate(
        [(span[:, None] + g * each == lines) & (span[:, None] < each) for g in range(ROW_GROUPS)]
    )
    slot_table = np.where(span < each, lines % (2 * most) // 2, most)
    slot_table = np.repeat(slot_table[:, None], cols, axis=1)
    far_whole, far_sent = call(
        far_kernel,
        "far",
        (flat_half, jax.ShapeDtypeStruct((ROW_GROUPS * cols, cols), jnp.bfloat16)),
        far_keys[2 * tokens :],
        counts,
        jnp.asarray(span_table.astype(np.float32).astype(ml_dtypes.bfloat16)),
        jnp.asarray(slot_table.astype(np.float32)),
        base,
        far_part,
        far_other,
        forward,
        places=[VMEM, SMEM] + [VMEM] * 6,
        scratch=(
            pltpu.VMEM(picks_shape, jnp.bfloat16),
            pltpu.VMEM((features, cols), jnp.bfloat16),
        ),
    )
    far_sent = along(far_sent, FAR)

    keys = jnp.concatenate([own_keys, their_keys], axis=1)
    keys = lax.optimization_barrier(keys.reshape(len(NEAR), tokens, 2 * cols))
    near = gram(activations, keys[0]) + gram(right, keys[1]) + gram(left, keys[2])
    other, far_whole = lax.optimization_barrier(
        (near[:, cols:].astype(jnp.bfloat16), far_whole)
    )
    other, far_whole = swap(other), along(far_whole, FAR)
    part = near[:, :cols] + 0.999 * momentum[0]

    order = np.concatenate([np.arange(0, SPAN, 2), np.arange(1, SPAN, 2)])
    both_high, both_low = (np.kron(np.eye(2, dtype=p.dtype), p[order]) for p in (high, low))
    backward_pair = jnp.asarray(np.concatenate([both_high, both_high, both_low], axis=0))

    message = jax.ShapeDtypeStruct((ROW_GROUPS * cols, 2 * cols), jnp.bfloat16)
    advanced, sent = call(
        spectrum_kernel,
        "spectrum",
        (flat, message),
        part,
        other,
        far_sent,
        picks,
        numbers,
        forward,
        scratch=(pltpu.VMEM((features, cols), jnp.bfloat16),),
    )

    def exchange(x):
        return lax.all_to_all(
            x.reshape(replicas, OWN_COLS, x.shape[1]), "dp", 0, 0, tiled=True
        ).reshape(x.shape)

    pieces = exchange(sent)
    (totals,) = call(
        total_kernel,
        "total",
        (jax.ShapeDtypeStruct((replicas * OWN_COLS, height), jnp.bfloat16),),
        pieces,
        backward_pair,
        scratch=(pltpu.VMEM((height, replicas * OWN_COLS), jnp.bfloat16),),
    )
    totals, far_whole = lax.optimization_barrier((totals, far_whole))
    (kept,) = call(kept_kernel, "kept", (flat,), advanced, far_whole, mask, forward, backward)
    (update,) = call(turn_kernel, "turn", (flat_half,), exchange(totals))
    return kept[None], update


def solution(mesh):
    in_specs = (
        P(("dp", "tensor"), None),
        P("dp", "tensor"),
        P("dp", None, "tensor"),
        P("dp", None, "tensor", None),
        P("dp"),
    )
    out_specs = (P("dp", None, "tensor"), P(None, "tensor"))
    body = functools.partial(shards, replicas=mesh.shape["dp"], group=mesh.shape["tensor"])
    return jax.shard_map(body, mesh=mesh, in_specs=in_specs, out_specs=out_specs, check_vma=False)
```

```python
import functools

import jax
import jax.numpy as jnp
import ml_dtypes
import numpy as np
from jax import lax
from jax.experimental import pallas as pl
from jax.experimental.pallas import tpu as pltpu
from jax.sharding import PartitionSpec as P

BLK = 32
SPAN = 64
WIDE = 4
ROW_GROUPS = 4
OWN_COLS = 8
NEAR = (0, 1, 3)
FAR = 2


def cosine_parts():
    n = np.arange(SPAN, dtype=np.float64)
    table = np.cos(np.pi * (2.0 * n[None, :] + 1.0) * n[:, None] / 128.0) * np.sqrt(2.0 / SPAN)
    table[0] *= np.sqrt(0.5)
    high = table.astype(ml_dtypes.bfloat16)
    low = (table - high.astype(np.float64)).astype(ml_dtypes.bfloat16)
    return high, low


def split(x):
    high = x.astype(jnp.bfloat16)
    return high, (x - high.astype(jnp.float32)).astype(jnp.bfloat16)


def spans_of(ref, i, count):
    first = i * count * SPAN
    return [ref[first + s * SPAN : first + (s + 1) * SPAN, :] for s in range(count)]


def beside(parts):
    return jnp.concatenate(parts, axis=1)


def product(table, parts):
    return jnp.dot(table[...], jnp.concatenate(parts, axis=0), preferred_element_type=jnp.float32)


def put(ref, i, count, value):
    cols = ref.shape[1]
    for s in range(count):
        first = (i * count + s) * SPAN
        ref[first : first + SPAN, :] = value[:, s * cols : (s + 1) * cols].astype(ref.dtype)


def keys_kernel(chips, tokens, keys, ids, own, partner, far):
    spot = lax.axis_index("tensor")
    chip, core = lax.shift_right_logical(spot, 1), lax.bitwise_and(spot, 1)

    def first(step, which):
        block = 2 * lax.bitwise_and(chip + step, chips - 1) + which
        return pl.multiple_of(block * tokens, 16)

    for place, step in enumerate(NEAR):
        here = slice(place * tokens, (place + 1) * tokens)
        own[here, :] = keys[pl.ds(first(step, core), tokens), :]
        partner[here, :] = keys[pl.ds(first(step, 1 - core), tokens), :]
    far[: 2 * tokens, :] = keys[pl.ds(first(FAR, 0), 2 * tokens), :]
    most, halves, spans = ids.shape
    wide = far.shape[1]
    rows = [ids[k].astype(jnp.float32) for k in range(most)]
    rows.append(jnp.zeros((16 - most * halves, spans), jnp.float32))
    rows = jnp.concatenate(rows, axis=0)
    rows = jnp.concatenate([rows, jnp.zeros((16, wide - spans), jnp.float32)], axis=1)
    far[2 * tokens :, :] = rows.astype(far.dtype)


def pair_kernel(tokens, far, mine, theirs):
    core = lax.bitwise_and(lax.axis_index("tensor"), 1)
    mine[...] = far[pl.ds(pl.multiple_of(core * tokens, 16), tokens), :]
    theirs[...] = far[pl.ds(pl.multiple_of((1 - core) * tokens, 16), tokens), :]


def routes_kernel(ids, count, base, mask, picks, numbers):
    cols = mask.shape[1]
    spans = mask.shape[0] // SPAN
    most = ids.shape[0]
    each = spans // ROW_GROUPS

    def number(a, b, k):
        return jnp.where(k < count[0], ids[k, b, a], -1)

    block = lax.shift_right_logical(lax.broadcasted_iota(jnp.int32, (SPAN, cols), 0), 1)
    first = lax.broadcasted_iota(jnp.int32, (SPAN, cols), 1) < SPAN

    def body(a, _):
        hit = jnp.zeros((SPAN, cols), jnp.bool_)
        for k in range(most):
            hit = hit | (jnp.where(first, number(a, 0, k), number(a, 1, k)) == block)
        rows = pl.ds(pl.multiple_of(a * SPAN, SPAN), SPAN)
        mask[rows, :] = hit.astype(jnp.float32).astype(mask.dtype)
        return 0

    lax.fori_loop(0, spans, body, 0)

    lane = lax.broadcasted_iota(jnp.int32, (SPAN, cols), 1)
    square = (cols, cols)
    column = lax.broadcasted_iota(jnp.int32, square, 1)
    slot = lax.shift_right_logical(lax.broadcasted_iota(jnp.int32, square, 0), 1)
    double = (column == slot).astype(jnp.float32).astype(jnp.bfloat16)
    place = column.astype(jnp.float32)
    for g in range(ROW_GROUPS):
        halves = []
        for b in range(2):
            line = jnp.full((SPAN, cols), -1, jnp.int32)
            for a in range(each):
                for k in range(most):
                    line = jnp.where(lane == a * most + k, number(g * each + a, b, k), line)
            halves.append(line)
        tile = jnp.concatenate(halves, axis=0).astype(jnp.float32)
        numbers[g * cols : (g + 1) * cols, :] = tile.astype(numbers.dtype)
        twice = jnp.dot(
            double, tile.T.astype(jnp.bfloat16), preferred_element_type=jnp.float32
        )
        for b in range(2):
            own = jnp.broadcast_to(twice[:, b * SPAN : b * SPAN + 1], square)
            target = jnp.where(own < 0.0, -1.0, base[...] + 2.0 * own)
            for i in range(picks.shape[1] // cols):
                picks[(2 * g + b) * cols : (2 * g + b + 1) * cols, i * cols : (i + 1) * cols] = (
                    (target == place + float(i * cols)).astype(jnp.float32).astype(picks.dtype)
                )


def chosen_rows(x, mask, forward, i):
    high, low = split(x)
    keep = beside(spans_of(mask, i, WIDE)).astype(jnp.float32)
    return product(forward, [high, low, high]) * keep


def chosen(picks, rows, group, first):
    cols = rows.shape[1]
    height = picks.shape[1]
    band = rows[group * height : (group + 1) * height, :]
    one, two = (
        jnp.dot(
            picks[(2 * group + b) * cols : (2 * group + b + 1) * cols, :],
            band,
            preferred_element_type=jnp.float32,
        )
        for b in range(2)
    )
    return jnp.where(first, one, two)


def left_half(cols):
    return lax.broadcasted_iota(jnp.int32, (cols, cols), 1) < SPAN


def far_kernel(
    numbers, count, spans, slots, base, part, other, forward, whole, sent, picks, rows
):
    cols = part.shape[1]
    height = picks.shape[1]
    square = (cols, cols)
    known = numbers[...].astype(jnp.float32)
    known = jnp.concatenate(
        [known, jnp.zeros((cols - known.shape[0], cols), jnp.float32)], axis=0
    ).T.astype(jnp.bfloat16)
    place = lax.broadcasted_iota(jnp.int32, square, 1).astype(jnp.float32)
    ones = jnp.ones(square, jnp.bfloat16)
    slot = slots[...]
    active = slot < count[0].astype(jnp.float32)
    for g in range(ROW_GROUPS):
        by_span = jnp.dot(
            spans[g * cols : (g + 1) * cols, :], known, preferred_element_type=jnp.float32
        )
        for b in range(2):
            single = jnp.where(place == 2.0 * slot + float(b), by_span, 0.0)
            own = jnp.dot(
                single.astype(jnp.bfloat16), ones, preferred_element_type=jnp.float32
            )
            target = jnp.where(active, base[...] + 2.0 * own, -1.0)
            for i in range(height // cols):
                picks[(2 * g + b) * cols : (2 * g + b + 1) * cols, i * cols : (i + 1) * cols] = (
                    (target == place + float(i * cols)).astype(jnp.float32).astype(picks.dtype)
                )
    for i in range(part.shape[0] // (SPAN * WIDE)):
        x = beside(
            [
                p + o.astype(jnp.float32)
                for p, o in zip(spans_of(part, i, WIDE), spans_of(other, i, WIDE))
            ]
        )
        put(whole, i, WIDE, x)
        high, low = split(x)
        put(rows, i, WIDE, product(forward, [high, low, high]))
    first = left_half(cols)
    for g in range(ROW_GROUPS):
        sent[g * cols : (g + 1) * cols, :] = chosen(picks, rows, g, first).astype(sent.dtype)


def spectrum_kernel(part, other, far, picks, numbers, forward, advanced, sent, rows):
    for i in range(part.shape[0] // (SPAN * WIDE)):
        x = beside(
            [
                p + o.astype(jnp.float32)
                for p, o in zip(spans_of(part, i, WIDE), spans_of(other, i, WIDE))
            ]
        )
        put(advanced, i, WIDE, x)
        high, low = split(x)
        put(rows, i, WIDE, product(forward, [high, low, high]))
    cols = part.shape[1]
    first = left_half(cols)
    for g in range(ROW_GROUPS):
        message = slice(g * cols, (g + 1) * cols)
        total = chosen(picks, rows, g, first) + far[message, :].astype(jnp.float32)
        sent[message, :cols] = total.T.astype(sent.dtype)
        sent[message, cols:] = numbers[message, :]


def kept_kernel(advanced, far, mask, forward, backward, kept):
    for i in range(kept.shape[0] // (SPAN * WIDE)):
        x = beside(
            [
                n + f.astype(jnp.float32)
                for n, f in zip(spans_of(advanced, i, WIDE), spans_of(far, i, WIDE))
            ]
        )
        high, low = split(chosen_rows(x, mask, forward, i))
        put(kept, i, WIDE, x - product(backward, [high, low, high]))


def total_kernel(pieces, backward, totals, placed):
    wide = pieces.shape[1] // 2
    spans = totals.shape[1] // SPAN
    lane = lax.broadcasted_iota(jnp.int32, (BLK, wide), 0).astype(jnp.float32)
    for t in range(pieces.shape[0] // wide):
        values = pieces[t * wide : (t + 1) * wide, :wide].astype(jnp.float32).T
        numbers = pieces[t * wide : (t + 1) * wide, wide:].astype(jnp.float32).T
        most = wide // (2 * spans)
        for a in range(spans):
            upper = jnp.zeros((BLK, wide), jnp.float32)
            lower = upper
            for k in range(most):
                at = a * most + k
                here = numbers[at : at + 1, :] == lane
                upper = jnp.where(here, values[2 * at : 2 * at + 1, :], upper)
                lower = jnp.where(here, values[2 * at + 1 : 2 * at + 2, :], lower)
            both = jnp.concatenate([upper, lower], axis=0)
            placed[a * SPAN : (a + 1) * SPAN, t * wide : (t + 1) * wide] = both.astype(placed.dtype)
    shape = (2 * OWN_COLS, placed.shape[1])
    column = lax.broadcasted_iota(jnp.int32, shape, 1) & (OWN_COLS - 1)
    row = lax.broadcasted_iota(jnp.int32, shape, 0) & (OWN_COLS - 1)
    total = lax.dot_general(
        (column == row).astype(jnp.float32).astype(placed.dtype),
        placed[...],
        (((1,), (1,)), ((), ())),
        preferred_element_type=jnp.float32,
    )
    pair = 2 * SPAN
    for i in range(totals.shape[1] // pair):
        high, low = split(total[:, i * pair : (i + 1) * pair])
        done = jnp.dot(
            jnp.concatenate([high, low, high], axis=1),
            backward[...],
            preferred_element_type=jnp.float32,
        ).astype(totals.dtype)
        for r in range(totals.shape[0] // shape[0]):
            totals[r * shape[0] : (r + 1) * shape[0], i * pair : (i + 1) * pair] = done


def turn_kernel(turned, update):
    cols, height = update.shape[1], turned.shape[1]
    for g in range(ROW_GROUPS):
        for i in range(height // cols):
            rows = g * height + i * cols
            block = turned[g * cols : (g + 1) * cols, i * cols : (i + 1) * cols]
            update[rows : rows + cols, :] = block.astype(jnp.float32).T.astype(update.dtype)


def gram(a, k):
    return lax.dot_general(a, k, (((0,), (0,)), ((), ())), preferred_element_type=jnp.float32)


VMEM, SMEM = (pl.BlockSpec(memory_space=space) for space in (pltpu.VMEM, pltpu.SMEM))


def call(kernel, name, outs, *args, places=None, scratch=()):
    return pl.pallas_call(
        kernel,
        out_shape=outs,
        in_specs=places or [VMEM] * len(args),
        out_specs=(VMEM,) * len(outs),
        scratch_shapes=scratch,
        compiler_params=pltpu.CompilerParams(vmem_limit_bytes=10 << 20),
        cost_estimate=pl.CostEstimate(flops=0, bytes_accessed=0, transcendentals=0),
        name=name,
    )(*args)


def shards(activations, key_grad, momentum, block_ids, counts, *, replicas, group):
    tokens, features = activations.shape
    cols = key_grad.shape[1]
    chips = group // 2

    def along(x, step):
        return lax.ppermute(x, "tensor", [(i, (i + 2 * step) % group) for i in range(group)])

    def swap(x):
        return lax.ppermute(x, "tensor", [(i, i ^ 1) for i in range(group)])

    near_rows = jax.ShapeDtypeStruct((len(NEAR) * tokens, cols), jnp.bfloat16)
    far_rows = jax.ShapeDtypeStruct((2 * tokens + 16, cols), jnp.bfloat16)
    ids = jnp.transpose(block_ids[0], (2, 1, 0))
    own_keys, partner_keys, far_keys = call(
        functools.partial(keys_kernel, chips, tokens),
        "keys",
        (near_rows, near_rows, far_rows),
        key_grad,
        ids,
    )
    far_keys = along(far_keys, FAR)
    activations, own_keys, partner_keys = lax.optimization_barrier(
        (activations, own_keys, partner_keys)
    )
    left, right = along(activations, 1), along(activations, -1)

    block_rows = jax.ShapeDtypeStruct((tokens, cols), jnp.bfloat16)
    far_own, far_theirs = call(
        functools.partial(pair_kernel, tokens), "pair", (block_rows, block_rows), far_keys
    )
    far_theirs = swap(far_theirs)
    far_other = swap(gram(activations, far_theirs).astype(jnp.bfloat16))
    far_part = gram(activations, far_own)
    their_keys = swap(partner_keys)

    flat = jax.ShapeDtypeStruct((features, cols), jnp.float32)
    flat_half = jax.ShapeDtypeStruct((features, cols), jnp.bfloat16)
    high, low = cosine_parts()
    forward = jnp.asarray(np.concatenate([high, high, low], axis=1))
    backward = jnp.asarray(np.concatenate([high.T, high.T, low.T], axis=1))
    height = features // ROW_GROUPS
    lines = np.arange(cols)
    base = SPAN * (lines // (2 * block_ids.shape[3])) + lines % 2
    base = jnp.asarray(np.repeat(base[:, None], cols, axis=1).astype(np.float32))
    picks_shape = (2 * ROW_GROUPS * cols, height)
    mask, picks, numbers = call(
        routes_kernel,
        "routes",
        (
            flat_half,
            jax.ShapeDtypeStruct(picks_shape, jnp.bfloat16),
            jax.ShapeDtypeStruct((ROW_GROUPS * cols, cols), jnp.bfloat16),
        ),
        ids,
        counts,
        base,
        places=[SMEM, SMEM, VMEM],
    )

    most = block_ids.shape[3]
    span = lines // (2 * most)
    each = features // SPAN // ROW_GROUPS
    span_table = np.concatenate(
        [(span[:, None] + g * each == lines) & (span[:, None] < each) for g in range(ROW_GROUPS)]
    )
    slot_table = np.where(span < each, lines % (2 * most) // 2, most)
    slot_table = np.repeat(slot_table[:, None], cols, axis=1)
    far_whole, far_sent = call(
        far_kernel,
        "far",
        (flat_half, jax.ShapeDtypeStruct((ROW_GROUPS * cols, cols), jnp.bfloat16)),
        far_keys[2 * tokens :],
        counts,
        jnp.asarray(span_table.astype(np.float32).astype(ml_dtypes.bfloat16)),
        jnp.asarray(slot_table.astype(np.float32)),
        base,
        far_part,
        far_other,
        forward,
        places=[VMEM, SMEM] + [VMEM] * 6,
        scratch=(
            pltpu.VMEM(picks_shape, jnp.bfloat16),
            pltpu.VMEM((features, cols), jnp.bfloat16),
        ),
    )
    far_sent = along(far_sent, FAR)

    keys = jnp.concatenate([own_keys, their_keys], axis=1)
    keys = lax.optimization_barrier(keys.reshape(len(NEAR), tokens, 2 * cols))
    left, right = lax.optimization_barrier((left, right))
    near = gram(activations, keys[0]) + gram(right, keys[1]) + gram(left, keys[2])
    other, far_whole = lax.optimization_barrier(
        (near[:, cols:].astype(jnp.bfloat16), far_whole)
    )
    other, far_whole = swap(other), along(far_whole, FAR)
    part = near[:, :cols] + 0.999 * momentum[0]

    order = np.concatenate([np.arange(0, SPAN, 2), np.arange(1, SPAN, 2)])
    both_high, both_low = (np.kron(np.eye(2, dtype=p.dtype), p[order]) for p in (high, low))
    backward_pair = jnp.asarray(np.concatenate([both_high, both_high, both_low], axis=0))

    message = jax.ShapeDtypeStruct((ROW_GROUPS * cols, 2 * cols), jnp.bfloat16)
    advanced, sent = call(
        spectrum_kernel,
        "spectrum",
        (flat, message),
        part,
        other,
        far_sent,
        picks,
        numbers,
        forward,
        scratch=(pltpu.VMEM((features, cols), jnp.bfloat16),),
    )

    def exchange(x):
        return lax.all_to_all(
            x.reshape(replicas, OWN_COLS, x.shape[1]), "dp", 0, 0, tiled=True
        ).reshape(x.shape)

    pieces = exchange(sent)
    (totals,) = call(
        total_kernel,
        "total",
        (jax.ShapeDtypeStruct((replicas * OWN_COLS, height), jnp.bfloat16),),
        pieces,
        backward_pair,
        scratch=(pltpu.VMEM((height, replicas * OWN_COLS), jnp.bfloat16),),
    )
    totals, far_whole = lax.optimization_barrier((totals, far_whole))
    (kept,) = call(kept_kernel, "kept", (flat,), advanced, far_whole, mask, forward, backward)
    (update,) = call(turn_kernel, "turn", (flat_half,), exchange(totals))
    return kept[None], update


def solution(mesh):
    in_specs = (
        P(("dp", "tensor"), None),
        P("dp", "tensor"),
        P("dp", None, "tensor"),
        P("dp", None, "tensor", None),
        P("dp"),
    )
    out_specs = (P("dp", None, "tensor"), P(None, "tensor"))
    body = functools.partial(shards, replicas=mesh.shape["dp"], group=mesh.shape["tensor"])
    return jax.shard_map(body, mesh=mesh, in_specs=in_specs, out_specs=out_specs, check_vma=False)
```

```python
import functools

import jax
import jax.numpy as jnp
import ml_dtypes
import numpy as np
from jax import lax
from jax.experimental import pallas as pl
from jax.experimental.pallas import tpu as pltpu
from jax.sharding import PartitionSpec as P

BLK = 32
SPAN = 64
WIDE = 4
ROW_GROUPS = 4
OWN_COLS = 8
NEAR = (0, 1, 3)
FAR = 2


def cosine_parts():
    n = np.arange(SPAN, dtype=np.float64)
    table = np.cos(np.pi * (2.0 * n[None, :] + 1.0) * n[:, None] / 128.0) * np.sqrt(2.0 / SPAN)
    table[0] *= np.sqrt(0.5)
    high = table.astype(ml_dtypes.bfloat16)
    low = (table - high.astype(np.float64)).astype(ml_dtypes.bfloat16)
    return high, low


def split(x):
    high = x.astype(jnp.bfloat16)
    return high, (x - high.astype(jnp.float32)).astype(jnp.bfloat16)


def spans_of(ref, i, count):
    first = i * count * SPAN
    return [ref[first + s * SPAN : first + (s + 1) * SPAN, :] for s in range(count)]


def beside(parts):
    return jnp.concatenate(parts, axis=1)


def product(table, parts):
    return jnp.dot(table[...], jnp.concatenate(parts, axis=0), preferred_element_type=jnp.float32)


def put(ref, i, count, value):
    cols = ref.shape[1]
    for s in range(count):
        first = (i * count + s) * SPAN
        ref[first : first + SPAN, :] = value[:, s * cols : (s + 1) * cols].astype(ref.dtype)


def far_keys_kernel(chips, tokens, keys, ids, far, numbers, done):
    chip = lax.shift_right_logical(lax.axis_index("tensor"), 1)
    first = 2 * lax.bitwise_and(chip + FAR, chips - 1) * tokens
    rows = pltpu.make_async_copy(
        keys.at[pl.ds(pl.multiple_of(first, 16), 2 * tokens)],
        far.at[pl.ds(0, 2 * tokens)],
        done.at[0],
    )
    listed = pltpu.make_async_copy(ids, numbers, done.at[1])
    rows.start()
    listed.start()
    listed.wait()
    most, halves, spans = ids.shape
    lines = [numbers[k].astype(jnp.float32) for k in range(most)]
    lines.append(jnp.zeros((16 - most * halves, spans), jnp.float32))
    lines = jnp.concatenate(lines, axis=0)
    lines = jnp.concatenate([lines, jnp.zeros((16, far.shape[1] - spans), jnp.float32)], axis=1)
    far[2 * tokens :, :] = lines.astype(far.dtype)
    rows.wait()


def keys_kernel(chips, tokens, keys, own, partner):
    spot = lax.axis_index("tensor")
    chip, core = lax.shift_right_logical(spot, 1), lax.bitwise_and(spot, 1)

    def block(step, which):
        first = (2 * lax.bitwise_and(chip + step, chips - 1) + which) * tokens
        return keys[pl.ds(pl.multiple_of(first, 16), tokens), :]

    for place, step in enumerate(NEAR):
        here = slice(place * tokens, (place + 1) * tokens)
        own[here, :] = block(step, core)
        partner[here, :] = block(step, 1 - core)


def pair_kernel(tokens, far, mine, theirs):
    core = lax.bitwise_and(lax.axis_index("tensor"), 1)
    mine[...] = far[pl.ds(pl.multiple_of(core * tokens, 16), tokens), :]
    theirs[...] = far[pl.ds(pl.multiple_of((1 - core) * tokens, 16), tokens), :]


def routes_kernel(ids, count, base, mask, picks, numbers):
    cols = mask.shape[1]
    spans = mask.shape[0] // SPAN
    most = ids.shape[0]
    each = spans // ROW_GROUPS

    def number(a, b, k):
        return jnp.where(k < count[0], ids[k, b, a], -1)

    block = lax.shift_right_logical(lax.broadcasted_iota(jnp.int32, (SPAN, cols), 0), 1)
    first = lax.broadcasted_iota(jnp.int32, (SPAN, cols), 1) < SPAN

    def body(a, _):
        hit = jnp.zeros((SPAN, cols), jnp.bool_)
        for k in range(most):
            hit = hit | (jnp.where(first, number(a, 0, k), number(a, 1, k)) == block)
        rows = pl.ds(pl.multiple_of(a * SPAN, SPAN), SPAN)
        mask[rows, :] = hit.astype(jnp.float32).astype(mask.dtype)
        return 0

    lax.fori_loop(0, spans, body, 0)

    lane = lax.broadcasted_iota(jnp.int32, (SPAN, cols), 1)
    square = (cols, cols)
    column = lax.broadcasted_iota(jnp.int32, square, 1)
    slot = lax.shift_right_logical(lax.broadcasted_iota(jnp.int32, square, 0), 1)
    double = (column == slot).astype(jnp.float32).astype(jnp.bfloat16)
    place = column.astype(jnp.float32)
    for g in range(ROW_GROUPS):
        halves = []
        for b in range(2):
            line = jnp.full((SPAN, cols), -1, jnp.int32)
            for a in range(each):
                for k in range(most):
                    line = jnp.where(lane == a * most + k, number(g * each + a, b, k), line)
            halves.append(line)
        tile = jnp.concatenate(halves, axis=0).astype(jnp.float32)
        numbers[g * cols : (g + 1) * cols, :] = tile.astype(numbers.dtype)
        twice = jnp.dot(
            double, tile.T.astype(jnp.bfloat16), preferred_element_type=jnp.float32
        )
        for b in range(2):
            own = jnp.broadcast_to(twice[:, b * SPAN : b * SPAN + 1], square)
            target = jnp.where(own < 0.0, -1.0, base[...] + 2.0 * own)
            for i in range(picks.shape[1] // cols):
                picks[(2 * g + b) * cols : (2 * g + b + 1) * cols, i * cols : (i + 1) * cols] = (
                    (target == place + float(i * cols)).astype(jnp.float32).astype(picks.dtype)
                )


def chosen_rows(x, mask, forward, i):
    high, low = split(x)
    keep = beside(spans_of(mask, i, WIDE)).astype(jnp.float32)
    return product(forward, [high, low, high]) * keep


def chosen(picks, rows, group, first):
    cols = rows.shape[1]
    height = picks.shape[1]
    band = rows[group * height : (group + 1) * height, :]
    one, two = (
        jnp.dot(
            picks[(2 * group + b) * cols : (2 * group + b + 1) * cols, :],
            band,
            preferred_element_type=jnp.float32,
        )
        for b in range(2)
    )
    return jnp.where(first, one, two)


def left_half(cols):
    return lax.broadcasted_iota(jnp.int32, (cols, cols), 1) < SPAN


def far_kernel(
    numbers, count, spans, slots, base, part, other, forward, whole, sent, picks, rows
):
    cols = part.shape[1]
    height = picks.shape[1]
    square = (cols, cols)
    known = numbers[...].astype(jnp.float32)
    known = jnp.concatenate(
        [known, jnp.zeros((cols - known.shape[0], cols), jnp.float32)], axis=0
    ).T.astype(jnp.bfloat16)
    place = lax.broadcasted_iota(jnp.int32, square, 1).astype(jnp.float32)
    ones = jnp.ones(square, jnp.bfloat16)
    slot = slots[...]
    active = slot < count[0].astype(jnp.float32)
    for g in range(ROW_GROUPS):
        by_span = jnp.dot(
            spans[g * cols : (g + 1) * cols, :], known, preferred_element_type=jnp.float32
        )
        for b in range(2):
            single = jnp.where(place == 2.0 * slot + float(b), by_span, 0.0)
            own = jnp.dot(
                single.astype(jnp.bfloat16), ones, preferred_element_type=jnp.float32
            )
            target = jnp.where(active, base[...] + 2.0 * own, -1.0)
            for i in range(height // cols):
                picks[(2 * g + b) * cols : (2 * g + b + 1) * cols, i * cols : (i + 1) * cols] = (
                    (target == place + float(i * cols)).astype(jnp.float32).astype(picks.dtype)
                )
    for i in range(part.shape[0] // (SPAN * WIDE)):
        x = beside(
            [
                p + o.astype(jnp.float32)
                for p, o in zip(spans_of(part, i, WIDE), spans_of(other, i, WIDE))
            ]
        )
        put(whole, i, WIDE, x)
        high, low = split(x)
        put(rows, i, WIDE, product(forward, [high, low, high]))
    first = left_half(cols)
    for g in range(ROW_GROUPS):
        sent[g * cols : (g + 1) * cols, :] = chosen(picks, rows, g, first).astype(sent.dtype)


def spectrum_kernel(part, other, far, picks, numbers, forward, advanced, sent, rows):
    for i in range(part.shape[0] // (SPAN * WIDE)):
        x = beside(
            [
                p + o.astype(jnp.float32)
                for p, o in zip(spans_of(part, i, WIDE), spans_of(other, i, WIDE))
            ]
        )
        put(advanced, i, WIDE, x)
        high, low = split(x)
        put(rows, i, WIDE, product(forward, [high, low, high]))
    cols = part.shape[1]
    first = left_half(cols)
    for g in range(ROW_GROUPS):
        message = slice(g * cols, (g + 1) * cols)
        total = chosen(picks, rows, g, first) + far[message, :].astype(jnp.float32)
        sent[message, :cols] = total.T.astype(sent.dtype)
        sent[message, cols:] = numbers[message, :]


def kept_kernel(advanced, far, mask, forward, backward, kept):
    for i in range(kept.shape[0] // (SPAN * WIDE)):
        x = beside(
            [
                n + f.astype(jnp.float32)
                for n, f in zip(spans_of(advanced, i, WIDE), spans_of(far, i, WIDE))
            ]
        )
        high, low = split(chosen_rows(x, mask, forward, i))
        put(kept, i, WIDE, x - product(backward, [high, low, high]))


def total_kernel(pieces, backward, totals, placed):
    wide = pieces.shape[1] // 2
    spans = totals.shape[1] // SPAN
    lane = lax.broadcasted_iota(jnp.int32, (BLK, wide), 0).astype(jnp.float32)
    for t in range(pieces.shape[0] // wide):
        values = pieces[t * wide : (t + 1) * wide, :wide].astype(jnp.float32).T
        numbers = pieces[t * wide : (t + 1) * wide, wide:].astype(jnp.float32).T
        most = wide // (2 * spans)
        for a in range(spans):
            upper = jnp.zeros((BLK, wide), jnp.float32)
            lower = upper
            for k in range(most):
                at = a * most + k
                here = numbers[at : at + 1, :] == lane
                upper = jnp.where(here, values[2 * at : 2 * at + 1, :], upper)
                lower = jnp.where(here, values[2 * at + 1 : 2 * at + 2, :], lower)
            both = jnp.concatenate([upper, lower], axis=0)
            placed[a * SPAN : (a + 1) * SPAN, t * wide : (t + 1) * wide] = both.astype(placed.dtype)
    shape = (2 * OWN_COLS, placed.shape[1])
    column = lax.broadcasted_iota(jnp.int32, shape, 1) & (OWN_COLS - 1)
    row = lax.broadcasted_iota(jnp.int32, shape, 0) & (OWN_COLS - 1)
    total = lax.dot_general(
        (column == row).astype(jnp.float32).astype(placed.dtype),
        placed[...],
        (((1,), (1,)), ((), ())),
        preferred_element_type=jnp.float32,
    )
    pair = 2 * SPAN
    for i in range(totals.shape[1] // pair):
        high, low = split(total[:, i * pair : (i + 1) * pair])
        done = jnp.dot(
            jnp.concatenate([high, low, high], axis=1),
            backward[...],
            preferred_element_type=jnp.float32,
        ).astype(totals.dtype)
        for r in range(totals.shape[0] // shape[0]):
            totals[r * shape[0] : (r + 1) * shape[0], i * pair : (i + 1) * pair] = done


def turn_kernel(turned, update):
    cols, height = update.shape[1], turned.shape[1]
    for g in range(ROW_GROUPS):
        for i in range(height // cols):
            rows = g * height + i * cols
            block = turned[g * cols : (g + 1) * cols, i * cols : (i + 1) * cols]
            update[rows : rows + cols, :] = block.astype(jnp.float32).T.astype(update.dtype)


def gram(a, k):
    return lax.dot_general(a, k, (((0,), (0,)), ((), ())), preferred_element_type=jnp.float32)


VMEM, SMEM, HBM = (
    pl.BlockSpec(memory_space=space) for space in (pltpu.VMEM, pltpu.SMEM, pltpu.HBM)
)


def call(kernel, name, outs, *args, places=None, scratch=()):
    return pl.pallas_call(
        kernel,
        out_shape=outs,
        in_specs=places or [VMEM] * len(args),
        out_specs=(VMEM,) * len(outs),
        scratch_shapes=scratch,
        compiler_params=pltpu.CompilerParams(vmem_limit_bytes=10 << 20),
        cost_estimate=pl.CostEstimate(flops=0, bytes_accessed=0, transcendentals=0),
        name=name,
    )(*args)


def shards(activations, key_grad, momentum, block_ids, counts, *, replicas, group):
    tokens, features = activations.shape
    cols = key_grad.shape[1]
    chips = group // 2

    def along(x, step):
        return lax.ppermute(x, "tensor", [(i, (i + 2 * step) % group) for i in range(group)])

    def swap(x):
        return lax.ppermute(x, "tensor", [(i, i ^ 1) for i in range(group)])

    near_rows = jax.ShapeDtypeStruct((len(NEAR) * tokens, cols), jnp.bfloat16)
    far_rows = jax.ShapeDtypeStruct((2 * tokens + 16, cols), jnp.bfloat16)
    ids = jnp.transpose(block_ids[0], (2, 1, 0))
    (far_keys,) = call(
        functools.partial(far_keys_kernel, chips, tokens),
        "far_keys",
        (far_rows,),
        pltpu.with_memory_space_constraint(key_grad, pltpu.HBM),
        pltpu.with_memory_space_constraint(ids, pltpu.HBM),
        places=[HBM, HBM],
        scratch=(pltpu.VMEM(ids.shape, jnp.int32), pltpu.SemaphoreType.DMA((2,))),
    )
    activations, key_grad, far_keys = lax.optimization_barrier(
        (activations, key_grad, far_keys)
    )
    far_keys = along(far_keys, FAR)
    left, right = along(activations, 1), along(activations, -1)

    block_rows = jax.ShapeDtypeStruct((tokens, cols), jnp.bfloat16)
    far_own, far_theirs = call(
        functools.partial(pair_kernel, tokens), "pair", (block_rows, block_rows), far_keys
    )
    far_theirs = swap(far_theirs)
    far_other = swap(gram(activations, far_theirs).astype(jnp.bfloat16))
    far_part = gram(activations, far_own)
    own_keys, partner_keys = call(
        functools.partial(keys_kernel, chips, tokens), "keys", (near_rows, near_rows), key_grad
    )
    their_keys = swap(partner_keys)

    flat = jax.ShapeDtypeStruct((features, cols), jnp.float32)
    flat_half = jax.ShapeDtypeStruct((features, cols), jnp.bfloat16)
    high, low = cosine_parts()
    forward = jnp.asarray(np.concatenate([high, high, low], axis=1))
    backward = jnp.asarray(np.concatenate([high.T, high.T, low.T], axis=1))
    height = features // ROW_GROUPS
    lines = np.arange(cols)
    base = SPAN * (lines // (2 * block_ids.shape[3])) + lines % 2
    base = jnp.asarray(np.repeat(base[:, None], cols, axis=1).astype(np.float32))
    picks_shape = (2 * ROW_GROUPS * cols, height)
    mask, picks, numbers = call(
        routes_kernel,
        "routes",
        (
            flat_half,
            jax.ShapeDtypeStruct(picks_shape, jnp.bfloat16),
            jax.ShapeDtypeStruct((ROW_GROUPS * cols, cols), jnp.bfloat16),
        ),
        ids,
        counts,
        base,
        places=[SMEM, SMEM, VMEM],
    )

    most = block_ids.shape[3]
    span = lines // (2 * most)
    each = features // SPAN // ROW_GROUPS
    span_table = np.concatenate(
        [(span[:, None] + g * each == lines) & (span[:, None] < each) for g in range(ROW_GROUPS)]
    )
    slot_table = np.where(span < each, lines % (2 * most) // 2, most)
    slot_table = np.repeat(slot_table[:, None], cols, axis=1)
    far_whole, far_sent = call(
        far_kernel,
        "far",
        (flat_half, jax.ShapeDtypeStruct((ROW_GROUPS * cols, cols), jnp.bfloat16)),
        far_keys[2 * tokens :],
        counts,
        jnp.asarray(span_table.astype(np.float32).astype(ml_dtypes.bfloat16)),
        jnp.asarray(slot_table.astype(np.float32)),
        base,
        far_part,
        far_other,
        forward,
        places=[VMEM, SMEM] + [VMEM] * 6,
        scratch=(
            pltpu.VMEM(picks_shape, jnp.bfloat16),
            pltpu.VMEM((features, cols), jnp.bfloat16),
        ),
    )
    far_sent = along(far_sent, FAR)

    keys = jnp.concatenate([own_keys, their_keys], axis=1)
    keys = lax.optimization_barrier(keys.reshape(len(NEAR), tokens, 2 * cols))
    left, right = lax.optimization_barrier((left, right))
    near = gram(activations, keys[0]) + gram(right, keys[1]) + gram(left, keys[2])
    other, far_whole = lax.optimization_barrier(
        (near[:, cols:].astype(jnp.bfloat16), far_whole)
    )
    other, far_whole = swap(other), along(far_whole, FAR)
    part = near[:, :cols] + 0.999 * momentum[0]

    order = np.concatenate([np.arange(0, SPAN, 2), np.arange(1, SPAN, 2)])
    both_high, both_low = (np.kron(np.eye(2, dtype=p.dtype), p[order]) for p in (high, low))
    backward_pair = jnp.asarray(np.concatenate([both_high, both_high, both_low], axis=0))

    message = jax.ShapeDtypeStruct((ROW_GROUPS * cols, 2 * cols), jnp.bfloat16)
    advanced, sent = call(
        spectrum_kernel,
        "spectrum",
        (flat, message),
        part,
        other,
        far_sent,
        picks,
        numbers,
        forward,
        scratch=(pltpu.VMEM((features, cols), jnp.bfloat16),),
    )

    def exchange(x):
        return lax.all_to_all(
            x.reshape(replicas, OWN_COLS, x.shape[1]), "dp", 0, 0, tiled=True
        ).reshape(x.shape)

    pieces = exchange(sent)
    (totals,) = call(
        total_kernel,
        "total",
        (jax.ShapeDtypeStruct((replicas * OWN_COLS, height), jnp.bfloat16),),
        pieces,
        backward_pair,
        scratch=(pltpu.VMEM((height, replicas * OWN_COLS), jnp.bfloat16),),
    )
    totals, far_whole = lax.optimization_barrier((totals, far_whole))
    (kept,) = call(kept_kernel, "kept", (flat,), advanced, far_whole, mask, forward, backward)
    (update,) = call(turn_kernel, "turn", (flat_half,), exchange(totals))
    return kept[None], update


def solution(mesh):
    in_specs = (
        P(("dp", "tensor"), None),
        P("dp", "tensor"),
        P("dp", None, "tensor"),
        P("dp", None, "tensor", None),
        P("dp"),
    )
    out_specs = (P("dp", None, "tensor"), P(None, "tensor"))
    body = functools.partial(shards, replicas=mesh.shape["dp"], group=mesh.shape["tensor"])
    return jax.shard_map(body, mesh=mesh, in_specs=in_specs, out_specs=out_specs, check_vma=False)
```

```python
import functools

import jax
import jax.numpy as jnp
import ml_dtypes
import numpy as np
from jax import lax
from jax.experimental import pallas as pl
from jax.experimental.pallas import tpu as pltpu
from jax.sharding import PartitionSpec as P

BLK = 32
SPAN = 64
WIDE = 4
ROW_GROUPS = 4
OWN_COLS = 8
NEAR = (0, 1, 3)
FAR = 2


def cosine_parts():
    n = np.arange(SPAN, dtype=np.float64)
    table = np.cos(np.pi * (2.0 * n[None, :] + 1.0) * n[:, None] / 128.0) * np.sqrt(2.0 / SPAN)
    table[0] *= np.sqrt(0.5)
    high = table.astype(ml_dtypes.bfloat16)
    low = (table - high.astype(np.float64)).astype(ml_dtypes.bfloat16)
    return high, low


def split(x):
    high = x.astype(jnp.bfloat16)
    return high, (x - high.astype(jnp.float32)).astype(jnp.bfloat16)


def spans_of(ref, i, count):
    first = i * count * SPAN
    return [ref[first + s * SPAN : first + (s + 1) * SPAN, :] for s in range(count)]


def beside(parts):
    return jnp.concatenate(parts, axis=1)


def product(table, parts):
    return jnp.dot(table[...], jnp.concatenate(parts, axis=0), preferred_element_type=jnp.float32)


def put(ref, i, count, value):
    cols = ref.shape[1]
    for s in range(count):
        first = (i * count + s) * SPAN
        ref[first : first + SPAN, :] = value[:, s * cols : (s + 1) * cols].astype(ref.dtype)


def far_keys_kernel(chips, tokens, keys, ids, far, numbers, done):
    chip = lax.shift_right_logical(lax.axis_index("tensor"), 1)
    first = 2 * lax.bitwise_and(chip + FAR, chips - 1) * tokens
    rows = pltpu.make_async_copy(
        keys.at[pl.ds(pl.multiple_of(first, 16), 2 * tokens)],
        far.at[pl.ds(0, 2 * tokens)],
        done.at[0],
    )
    listed = pltpu.make_async_copy(ids, numbers, done.at[1])
    rows.start()
    listed.start()
    listed.wait()
    most, halves, spans = ids.shape
    lines = [numbers[k].astype(jnp.float32) for k in range(most)]
    lines.append(jnp.zeros((16 - most * halves, spans), jnp.float32))
    lines = jnp.concatenate(lines, axis=0)
    lines = jnp.concatenate([lines, jnp.zeros((16, far.shape[1] - spans), jnp.float32)], axis=1)
    far[2 * tokens :, :] = lines.astype(far.dtype)
    rows.wait()


def keys_kernel(chips, tokens, keys, own, partner):
    spot = lax.axis_index("tensor")
    chip, core = lax.shift_right_logical(spot, 1), lax.bitwise_and(spot, 1)

    def block(step, which):
        first = (2 * lax.bitwise_and(chip + step, chips - 1) + which) * tokens
        return keys[pl.ds(pl.multiple_of(first, 16), tokens), :]

    for place, step in enumerate(NEAR):
        here = slice(place * tokens, (place + 1) * tokens)
        own[here, :] = block(step, core)
        partner[here, :] = block(step, 1 - core)


def pair_kernel(tokens, far, mine, theirs):
    core = lax.bitwise_and(lax.axis_index("tensor"), 1)
    mine[...] = far[pl.ds(pl.multiple_of(core * tokens, 16), tokens), :]
    theirs[...] = far[pl.ds(pl.multiple_of((1 - core) * tokens, 16), tokens), :]


def routes_kernel(ids, count, base, mask, picks, numbers):
    cols = mask.shape[1]
    spans = mask.shape[0] // SPAN
    most = ids.shape[0]
    each = spans // ROW_GROUPS

    def number(a, b, k):
        return jnp.where(k < count[0], ids[k, b, a], -1)

    block = lax.shift_right_logical(lax.broadcasted_iota(jnp.int32, (SPAN, cols), 0), 1)
    first = lax.broadcasted_iota(jnp.int32, (SPAN, cols), 1) < SPAN

    def body(a, _):
        hit = jnp.zeros((SPAN, cols), jnp.bool_)
        for k in range(most):
            hit = hit | (jnp.where(first, number(a, 0, k), number(a, 1, k)) == block)
        rows = pl.ds(pl.multiple_of(a * SPAN, SPAN), SPAN)
        mask[rows, :] = hit.astype(jnp.float32).astype(mask.dtype)
        return 0

    lax.fori_loop(0, spans, body, 0)

    lane = lax.broadcasted_iota(jnp.int32, (SPAN, cols), 1)
    square = (cols, cols)
    column = lax.broadcasted_iota(jnp.int32, square, 1)
    slot = lax.shift_right_logical(lax.broadcasted_iota(jnp.int32, square, 0), 1)
    double = (column == slot).astype(jnp.float32).astype(jnp.bfloat16)
    place = column.astype(jnp.float32)
    row = lax.broadcasted_iota(jnp.int32, square, 0)
    spread = lax.shift_right_logical(column, 3) == (row & (OWN_COLS - 1))
    gather = (column == (row & (OWN_COLS - 1)) + cols - OWN_COLS).astype(jnp.float32)
    gather = gather.astype(jnp.bfloat16)
    for g in range(ROW_GROUPS):
        halves = []
        for b in range(2):
            line = jnp.full((SPAN, cols), -1, jnp.int32)
            for a in range(each):
                for k in range(most):
                    line = jnp.where(lane == a * most + k, number(g * each + a, b, k), line)
            halves.append(line)
        tile = jnp.concatenate(halves, axis=0).astype(jnp.float32)
        packed = jnp.dot(
            jnp.where(spread, tile, 0.0).astype(jnp.bfloat16),
            gather,
            preferred_element_type=jnp.float32,
        )
        numbers[g * cols : (g + 1) * cols, :] = packed.astype(numbers.dtype)
        twice = jnp.dot(
            double, tile.T.astype(jnp.bfloat16), preferred_element_type=jnp.float32
        )
        for b in range(2):
            own = jnp.broadcast_to(twice[:, b * SPAN : b * SPAN + 1], square)
            target = jnp.where(own < 0.0, -1.0, base[...] + 2.0 * own)
            for i in range(picks.shape[1] // cols):
                picks[(2 * g + b) * cols : (2 * g + b + 1) * cols, i * cols : (i + 1) * cols] = (
                    (target == place + float(i * cols)).astype(jnp.float32).astype(picks.dtype)
                )


def chosen_rows(x, mask, forward, i):
    high, low = split(x)
    keep = beside(spans_of(mask, i, WIDE)).astype(jnp.float32)
    return product(forward, [high, low, high]) * keep


def chosen(picks, rows, group, first):
    cols = rows.shape[1]
    height = picks.shape[1]
    band = rows[group * height : (group + 1) * height, :]
    one, two = (
        jnp.dot(
            picks[(2 * group + b) * cols : (2 * group + b + 1) * cols, :],
            band,
            preferred_element_type=jnp.float32,
        )
        for b in range(2)
    )
    return jnp.where(first, one, two)


def left_half(cols):
    return lax.broadcasted_iota(jnp.int32, (cols, cols), 1) < SPAN


def far_kernel(
    numbers, count, spans, slots, base, part, other, forward, whole, sent, picks, rows
):
    cols = part.shape[1]
    height = picks.shape[1]
    square = (cols, cols)
    known = numbers[...].astype(jnp.float32)
    known = jnp.concatenate(
        [known, jnp.zeros((cols - known.shape[0], cols), jnp.float32)], axis=0
    ).T.astype(jnp.bfloat16)
    place = lax.broadcasted_iota(jnp.int32, square, 1).astype(jnp.float32)
    ones = jnp.ones(square, jnp.bfloat16)
    slot = slots[...]
    active = slot < count[0].astype(jnp.float32)
    for g in range(ROW_GROUPS):
        by_span = jnp.dot(
            spans[g * cols : (g + 1) * cols, :], known, preferred_element_type=jnp.float32
        )
        for b in range(2):
            single = jnp.where(place == 2.0 * slot + float(b), by_span, 0.0)
            own = jnp.dot(
                single.astype(jnp.bfloat16), ones, preferred_element_type=jnp.float32
            )
            target = jnp.where(active, base[...] + 2.0 * own, -1.0)
            for i in range(height // cols):
                picks[(2 * g + b) * cols : (2 * g + b + 1) * cols, i * cols : (i + 1) * cols] = (
                    (target == place + float(i * cols)).astype(jnp.float32).astype(picks.dtype)
                )
    for i in range(part.shape[0] // (SPAN * WIDE)):
        x = beside(
            [
                p + o.astype(jnp.float32)
                for p, o in zip(spans_of(part, i, WIDE), spans_of(other, i, WIDE))
            ]
        )
        put(whole, i, WIDE, x)
        high, low = split(x)
        put(rows, i, WIDE, product(forward, [high, low, high]))
    first = left_half(cols)
    for g in range(ROW_GROUPS):
        sent[g * cols : (g + 1) * cols, :] = chosen(picks, rows, g, first).astype(sent.dtype)


def spectrum_kernel(part, other, far, picks, numbers, forward, advanced, sent, rows):
    for i in range(part.shape[0] // (SPAN * WIDE)):
        x = beside(
            [
                p + o.astype(jnp.float32)
                for p, o in zip(spans_of(part, i, WIDE), spans_of(other, i, WIDE))
            ]
        )
        put(advanced, i, WIDE, x)
        high, low = split(x)
        put(rows, i, WIDE, product(forward, [high, low, high]))
    cols = part.shape[1]
    first = left_half(cols)
    for g in range(ROW_GROUPS):
        message = slice(g * cols, (g + 1) * cols)
        total = chosen(picks, rows, g, first) + far[message, :].astype(jnp.float32)
        sent[message, :] = (total.T + numbers[message, :].astype(jnp.float32)).astype(sent.dtype)


def kept_kernel(advanced, far, mask, forward, backward, kept):
    for i in range(kept.shape[0] // (SPAN * WIDE)):
        x = beside(
            [
                n + f.astype(jnp.float32)
                for n, f in zip(spans_of(advanced, i, WIDE), spans_of(far, i, WIDE))
            ]
        )
        high, low = split(chosen_rows(x, mask, forward, i))
        put(kept, i, WIDE, x - product(backward, [high, low, high]))


def total_kernel(pieces, unpack, backward, totals, placed):
    wide = pieces.shape[1]
    spans = totals.shape[1] // SPAN
    lane = lax.broadcasted_iota(jnp.int32, (BLK, wide), 0).astype(jnp.float32)
    for t in range(pieces.shape[0] // wide):
        values = pieces[t * wide : (t + 1) * wide, :].astype(jnp.float32).T
        numbers = jnp.dot(
            values[wide - OWN_COLS :, :].astype(jnp.bfloat16),
            unpack[...],
            preferred_element_type=jnp.float32,
        )
        most = wide // (2 * spans)
        for a in range(spans):
            upper = jnp.zeros((BLK, wide), jnp.float32)
            lower = upper
            for k in range(most):
                at = a * most + k
                down, across = at % OWN_COLS, at // OWN_COLS * wide
                here = numbers[down : down + 1, across : across + wide] == lane
                upper = jnp.where(here, values[2 * at : 2 * at + 1, :], upper)
                lower = jnp.where(here, values[2 * at + 1 : 2 * at + 2, :], lower)
            both = jnp.concatenate([upper, lower], axis=0)
            placed[a * SPAN : (a + 1) * SPAN, t * wide : (t + 1) * wide] = both.astype(placed.dtype)
    shape = (2 * OWN_COLS, placed.shape[1])
    column = lax.broadcasted_iota(jnp.int32, shape, 1) & (OWN_COLS - 1)
    row = lax.broadcasted_iota(jnp.int32, shape, 0) & (OWN_COLS - 1)
    total = lax.dot_general(
        (column == row).astype(jnp.float32).astype(placed.dtype),
        placed[...],
        (((1,), (1,)), ((), ())),
        preferred_element_type=jnp.float32,
    )
    pair = 2 * SPAN
    for i in range(totals.shape[1] // pair):
        high, low = split(total[:, i * pair : (i + 1) * pair])
        done = jnp.dot(
            jnp.concatenate([high, low, high], axis=1),
            backward[...],
            preferred_element_type=jnp.float32,
        ).astype(totals.dtype)
        for r in range(totals.shape[0] // shape[0]):
            totals[r * shape[0] : (r + 1) * shape[0], i * pair : (i + 1) * pair] = done


def turn_kernel(turned, update):
    cols, height = update.shape[1], turned.shape[1]
    for g in range(ROW_GROUPS):
        for i in range(height // cols):
            rows = g * height + i * cols
            block = turned[g * cols : (g + 1) * cols, i * cols : (i + 1) * cols]
            update[rows : rows + cols, :] = block.astype(jnp.float32).T.astype(update.dtype)


def gram(a, k):
    return lax.dot_general(a, k, (((0,), (0,)), ((), ())), preferred_element_type=jnp.float32)


VMEM, SMEM, HBM = (
    pl.BlockSpec(memory_space=space) for space in (pltpu.VMEM, pltpu.SMEM, pltpu.HBM)
)


def call(kernel, name, outs, *args, places=None, scratch=()):
    return pl.pallas_call(
        kernel,
        out_shape=outs,
        in_specs=places or [VMEM] * len(args),
        out_specs=(VMEM,) * len(outs),
        scratch_shapes=scratch,
        compiler_params=pltpu.CompilerParams(vmem_limit_bytes=10 << 20),
        cost_estimate=pl.CostEstimate(flops=0, bytes_accessed=0, transcendentals=0),
        name=name,
    )(*args)


def shards(activations, key_grad, momentum, block_ids, counts, *, replicas, group):
    tokens, features = activations.shape
    cols = key_grad.shape[1]
    chips = group // 2

    def along(x, step):
        return lax.ppermute(x, "tensor", [(i, (i + 2 * step) % group) for i in range(group)])

    def swap(x):
        return lax.ppermute(x, "tensor", [(i, i ^ 1) for i in range(group)])

    near_rows = jax.ShapeDtypeStruct((len(NEAR) * tokens, cols), jnp.bfloat16)
    far_rows = jax.ShapeDtypeStruct((2 * tokens + 16, cols), jnp.bfloat16)
    ids = jnp.transpose(block_ids[0], (2, 1, 0))
    (far_keys,) = call(
        functools.partial(far_keys_kernel, chips, tokens),
        "far_keys",
        (far_rows,),
        pltpu.with_memory_space_constraint(key_grad, pltpu.HBM),
        pltpu.with_memory_space_constraint(ids, pltpu.HBM),
        places=[HBM, HBM],
        scratch=(pltpu.VMEM(ids.shape, jnp.int32), pltpu.SemaphoreType.DMA((2,))),
    )
    activations, key_grad, far_keys = lax.optimization_barrier(
        (activations, key_grad, far_keys)
    )
    far_keys = along(far_keys, FAR)
    left, right = along(activations, 1), along(activations, -1)

    block_rows = jax.ShapeDtypeStruct((tokens, cols), jnp.bfloat16)
    far_own, far_theirs = call(
        functools.partial(pair_kernel, tokens), "pair", (block_rows, block_rows), far_keys
    )
    far_theirs = swap(far_theirs)
    far_other = swap(gram(activations, far_theirs).astype(jnp.bfloat16))
    far_part = gram(activations, far_own)
    own_keys, partner_keys = call(
        functools.partial(keys_kernel, chips, tokens), "keys", (near_rows, near_rows), key_grad
    )
    their_keys = swap(partner_keys)

    flat = jax.ShapeDtypeStruct((features, cols), jnp.float32)
    flat_half = jax.ShapeDtypeStruct((features, cols), jnp.bfloat16)
    high, low = cosine_parts()
    forward = jnp.asarray(np.concatenate([high, high, low], axis=1))
    backward = jnp.asarray(np.concatenate([high.T, high.T, low.T], axis=1))
    height = features // ROW_GROUPS
    lines = np.arange(cols)
    base = SPAN * (lines // (2 * block_ids.shape[3])) + lines % 2
    base = jnp.asarray(np.repeat(base[:, None], cols, axis=1).astype(np.float32))
    picks_shape = (2 * ROW_GROUPS * cols, height)
    mask, picks, numbers = call(
        routes_kernel,
        "routes",
        (
            flat_half,
            jax.ShapeDtypeStruct(picks_shape, jnp.bfloat16),
            jax.ShapeDtypeStruct((ROW_GROUPS * cols, cols), jnp.bfloat16),
        ),
        ids,
        counts,
        base,
        places=[SMEM, SMEM, VMEM],
    )

    most = block_ids.shape[3]
    span = lines // (2 * most)
    each = features // SPAN // ROW_GROUPS
    span_table = np.concatenate(
        [(span[:, None] + g * each == lines) & (span[:, None] < each) for g in range(ROW_GROUPS)]
    )
    slot_table = np.where(span < each, lines % (2 * most) // 2, most)
    slot_table = np.repeat(slot_table[:, None], cols, axis=1)
    far_whole, far_sent = call(
        far_kernel,
        "far",
        (flat_half, jax.ShapeDtypeStruct((ROW_GROUPS * cols, cols), jnp.bfloat16)),
        far_keys[2 * tokens :],
        counts,
        jnp.asarray(span_table.astype(np.float32).astype(ml_dtypes.bfloat16)),
        jnp.asarray(slot_table.astype(np.float32)),
        base,
        far_part,
        far_other,
        forward,
        places=[VMEM, SMEM] + [VMEM] * 6,
        scratch=(
            pltpu.VMEM(picks_shape, jnp.bfloat16),
            pltpu.VMEM((features, cols), jnp.bfloat16),
        ),
    )
    far_sent = along(far_sent, FAR)

    keys = jnp.concatenate([own_keys, their_keys], axis=1)
    keys = lax.optimization_barrier(keys.reshape(len(NEAR), tokens, 2 * cols))
    left, right = lax.optimization_barrier((left, right))
    near = gram(activations, keys[0]) + gram(right, keys[1]) + gram(left, keys[2])
    other, far_whole = lax.optimization_barrier(
        (near[:, cols:].astype(jnp.bfloat16), far_whole)
    )
    other, far_whole = swap(other), along(far_whole, FAR)
    part = near[:, :cols] + 0.999 * momentum[0]

    order = np.concatenate([np.arange(0, SPAN, 2), np.arange(1, SPAN, 2)])
    both_high, both_low = (np.kron(np.eye(2, dtype=p.dtype), p[order]) for p in (high, low))
    backward_pair = jnp.asarray(np.concatenate([both_high, both_high, both_low], axis=0))

    message = jax.ShapeDtypeStruct((ROW_GROUPS * cols, cols), jnp.bfloat16)
    advanced, sent = call(
        spectrum_kernel,
        "spectrum",
        (flat, message),
        part,
        other,
        far_sent,
        picks,
        numbers,
        forward,
        scratch=(pltpu.VMEM((features, cols), jnp.bfloat16),),
    )

    def exchange(x):
        return lax.all_to_all(
            x.reshape(replicas, OWN_COLS, x.shape[1]), "dp", 0, 0, tiled=True
        ).reshape(x.shape)

    pieces = exchange(sent)
    unpack = np.concatenate(
        [
            np.kron(np.eye(cols // OWN_COLS), np.outer(np.eye(OWN_COLS)[c], np.ones(OWN_COLS)))
            for c in range(OWN_COLS)
        ],
        axis=1,
    )
    (totals,) = call(
        total_kernel,
        "total",
        (jax.ShapeDtypeStruct((replicas * OWN_COLS, height), jnp.bfloat16),),
        pieces,
        jnp.asarray(unpack.astype(ml_dtypes.bfloat16)),
        backward_pair,
        scratch=(pltpu.VMEM((height, replicas * OWN_COLS), jnp.bfloat16),),
    )
    totals, far_whole = lax.optimization_barrier((totals, far_whole))
    (kept,) = call(kept_kernel, "kept", (flat,), advanced, far_whole, mask, forward, backward)
    (update,) = call(turn_kernel, "turn", (flat_half,), exchange(totals))
    return kept[None], update


def solution(mesh):
    in_specs = (
        P(("dp", "tensor"), None),
        P("dp", "tensor"),
        P("dp", None, "tensor"),
        P("dp", None, "tensor", None),
        P("dp"),
    )
    out_specs = (P("dp", None, "tensor"), P(None, "tensor"))
    body = functools.partial(shards, replicas=mesh.shape["dp"], group=mesh.shape["tensor"])
    return jax.shard_map(body, mesh=mesh, in_specs=in_specs, out_specs=out_specs, check_vma=False)
```

```python
import functools

import jax
import jax.numpy as jnp
import ml_dtypes
import numpy as np
from jax import lax
from jax.experimental import pallas as pl
from jax.experimental.pallas import tpu as pltpu
from jax.sharding import PartitionSpec as P

BLK = 32
SPAN = 64
WIDE = 4
ROW_GROUPS = 4
OWN_COLS = 8
NEAR = (0, 1, 3)
FAR = 2


def cosine_parts():
    n = np.arange(SPAN, dtype=np.float64)
    table = np.cos(np.pi * (2.0 * n[None, :] + 1.0) * n[:, None] / 128.0) * np.sqrt(2.0 / SPAN)
    table[0] *= np.sqrt(0.5)
    high = table.astype(ml_dtypes.bfloat16)
    low = (table - high.astype(np.float64)).astype(ml_dtypes.bfloat16)
    return high, low


def split(x):
    high = x.astype(jnp.bfloat16)
    return high, (x - high.astype(jnp.float32)).astype(jnp.bfloat16)


def spans_of(ref, i, count):
    first = i * count * SPAN
    return [ref[first + s * SPAN : first + (s + 1) * SPAN, :] for s in range(count)]


def beside(parts):
    return jnp.concatenate(parts, axis=1)


def product(table, parts):
    return jnp.dot(table[...], jnp.concatenate(parts, axis=0), preferred_element_type=jnp.float32)


def put(ref, i, count, value):
    cols = ref.shape[1]
    for s in range(count):
        first = (i * count + s) * SPAN
        ref[first : first + SPAN, :] = value[:, s * cols : (s + 1) * cols].astype(ref.dtype)


def far_keys_kernel(tokens, keys, ids, far, numbers, done):
    chip = lax.shift_right_logical(lax.axis_index("tensor"), 1)
    first = 2 * lax.bitwise_xor(chip, FAR) * tokens
    rows = pltpu.make_async_copy(
        keys.at[pl.ds(pl.multiple_of(first, 16), 2 * tokens)],
        far.at[pl.ds(0, 2 * tokens)],
        done.at[0],
    )
    listed = pltpu.make_async_copy(ids, numbers, done.at[1])
    rows.start()
    listed.start()
    listed.wait()
    most, halves, spans = ids.shape
    lines = [numbers[k].astype(jnp.float32) for k in range(most)]
    lines.append(jnp.zeros((16 - most * halves, spans), jnp.float32))
    lines = jnp.concatenate(lines, axis=0)
    lines = jnp.concatenate([lines, jnp.zeros((16, far.shape[1] - spans), jnp.float32)], axis=1)
    far[2 * tokens :, :] = lines.astype(far.dtype)
    rows.wait()


def keys_kernel(tokens, keys, own, partner):
    spot = lax.axis_index("tensor")
    chip, core = lax.shift_right_logical(spot, 1), lax.bitwise_and(spot, 1)

    def block(step, which):
        first = (2 * lax.bitwise_xor(chip, step) + which) * tokens
        return keys[pl.ds(pl.multiple_of(first, 16), tokens), :]

    for place, step in enumerate(NEAR):
        here = slice(place * tokens, (place + 1) * tokens)
        own[here, :] = block(step, core)
        partner[here, :] = block(step, 1 - core)


def pair_kernel(tokens, far, mine, theirs):
    core = lax.bitwise_and(lax.axis_index("tensor"), 1)
    mine[...] = far[pl.ds(pl.multiple_of(core * tokens, 16), tokens), :]
    theirs[...] = far[pl.ds(pl.multiple_of((1 - core) * tokens, 16), tokens), :]


def routes_kernel(ids, count, base, mask, picks, numbers):
    cols = mask.shape[1]
    spans = mask.shape[0] // SPAN
    most = ids.shape[0]
    each = spans // ROW_GROUPS

    def number(a, b, k):
        return jnp.where(k < count[0], ids[k, b, a], -1)

    block = lax.shift_right_logical(lax.broadcasted_iota(jnp.int32, (SPAN, cols), 0), 1)
    first = lax.broadcasted_iota(jnp.int32, (SPAN, cols), 1) < SPAN

    def body(a, _):
        hit = jnp.zeros((SPAN, cols), jnp.bool_)
        for k in range(most):
            hit = hit | (jnp.where(first, number(a, 0, k), number(a, 1, k)) == block)
        rows = pl.ds(pl.multiple_of(a * SPAN, SPAN), SPAN)
        mask[rows, :] = hit.astype(jnp.float32).astype(mask.dtype)
        return 0

    lax.fori_loop(0, spans, body, 0)

    lane = lax.broadcasted_iota(jnp.int32, (SPAN, cols), 1)
    square = (cols, cols)
    column = lax.broadcasted_iota(jnp.int32, square, 1)
    slot = lax.shift_right_logical(lax.broadcasted_iota(jnp.int32, square, 0), 1)
    double = (column == slot).astype(jnp.float32).astype(jnp.bfloat16)
    place = column.astype(jnp.float32)
    row = lax.broadcasted_iota(jnp.int32, square, 0)
    spread = lax.shift_right_logical(column, 3) == (row & (OWN_COLS - 1))
    gather = (column == (row & (OWN_COLS - 1)) + cols - OWN_COLS).astype(jnp.float32)
    gather = gather.astype(jnp.bfloat16)
    for g in range(ROW_GROUPS):
        halves = []
        for b in range(2):
            line = jnp.full((SPAN, cols), -1, jnp.int32)
            for a in range(each):
                for k in range(most):
                    line = jnp.where(lane == a * most + k, number(g * each + a, b, k), line)
            halves.append(line)
        tile = jnp.concatenate(halves, axis=0).astype(jnp.float32)
        packed = jnp.dot(
            jnp.where(spread, tile, 0.0).astype(jnp.bfloat16),
            gather,
            preferred_element_type=jnp.float32,
        )
        numbers[g * cols : (g + 1) * cols, :] = packed.astype(numbers.dtype)
        twice = jnp.dot(
            double, tile.T.astype(jnp.bfloat16), preferred_element_type=jnp.float32
        )
        for b in range(2):
            own = jnp.broadcast_to(twice[:, b * SPAN : b * SPAN + 1], square)
            target = jnp.where(own < 0.0, -1.0, base[...] + 2.0 * own)
            for i in range(picks.shape[1] // cols):
                picks[(2 * g + b) * cols : (2 * g + b + 1) * cols, i * cols : (i + 1) * cols] = (
                    (target == place + float(i * cols)).astype(jnp.float32).astype(picks.dtype)
                )


def chosen_rows(x, mask, forward, i):
    high, low = split(x)
    keep = beside(spans_of(mask, i, WIDE)).astype(jnp.float32)
    return product(forward, [high, low, high]) * keep


def chosen(picks, rows, group, first):
    cols = rows.shape[1]
    height = picks.shape[1]
    band = rows[group * height : (group + 1) * height, :]
    one, two = (
        jnp.dot(
            picks[(2 * group + b) * cols : (2 * group + b + 1) * cols, :],
            band,
            preferred_element_type=jnp.float32,
        )
        for b in range(2)
    )
    return jnp.where(first, one, two)


def left_half(cols):
    return lax.broadcasted_iota(jnp.int32, (cols, cols), 1) < SPAN


def far_kernel(
    numbers, count, spans, slots, base, part, other, forward, whole, sent, picks, rows
):
    cols = part.shape[1]
    height = picks.shape[1]
    square = (cols, cols)
    known = numbers[...].astype(jnp.float32)
    known = jnp.concatenate(
        [known, jnp.zeros((cols - known.shape[0], cols), jnp.float32)], axis=0
    ).T.astype(jnp.bfloat16)
    place = lax.broadcasted_iota(jnp.int32, square, 1).astype(jnp.float32)
    ones = jnp.ones(square, jnp.bfloat16)
    slot = slots[...]
    active = slot < count[0].astype(jnp.float32)
    for g in range(ROW_GROUPS):
        by_span = jnp.dot(
            spans[g * cols : (g + 1) * cols, :], known, preferred_element_type=jnp.float32
        )
        for b in range(2):
            single = jnp.where(place == 2.0 * slot + float(b), by_span, 0.0)
            own = jnp.dot(
                single.astype(jnp.bfloat16), ones, preferred_element_type=jnp.float32
            )
            target = jnp.where(active, base[...] + 2.0 * own, -1.0)
            for i in range(height // cols):
                picks[(2 * g + b) * cols : (2 * g + b + 1) * cols, i * cols : (i + 1) * cols] = (
                    (target == place + float(i * cols)).astype(jnp.float32).astype(picks.dtype)
                )
    for i in range(part.shape[0] // (SPAN * WIDE)):
        x = beside(
            [
                p + o.astype(jnp.float32)
                for p, o in zip(spans_of(part, i, WIDE), spans_of(other, i, WIDE))
            ]
        )
        put(whole, i, WIDE, x)
        high, low = split(x)
        put(rows, i, WIDE, product(forward, [high, low, high]))
    first = left_half(cols)
    for g in range(ROW_GROUPS):
        sent[g * cols : (g + 1) * cols, :] = chosen(picks, rows, g, first).astype(sent.dtype)


def spectrum_kernel(part, other, far, picks, numbers, forward, advanced, sent, rows):
    for i in range(part.shape[0] // (SPAN * WIDE)):
        x = beside(
            [
                p + o.astype(jnp.float32)
                for p, o in zip(spans_of(part, i, WIDE), spans_of(other, i, WIDE))
            ]
        )
        put(advanced, i, WIDE, x)
        high, low = split(x)
        put(rows, i, WIDE, product(forward, [high, low, high]))
    cols = part.shape[1]
    first = left_half(cols)
    for g in range(ROW_GROUPS):
        message = slice(g * cols, (g + 1) * cols)
        total = chosen(picks, rows, g, first) + far[message, :].astype(jnp.float32)
        sent[message, :] = (total.T + numbers[message, :].astype(jnp.float32)).astype(sent.dtype)


def kept_kernel(advanced, far, mask, forward, backward, kept):
    for i in range(kept.shape[0] // (SPAN * WIDE)):
        x = beside(
            [
                n + f.astype(jnp.float32)
                for n, f in zip(spans_of(advanced, i, WIDE), spans_of(far, i, WIDE))
            ]
        )
        high, low = split(chosen_rows(x, mask, forward, i))
        put(kept, i, WIDE, x - product(backward, [high, low, high]))


def total_kernel(pieces, unpack, backward, totals, placed):
    wide = pieces.shape[1]
    spans = totals.shape[1] // SPAN
    lane = lax.broadcasted_iota(jnp.int32, (BLK, wide), 0).astype(jnp.float32)
    for t in range(pieces.shape[0] // wide):
        values = pieces[t * wide : (t + 1) * wide, :].astype(jnp.float32).T
        numbers = jnp.dot(
            values[wide - OWN_COLS :, :].astype(jnp.bfloat16),
            unpack[...],
            preferred_element_type=jnp.float32,
        )
        most = wide // (2 * spans)
        for a in range(spans):
            upper = jnp.zeros((BLK, wide), jnp.float32)
            lower = upper
            for k in range(most):
                at = a * most + k
                down, across = at % OWN_COLS, at // OWN_COLS * wide
                here = numbers[down : down + 1, across : across + wide] == lane
                upper = jnp.where(here, values[2 * at : 2 * at + 1, :], upper)
                lower = jnp.where(here, values[2 * at + 1 : 2 * at + 2, :], lower)
            both = jnp.concatenate([upper, lower], axis=0)
            placed[a * SPAN : (a + 1) * SPAN, t * wide : (t + 1) * wide] = both.astype(placed.dtype)
    shape = (2 * OWN_COLS, placed.shape[1])
    column = lax.broadcasted_iota(jnp.int32, shape, 1) & (OWN_COLS - 1)
    row = lax.broadcasted_iota(jnp.int32, shape, 0) & (OWN_COLS - 1)
    total = lax.dot_general(
        (column == row).astype(jnp.float32).astype(placed.dtype),
        placed[...],
        (((1,), (1,)), ((), ())),
        preferred_element_type=jnp.float32,
    )
    pair = 2 * SPAN
    for i in range(totals.shape[1] // pair):
        high, low = split(total[:, i * pair : (i + 1) * pair])
        done = jnp.dot(
            jnp.concatenate([high, low, high], axis=1),
            backward[...],
            preferred_element_type=jnp.float32,
        ).astype(totals.dtype)
        for r in range(totals.shape[0] // shape[0]):
            totals[r * shape[0] : (r + 1) * shape[0], i * pair : (i + 1) * pair] = done


def turn_kernel(turned, update):
    cols, height = update.shape[1], turned.shape[1]
    for g in range(ROW_GROUPS):
        for i in range(height // cols):
            rows = g * height + i * cols
            block = turned[g * cols : (g + 1) * cols, i * cols : (i + 1) * cols]
            update[rows : rows + cols, :] = block.astype(jnp.float32).T.astype(update.dtype)


def gram(a, k):
    return lax.dot_general(a, k, (((0,), (0,)), ((), ())), preferred_element_type=jnp.float32)


VMEM, SMEM, HBM = (
    pl.BlockSpec(memory_space=space) for space in (pltpu.VMEM, pltpu.SMEM, pltpu.HBM)
)


def call(kernel, name, outs, *args, places=None, scratch=()):
    return pl.pallas_call(
        kernel,
        out_shape=outs,
        in_specs=places or [VMEM] * len(args),
        out_specs=(VMEM,) * len(outs),
        scratch_shapes=scratch,
        compiler_params=pltpu.CompilerParams(vmem_limit_bytes=10 << 20),
        cost_estimate=pl.CostEstimate(flops=0, bytes_accessed=0, transcendentals=0),
        name=name,
    )(*args)


def shards(activations, key_grad, momentum, block_ids, counts, *, replicas, group):
    tokens, features = activations.shape
    cols = key_grad.shape[1]

    def along(x, step):
        return lax.ppermute(x, "tensor", [(i, i ^ (2 * step)) for i in range(group)])

    def swap(x):
        return lax.ppermute(x, "tensor", [(i, i ^ 1) for i in range(group)])

    near_rows = jax.ShapeDtypeStruct((len(NEAR) * tokens, cols), jnp.bfloat16)
    far_rows = jax.ShapeDtypeStruct((2 * tokens + 16, cols), jnp.bfloat16)
    ids = jnp.transpose(block_ids[0], (2, 1, 0))
    (far_keys,) = call(
        functools.partial(far_keys_kernel, tokens),
        "far_keys",
        (far_rows,),
        pltpu.with_memory_space_constraint(key_grad, pltpu.HBM),
        pltpu.with_memory_space_constraint(ids, pltpu.HBM),
        places=[HBM, HBM],
        scratch=(pltpu.VMEM(ids.shape, jnp.int32), pltpu.SemaphoreType.DMA((2,))),
    )
    activations, key_grad, far_keys = lax.optimization_barrier(
        (activations, key_grad, far_keys)
    )
    far_keys = along(far_keys, FAR)
    first, second = (along(activations, step) for step in NEAR[1:])

    block_rows = jax.ShapeDtypeStruct((tokens, cols), jnp.bfloat16)
    far_own, far_theirs = call(
        functools.partial(pair_kernel, tokens), "pair", (block_rows, block_rows), far_keys
    )
    far_theirs = swap(far_theirs)
    far_other = swap(gram(activations, far_theirs).astype(jnp.bfloat16))
    far_part = gram(activations, far_own)
    own_keys, partner_keys = call(
        functools.partial(keys_kernel, tokens), "keys", (near_rows, near_rows), key_grad
    )
    their_keys = swap(partner_keys)

    flat = jax.ShapeDtypeStruct((features, cols), jnp.float32)
    flat_half = jax.ShapeDtypeStruct((features, cols), jnp.bfloat16)
    high, low = cosine_parts()
    forward = jnp.asarray(np.concatenate([high, high, low], axis=1))
    backward = jnp.asarray(np.concatenate([high.T, high.T, low.T], axis=1))
    height = features // ROW_GROUPS
    lines = np.arange(cols)
    base = SPAN * (lines // (2 * block_ids.shape[3])) + lines % 2
    base = jnp.asarray(np.repeat(base[:, None], cols, axis=1).astype(np.float32))
    picks_shape = (2 * ROW_GROUPS * cols, height)
    mask, picks, numbers = call(
        routes_kernel,
        "routes",
        (
            flat_half,
            jax.ShapeDtypeStruct(picks_shape, jnp.bfloat16),
            jax.ShapeDtypeStruct((ROW_GROUPS * cols, cols), jnp.bfloat16),
        ),
        ids,
        counts,
        base,
        places=[SMEM, SMEM, VMEM],
    )

    most = block_ids.shape[3]
    span = lines // (2 * most)
    each = features // SPAN // ROW_GROUPS
    span_table = np.concatenate(
        [(span[:, None] + g * each == lines) & (span[:, None] < each) for g in range(ROW_GROUPS)]
    )
    slot_table = np.where(span < each, lines % (2 * most) // 2, most)
    slot_table = np.repeat(slot_table[:, None], cols, axis=1)
    far_whole, far_sent = call(
        far_kernel,
        "far",
        (flat_half, jax.ShapeDtypeStruct((ROW_GROUPS * cols, cols), jnp.bfloat16)),
        far_keys[2 * tokens :],
        counts,
        jnp.asarray(span_table.astype(np.float32).astype(ml_dtypes.bfloat16)),
        jnp.asarray(slot_table.astype(np.float32)),
        base,
        far_part,
        far_other,
        forward,
        places=[VMEM, SMEM] + [VMEM] * 6,
        scratch=(
            pltpu.VMEM(picks_shape, jnp.bfloat16),
            pltpu.VMEM((features, cols), jnp.bfloat16),
        ),
    )
    far_sent = along(far_sent, FAR)

    keys = jnp.concatenate([own_keys, their_keys], axis=1)
    keys = lax.optimization_barrier(keys.reshape(len(NEAR), tokens, 2 * cols))
    first, second = lax.optimization_barrier((first, second))
    near = gram(activations, keys[0]) + gram(first, keys[1]) + gram(second, keys[2])
    other, far_whole = lax.optimization_barrier(
        (near[:, cols:].astype(jnp.bfloat16), far_whole)
    )
    other, far_whole = swap(other), along(far_whole, FAR)
    part = near[:, :cols] + 0.999 * momentum[0]

    order = np.concatenate([np.arange(0, SPAN, 2), np.arange(1, SPAN, 2)])
    both_high, both_low = (np.kron(np.eye(2, dtype=p.dtype), p[order]) for p in (high, low))
    backward_pair = jnp.asarray(np.concatenate([both_high, both_high, both_low], axis=0))

    message = jax.ShapeDtypeStruct((ROW_GROUPS * cols, cols), jnp.bfloat16)
    advanced, sent = call(
        spectrum_kernel,
        "spectrum",
        (flat, message),
        part,
        other,
        far_sent,
        picks,
        numbers,
        forward,
        scratch=(pltpu.VMEM((features, cols), jnp.bfloat16),),
    )

    def exchange(x):
        return lax.all_to_all(
            x.reshape(replicas, OWN_COLS, x.shape[1]), "dp", 0, 0, tiled=True
        ).reshape(x.shape)

    pieces = exchange(sent)
    unpack = np.concatenate(
        [
            np.kron(np.eye(cols // OWN_COLS), np.outer(np.eye(OWN_COLS)[c], np.ones(OWN_COLS)))
            for c in range(OWN_COLS)
        ],
        axis=1,
    )
    (totals,) = call(
        total_kernel,
        "total",
        (jax.ShapeDtypeStruct((replicas * OWN_COLS, height), jnp.bfloat16),),
        pieces,
        jnp.asarray(unpack.astype(ml_dtypes.bfloat16)),
        backward_pair,
        scratch=(pltpu.VMEM((height, replicas * OWN_COLS), jnp.bfloat16),),
    )
    totals, far_whole = lax.optimization_barrier((totals, far_whole))
    (kept,) = call(kept_kernel, "kept", (flat,), advanced, far_whole, mask, forward, backward)
    (update,) = call(turn_kernel, "turn", (flat_half,), exchange(totals))
    return kept[None], update


def solution(mesh):
    in_specs = (
        P(("dp", "tensor"), None),
        P("dp", "tensor"),
        P("dp", None, "tensor"),
        P("dp", None, "tensor", None),
        P("dp"),
    )
    out_specs = (P("dp", None, "tensor"), P(None, "tensor"))
    body = functools.partial(shards, replicas=mesh.shape["dp"], group=mesh.shape["tensor"])
    return jax.shard_map(body, mesh=mesh, in_specs=in_specs, out_specs=out_specs, check_vma=False)
```

```python
import functools

import jax
import jax.numpy as jnp
import ml_dtypes
import numpy as np
from jax import lax
from jax.experimental import pallas as pl
from jax.experimental.pallas import tpu as pltpu
from jax.sharding import PartitionSpec as P

BLK = 32
SPAN = 64
WIDE = 4
ROW_GROUPS = 4
OWN_COLS = 8
NEAR = (0, 3, 1)
FAR = 2


def cosine_parts():
    n = np.arange(SPAN, dtype=np.float64)
    table = np.cos(np.pi * (2.0 * n[None, :] + 1.0) * n[:, None] / 128.0) * np.sqrt(2.0 / SPAN)
    table[0] *= np.sqrt(0.5)
    high = table.astype(ml_dtypes.bfloat16)
    low = (table - high.astype(np.float64)).astype(ml_dtypes.bfloat16)
    return high, low


def split(x):
    high = x.astype(jnp.bfloat16)
    return high, (x - high.astype(jnp.float32)).astype(jnp.bfloat16)


def spans_of(ref, i, count):
    first = i * count * SPAN
    return [ref[first + s * SPAN : first + (s + 1) * SPAN, :] for s in range(count)]


def beside(parts):
    return jnp.concatenate(parts, axis=1)


def product(table, parts):
    return jnp.dot(table[...], jnp.concatenate(parts, axis=0), preferred_element_type=jnp.float32)


def put(ref, i, count, value):
    cols = ref.shape[1]
    for s in range(count):
        first = (i * count + s) * SPAN
        ref[first : first + SPAN, :] = value[:, s * cols : (s + 1) * cols].astype(ref.dtype)


def far_keys_kernel(tokens, keys, ids, far, numbers, done):
    chip = lax.shift_right_logical(lax.axis_index("tensor"), 1)
    first = 2 * lax.bitwise_xor(chip, FAR) * tokens
    rows = pltpu.make_async_copy(
        keys.at[pl.ds(pl.multiple_of(first, 16), 2 * tokens)],
        far.at[pl.ds(0, 2 * tokens)],
        done.at[0],
    )
    listed = pltpu.make_async_copy(ids, numbers, done.at[1])
    rows.start()
    listed.start()
    listed.wait()
    most, halves, spans = ids.shape
    lines = [numbers[k].astype(jnp.float32) for k in range(most)]
    lines.append(jnp.zeros((16 - most * halves, spans), jnp.float32))
    lines = jnp.concatenate(lines, axis=0)
    lines = jnp.concatenate([lines, jnp.zeros((16, far.shape[1] - spans), jnp.float32)], axis=1)
    far[2 * tokens :, :] = lines.astype(far.dtype)
    rows.wait()


def keys_kernel(tokens, keys, own, partner):
    spot = lax.axis_index("tensor")
    chip, core = lax.shift_right_logical(spot, 1), lax.bitwise_and(spot, 1)

    def block(step, which):
        first = (2 * lax.bitwise_xor(chip, step) + which) * tokens
        return keys[pl.ds(pl.multiple_of(first, 16), tokens), :]

    for place, step in enumerate(NEAR):
        here = slice(place * tokens, (place + 1) * tokens)
        own[here, :] = block(step, core)
        partner[here, :] = block(step, 1 - core)


def pair_kernel(tokens, far, mine, theirs):
    core = lax.bitwise_and(lax.axis_index("tensor"), 1)
    mine[...] = far[pl.ds(pl.multiple_of(core * tokens, 16), tokens), :]
    theirs[...] = far[pl.ds(pl.multiple_of((1 - core) * tokens, 16), tokens), :]


def routes_kernel(ids, count, base, mask, picks, numbers):
    cols = mask.shape[1]
    spans = mask.shape[0] // SPAN
    most = ids.shape[0]
    each = spans // ROW_GROUPS

    def number(a, b, k):
        return jnp.where(k < count[0], ids[k, b, a], -1)

    block = lax.shift_right_logical(lax.broadcasted_iota(jnp.int32, (SPAN, cols), 0), 1)
    first = lax.broadcasted_iota(jnp.int32, (SPAN, cols), 1) < SPAN

    def body(a, _):
        hit = jnp.zeros((SPAN, cols), jnp.bool_)
        for k in range(most):
            hit = hit | (jnp.where(first, number(a, 0, k), number(a, 1, k)) == block)
        rows = pl.ds(pl.multiple_of(a * SPAN, SPAN), SPAN)
        mask[rows, :] = hit.astype(jnp.float32).astype(mask.dtype)
        return 0

    lax.fori_loop(0, spans, body, 0)

    lane = lax.broadcasted_iota(jnp.int32, (SPAN, cols), 1)
    square = (cols, cols)
    column = lax.broadcasted_iota(jnp.int32, square, 1)
    slot = lax.shift_right_logical(lax.broadcasted_iota(jnp.int32, square, 0), 1)
    double = (column == slot).astype(jnp.float32).astype(jnp.bfloat16)
    place = column.astype(jnp.float32)
    row = lax.broadcasted_iota(jnp.int32, square, 0)
    spread = lax.shift_right_logical(column, 3) == (row & (OWN_COLS - 1))
    gather = (column == (row & (OWN_COLS - 1)) + cols - OWN_COLS).astype(jnp.float32)
    gather = gather.astype(jnp.bfloat16)
    for g in range(ROW_GROUPS):
        halves = []
        for b in range(2):
            line = jnp.full((SPAN, cols), -1, jnp.int32)
            for a in range(each):
                for k in range(most):
                    line = jnp.where(lane == a * most + k, number(g * each + a, b, k), line)
            halves.append(line)
        tile = jnp.concatenate(halves, axis=0).astype(jnp.float32)
        packed = jnp.dot(
            jnp.where(spread, tile, 0.0).astype(jnp.bfloat16),
            gather,
            preferred_element_type=jnp.float32,
        )
        numbers[g * cols : (g + 1) * cols, :] = packed.astype(numbers.dtype)
        twice = jnp.dot(
            double, tile.T.astype(jnp.bfloat16), preferred_element_type=jnp.float32
        )
        for b in range(2):
            own = jnp.broadcast_to(twice[:, b * SPAN : b * SPAN + 1], square)
            target = jnp.where(own < 0.0, -1.0, base[...] + 2.0 * own)
            for i in range(picks.shape[1] // cols):
                picks[(2 * g + b) * cols : (2 * g + b + 1) * cols, i * cols : (i + 1) * cols] = (
                    (target == place + float(i * cols)).astype(jnp.float32).astype(picks.dtype)
                )


def chosen_rows(x, mask, forward, i):
    high, low = split(x)
    keep = beside(spans_of(mask, i, WIDE)).astype(jnp.float32)
    return product(forward, [high, low, high]) * keep


def chosen(picks, rows, group, first):
    cols = rows.shape[1]
    height = picks.shape[1]
    band = rows[group * height : (group + 1) * height, :]
    one, two = (
        jnp.dot(
            picks[(2 * group + b) * cols : (2 * group + b + 1) * cols, :],
            band,
            preferred_element_type=jnp.float32,
        )
        for b in range(2)
    )
    return jnp.where(first, one, two)


def left_half(cols):
    return lax.broadcasted_iota(jnp.int32, (cols, cols), 1) < SPAN


def far_kernel(
    numbers, count, spans, slots, base, part, other, forward, whole, sent, picks, rows
):
    cols = part.shape[1]
    height = picks.shape[1]
    square = (cols, cols)
    known = numbers[...].astype(jnp.float32)
    known = jnp.concatenate(
        [known, jnp.zeros((cols - known.shape[0], cols), jnp.float32)], axis=0
    ).T.astype(jnp.bfloat16)
    place = lax.broadcasted_iota(jnp.int32, square, 1).astype(jnp.float32)
    ones = jnp.ones(square, jnp.bfloat16)
    slot = slots[...]
    active = slot < count[0].astype(jnp.float32)
    for g in range(ROW_GROUPS):
        by_span = jnp.dot(
            spans[g * cols : (g + 1) * cols, :], known, preferred_element_type=jnp.float32
        )
        for b in range(2):
            single = jnp.where(place == 2.0 * slot + float(b), by_span, 0.0)
            own = jnp.dot(
                single.astype(jnp.bfloat16), ones, preferred_element_type=jnp.float32
            )
            target = jnp.where(active, base[...] + 2.0 * own, -1.0)
            for i in range(height // cols):
                picks[(2 * g + b) * cols : (2 * g + b + 1) * cols, i * cols : (i + 1) * cols] = (
                    (target == place + float(i * cols)).astype(jnp.float32).astype(picks.dtype)
                )
    for i in range(part.shape[0] // (SPAN * WIDE)):
        x = beside(
            [
                p + o.astype(jnp.float32)
                for p, o in zip(spans_of(part, i, WIDE), spans_of(other, i, WIDE))
            ]
        )
        put(whole, i, WIDE, x)
        high, low = split(x)
        put(rows, i, WIDE, product(forward, [high, low, high]))
    first = left_half(cols)
    for g in range(ROW_GROUPS):
        sent[g * cols : (g + 1) * cols, :] = chosen(picks, rows, g, first).astype(sent.dtype)


def spectrum_kernel(part, other, far, picks, numbers, forward, advanced, sent, rows):
    for i in range(part.shape[0] // (SPAN * WIDE)):
        x = beside(
            [
                p + o.astype(jnp.float32)
                for p, o in zip(spans_of(part, i, WIDE), spans_of(other, i, WIDE))
            ]
        )
        put(advanced, i, WIDE, x)
        high, low = split(x)
        put(rows, i, WIDE, product(forward, [high, low, high]))
    cols = part.shape[1]
    first = left_half(cols)
    for g in range(ROW_GROUPS):
        message = slice(g * cols, (g + 1) * cols)
        total = chosen(picks, rows, g, first) + far[message, :].astype(jnp.float32)
        sent[message, :] = (total.T + numbers[message, :].astype(jnp.float32)).astype(sent.dtype)


def kept_kernel(advanced, far, mask, forward, backward, kept):
    for i in range(kept.shape[0] // (SPAN * WIDE)):
        x = beside(
            [
                n + f.astype(jnp.float32)
                for n, f in zip(spans_of(advanced, i, WIDE), spans_of(far, i, WIDE))
            ]
        )
        high, low = split(chosen_rows(x, mask, forward, i))
        put(kept, i, WIDE, x - product(backward, [high, low, high]))


def total_kernel(pieces, unpack, backward, totals, placed):
    wide = pieces.shape[1]
    spans = totals.shape[1] // SPAN
    lane = lax.broadcasted_iota(jnp.int32, (BLK, wide), 0).astype(jnp.float32)
    for t in range(pieces.shape[0] // wide):
        values = pieces[t * wide : (t + 1) * wide, :].astype(jnp.float32).T
        numbers = jnp.dot(
            values[wide - OWN_COLS :, :].astype(jnp.bfloat16),
            unpack[...],
            preferred_element_type=jnp.float32,
        )
        most = wide // (2 * spans)
        for a in range(spans):
            upper = jnp.zeros((BLK, wide), jnp.float32)
            lower = upper
            for k in range(most):
                at = a * most + k
                down, across = at % OWN_COLS, at // OWN_COLS * wide
                here = numbers[down : down + 1, across : across + wide] == lane
                upper = jnp.where(here, values[2 * at : 2 * at + 1, :], upper)
                lower = jnp.where(here, values[2 * at + 1 : 2 * at + 2, :], lower)
            both = jnp.concatenate([upper, lower], axis=0)
            placed[a * SPAN : (a + 1) * SPAN, t * wide : (t + 1) * wide] = both.astype(placed.dtype)
    shape = (2 * OWN_COLS, placed.shape[1])
    column = lax.broadcasted_iota(jnp.int32, shape, 1) & (OWN_COLS - 1)
    row = lax.broadcasted_iota(jnp.int32, shape, 0) & (OWN_COLS - 1)
    total = lax.dot_general(
        (column == row).astype(jnp.float32).astype(placed.dtype),
        placed[...],
        (((1,), (1,)), ((), ())),
        preferred_element_type=jnp.float32,
    )
    pair = 2 * SPAN
    for i in range(totals.shape[1] // pair):
        high, low = split(total[:, i * pair : (i + 1) * pair])
        done = jnp.dot(
            jnp.concatenate([high, low, high], axis=1),
            backward[...],
            preferred_element_type=jnp.float32,
        ).astype(totals.dtype)
        for r in range(totals.shape[0] // shape[0]):
            totals[r * shape[0] : (r + 1) * shape[0], i * pair : (i + 1) * pair] = done


def turn_kernel(turned, update):
    cols, height = update.shape[1], turned.shape[1]
    for g in range(ROW_GROUPS):
        for i in range(height // cols):
            rows = g * height + i * cols
            block = turned[g * cols : (g + 1) * cols, i * cols : (i + 1) * cols]
            update[rows : rows + cols, :] = block.astype(jnp.float32).T.astype(update.dtype)


def gram(a, k):
    return lax.dot_general(a, k, (((0,), (0,)), ((), ())), preferred_element_type=jnp.float32)


VMEM, SMEM, HBM = (
    pl.BlockSpec(memory_space=space) for space in (pltpu.VMEM, pltpu.SMEM, pltpu.HBM)
)


def call(kernel, name, outs, *args, places=None, scratch=()):
    return pl.pallas_call(
        kernel,
        out_shape=outs,
        in_specs=places or [VMEM] * len(args),
        out_specs=(VMEM,) * len(outs),
        scratch_shapes=scratch,
        compiler_params=pltpu.CompilerParams(vmem_limit_bytes=10 << 20),
        cost_estimate=pl.CostEstimate(flops=0, bytes_accessed=0, transcendentals=0),
        name=name,
    )(*args)


def shards(activations, key_grad, momentum, block_ids, counts, *, replicas, group):
    tokens, features = activations.shape
    cols = key_grad.shape[1]

    def along(x, step):
        return lax.ppermute(x, "tensor", [(i, i ^ (2 * step)) for i in range(group)])

    def swap(x):
        return lax.ppermute(x, "tensor", [(i, i ^ 1) for i in range(group)])

    near_rows = jax.ShapeDtypeStruct((len(NEAR) * tokens, cols), jnp.bfloat16)
    far_rows = jax.ShapeDtypeStruct((2 * tokens + 16, cols), jnp.bfloat16)
    ids = jnp.transpose(block_ids[0], (2, 1, 0))
    (far_keys,) = call(
        functools.partial(far_keys_kernel, tokens),
        "far_keys",
        (far_rows,),
        pltpu.with_memory_space_constraint(key_grad, pltpu.HBM),
        pltpu.with_memory_space_constraint(ids, pltpu.HBM),
        places=[HBM, HBM],
        scratch=(pltpu.VMEM(ids.shape, jnp.int32), pltpu.SemaphoreType.DMA((2,))),
    )
    activations, key_grad, far_keys = lax.optimization_barrier(
        (activations, key_grad, far_keys)
    )
    far_keys = along(far_keys, FAR)
    first, second = (along(activations, step) for step in NEAR[1:])

    block_rows = jax.ShapeDtypeStruct((tokens, cols), jnp.bfloat16)
    far_own, far_theirs = call(
        functools.partial(pair_kernel, tokens), "pair", (block_rows, block_rows), far_keys
    )
    far_theirs = swap(far_theirs)
    far_other = swap(gram(activations, far_theirs).astype(jnp.bfloat16))
    far_part = gram(activations, far_own)
    own_keys, partner_keys = call(
        functools.partial(keys_kernel, tokens), "keys", (near_rows, near_rows), key_grad
    )
    their_keys = swap(partner_keys)

    flat = jax.ShapeDtypeStruct((features, cols), jnp.float32)
    flat_half = jax.ShapeDtypeStruct((features, cols), jnp.bfloat16)
    high, low = cosine_parts()
    forward = jnp.asarray(np.concatenate([high, high, low], axis=1))
    backward = jnp.asarray(np.concatenate([high.T, high.T, low.T], axis=1))
    height = features // ROW_GROUPS
    lines = np.arange(cols)
    base = SPAN * (lines // (2 * block_ids.shape[3])) + lines % 2
    base = jnp.asarray(np.repeat(base[:, None], cols, axis=1).astype(np.float32))
    picks_shape = (2 * ROW_GROUPS * cols, height)
    mask, picks, numbers = call(
        routes_kernel,
        "routes",
        (
            flat_half,
            jax.ShapeDtypeStruct(picks_shape, jnp.bfloat16),
            jax.ShapeDtypeStruct((ROW_GROUPS * cols, cols), jnp.bfloat16),
        ),
        ids,
        counts,
        base,
        places=[SMEM, SMEM, VMEM],
    )

    most = block_ids.shape[3]
    span = lines // (2 * most)
    each = features // SPAN // ROW_GROUPS
    span_table = np.concatenate(
        [(span[:, None] + g * each == lines) & (span[:, None] < each) for g in range(ROW_GROUPS)]
    )
    slot_table = np.where(span < each, lines % (2 * most) // 2, most)
    slot_table = np.repeat(slot_table[:, None], cols, axis=1)
    far_whole, far_sent = call(
        far_kernel,
        "far",
        (flat_half, jax.ShapeDtypeStruct((ROW_GROUPS * cols, cols), jnp.bfloat16)),
        far_keys[2 * tokens :],
        counts,
        jnp.asarray(span_table.astype(np.float32).astype(ml_dtypes.bfloat16)),
        jnp.asarray(slot_table.astype(np.float32)),
        base,
        far_part,
        far_other,
        forward,
        places=[VMEM, SMEM] + [VMEM] * 6,
        scratch=(
            pltpu.VMEM(picks_shape, jnp.bfloat16),
            pltpu.VMEM((features, cols), jnp.bfloat16),
        ),
    )
    far_sent = along(far_sent, FAR)

    keys = jnp.concatenate([own_keys, their_keys], axis=1)
    keys = lax.optimization_barrier(keys.reshape(len(NEAR), tokens, 2 * cols))
    first, second = lax.optimization_barrier((first, second))
    near = gram(activations, keys[0]) + gram(first, keys[1]) + gram(second, keys[2])
    other, far_whole = lax.optimization_barrier(
        (near[:, cols:].astype(jnp.bfloat16), far_whole)
    )
    other, far_whole = swap(other), along(far_whole, FAR)
    part = near[:, :cols] + 0.999 * momentum[0]

    order = np.concatenate([np.arange(0, SPAN, 2), np.arange(1, SPAN, 2)])
    both_high, both_low = (np.kron(np.eye(2, dtype=p.dtype), p[order]) for p in (high, low))
    backward_pair = jnp.asarray(np.concatenate([both_high, both_high, both_low], axis=0))

    message = jax.ShapeDtypeStruct((ROW_GROUPS * cols, cols), jnp.bfloat16)
    advanced, sent = call(
        spectrum_kernel,
        "spectrum",
        (flat, message),
        part,
        other,
        far_sent,
        picks,
        numbers,
        forward,
        scratch=(pltpu.VMEM((features, cols), jnp.bfloat16),),
    )

    def exchange(x):
        return lax.all_to_all(
            x.reshape(replicas, OWN_COLS, x.shape[1]), "dp", 0, 0, tiled=True
        ).reshape(x.shape)

    pieces = exchange(sent)
    unpack = np.concatenate(
        [
            np.kron(np.eye(cols // OWN_COLS), np.outer(np.eye(OWN_COLS)[c], np.ones(OWN_COLS)))
            for c in range(OWN_COLS)
        ],
        axis=1,
    )
    (totals,) = call(
        total_kernel,
        "total",
        (jax.ShapeDtypeStruct((replicas * OWN_COLS, height), jnp.bfloat16),),
        pieces,
        jnp.asarray(unpack.astype(ml_dtypes.bfloat16)),
        backward_pair,
        scratch=(pltpu.VMEM((height, replicas * OWN_COLS), jnp.bfloat16),),
    )
    totals, far_whole = lax.optimization_barrier((totals, far_whole))
    (kept,) = call(kept_kernel, "kept", (flat,), advanced, far_whole, mask, forward, backward)
    (update,) = call(turn_kernel, "turn", (flat_half,), exchange(totals))
    return kept[None], update


def solution(mesh):
    in_specs = (
        P(("dp", "tensor"), None),
        P("dp", "tensor"),
        P("dp", None, "tensor"),
        P("dp", None, "tensor", None),
        P("dp"),
    )
    out_specs = (P("dp", None, "tensor"), P(None, "tensor"))
    body = functools.partial(shards, replicas=mesh.shape["dp"], group=mesh.shape["tensor"])
    return jax.shard_map(body, mesh=mesh, in_specs=in_specs, out_specs=out_specs, check_vma=False)
```

```python
import functools

import jax
import jax.numpy as jnp
import ml_dtypes
import numpy as np
from jax import lax
from jax.experimental import pallas as pl
from jax.experimental.pallas import tpu as pltpu
from jax.sharding import PartitionSpec as P

BLK = 32
SPAN = 64
WIDE = 4
ROW_GROUPS = 4
OWN_COLS = 8
NEAR = (0, 3, 1)
FAR = 2


def cosine_parts():
    n = np.arange(SPAN, dtype=np.float64)
    table = np.cos(np.pi * (2.0 * n[None, :] + 1.0) * n[:, None] / 128.0) * np.sqrt(2.0 / SPAN)
    table[0] *= np.sqrt(0.5)
    high = table.astype(ml_dtypes.bfloat16)
    low = (table - high.astype(np.float64)).astype(ml_dtypes.bfloat16)
    return high, low


def split(x):
    high = x.astype(jnp.bfloat16)
    return high, (x - high.astype(jnp.float32)).astype(jnp.bfloat16)


def spans_of(ref, i, count):
    first = i * count * SPAN
    return [ref[first + s * SPAN : first + (s + 1) * SPAN, :] for s in range(count)]


def beside(parts):
    return jnp.concatenate(parts, axis=1)


def product(table, parts):
    return jnp.dot(table[...], jnp.concatenate(parts, axis=0), preferred_element_type=jnp.float32)


def put(ref, i, count, value):
    cols = ref.shape[1]
    for s in range(count):
        first = (i * count + s) * SPAN
        ref[first : first + SPAN, :] = value[:, s * cols : (s + 1) * cols].astype(ref.dtype)


def far_keys_kernel(tokens, keys, ids, far, numbers, done):
    chip = lax.shift_right_logical(lax.axis_index("tensor"), 1)
    first = 2 * lax.bitwise_xor(chip, FAR) * tokens
    rows = pltpu.make_async_copy(
        keys.at[pl.ds(pl.multiple_of(first, 16), 2 * tokens)],
        far.at[pl.ds(0, 2 * tokens)],
        done.at[0],
    )
    listed = pltpu.make_async_copy(ids, numbers, done.at[1])
    rows.start()
    listed.start()
    listed.wait()
    most, halves, spans = ids.shape
    lines = [numbers[k].astype(jnp.float32) for k in range(most)]
    lines.append(jnp.zeros((16 - most * halves, spans), jnp.float32))
    lines = jnp.concatenate(lines, axis=0)
    lines = jnp.concatenate([lines, jnp.zeros((16, far.shape[1] - spans), jnp.float32)], axis=1)
    far[2 * tokens :, :] = lines.astype(far.dtype)
    rows.wait()


def keys_kernel(tokens, keys, own, partner):
    spot = lax.axis_index("tensor")
    chip, core = lax.shift_right_logical(spot, 1), lax.bitwise_and(spot, 1)

    def block(step, which):
        first = (2 * lax.bitwise_xor(chip, step) + which) * tokens
        return keys[pl.ds(pl.multiple_of(first, 16), tokens), :]

    for place, step in enumerate(NEAR):
        here = slice(place * tokens, (place + 1) * tokens)
        own[here, :] = block(step, core)
        partner[here, :] = block(step, 1 - core)


def pair_kernel(tokens, far, mine, theirs):
    core = lax.bitwise_and(lax.axis_index("tensor"), 1)
    mine[...] = far[pl.ds(pl.multiple_of(core * tokens, 16), tokens), :]
    theirs[...] = far[pl.ds(pl.multiple_of((1 - core) * tokens, 16), tokens), :]


def routes_kernel(ids, count, base, mask, picks, numbers):
    cols = mask.shape[1]
    spans = mask.shape[0] // SPAN
    most = ids.shape[0]
    each = spans // ROW_GROUPS

    def number(a, b, k):
        return jnp.where(k < count[0], ids[k, b, a], -1)

    block = lax.shift_right_logical(lax.broadcasted_iota(jnp.int32, (SPAN, cols), 0), 1)
    first = lax.broadcasted_iota(jnp.int32, (SPAN, cols), 1) < SPAN

    def body(a, _):
        hit = jnp.zeros((SPAN, cols), jnp.bool_)
        for k in range(most):
            hit = hit | (jnp.where(first, number(a, 0, k), number(a, 1, k)) == block)
        rows = pl.ds(pl.multiple_of(a * SPAN, SPAN), SPAN)
        mask[rows, :] = hit.astype(jnp.float32).astype(mask.dtype)
        return 0

    lax.fori_loop(0, spans, body, 0)

    lane = lax.broadcasted_iota(jnp.int32, (SPAN, cols), 1)
    square = (cols, cols)
    column = lax.broadcasted_iota(jnp.int32, square, 1)
    slot = lax.shift_right_logical(lax.broadcasted_iota(jnp.int32, square, 0), 1)
    double = (column == slot).astype(jnp.float32).astype(jnp.bfloat16)
    place = column.astype(jnp.float32)
    row = lax.broadcasted_iota(jnp.int32, square, 0)
    spread = lax.shift_right_logical(column, 3) == (row & (OWN_COLS - 1))
    gather = (column == (row & (OWN_COLS - 1)) + cols - OWN_COLS).astype(jnp.float32)
    gather = gather.astype(jnp.bfloat16)
    for g in range(ROW_GROUPS):
        halves = []
        for b in range(2):
            line = jnp.full((SPAN, cols), -1, jnp.int32)
            for a in range(each):
                for k in range(most):
                    line = jnp.where(lane == a * most + k, number(g * each + a, b, k), line)
            halves.append(line)
        tile = jnp.concatenate(halves, axis=0).astype(jnp.float32)
        packed = jnp.dot(
            jnp.where(spread, tile, 0.0).astype(jnp.bfloat16),
            gather,
            preferred_element_type=jnp.float32,
        )
        numbers[g * cols : (g + 1) * cols, :] = packed.astype(numbers.dtype)
        twice = jnp.dot(
            double, tile.T.astype(jnp.bfloat16), preferred_element_type=jnp.float32
        )
        for b in range(2):
            own = jnp.broadcast_to(twice[:, b * SPAN : b * SPAN + 1], square)
            target = jnp.where(own < 0.0, -1.0, base[...] + 2.0 * own)
            for i in range(picks.shape[1] // cols):
                picks[(2 * g + b) * cols : (2 * g + b + 1) * cols, i * cols : (i + 1) * cols] = (
                    (target == place + float(i * cols)).astype(jnp.float32).astype(picks.dtype)
                )


def chosen_rows(x, mask, forward, i):
    high, low = split(x)
    keep = beside(spans_of(mask, i, WIDE)).astype(jnp.float32)
    return product(forward, [high, low, high]) * keep


def chosen(picks, rows, group, first):
    cols = rows.shape[1]
    height = picks.shape[1]
    band = rows[group * height : (group + 1) * height, :]
    one, two = (
        jnp.dot(
            picks[(2 * group + b) * cols : (2 * group + b + 1) * cols, :],
            band,
            preferred_element_type=jnp.float32,
        )
        for b in range(2)
    )
    return jnp.where(first, one, two)


def left_half(cols):
    return lax.broadcasted_iota(jnp.int32, (cols, cols), 1) < SPAN


def far_kernel(
    numbers, count, spans, slots, base, part, other, forward, whole, sent, picks, rows
):
    cols = part.shape[1]
    height = picks.shape[1]
    square = (cols, cols)
    known = numbers[...].astype(jnp.float32)
    known = jnp.concatenate(
        [known, jnp.zeros((cols - known.shape[0], cols), jnp.float32)], axis=0
    ).T.astype(jnp.bfloat16)
    place = lax.broadcasted_iota(jnp.int32, square, 1).astype(jnp.float32)
    ones = jnp.ones(square, jnp.bfloat16)
    slot = slots[...]
    active = slot < count[0].astype(jnp.float32)
    for g in range(ROW_GROUPS):
        by_span = jnp.dot(
            spans[g * cols : (g + 1) * cols, :], known, preferred_element_type=jnp.float32
        )
        for b in range(2):
            single = jnp.where(place == 2.0 * slot + float(b), by_span, 0.0)
            own = jnp.dot(
                single.astype(jnp.bfloat16), ones, preferred_element_type=jnp.float32
            )
            target = jnp.where(active, base[...] + 2.0 * own, -1.0)
            for i in range(height // cols):
                picks[(2 * g + b) * cols : (2 * g + b + 1) * cols, i * cols : (i + 1) * cols] = (
                    (target == place + float(i * cols)).astype(jnp.float32).astype(picks.dtype)
                )
    for i in range(part.shape[0] // (SPAN * WIDE)):
        x = beside(
            [
                p + o.astype(jnp.float32)
                for p, o in zip(spans_of(part, i, WIDE), spans_of(other, i, WIDE))
            ]
        )
        put(whole, i, WIDE, x)
        high, low = split(x)
        put(rows, i, WIDE, product(forward, [high, low, high]))
    first = left_half(cols)
    for g in range(ROW_GROUPS):
        sent[g * cols : (g + 1) * cols, :] = chosen(picks, rows, g, first).astype(sent.dtype)


def spectrum_kernel(part, other, far, picks, numbers, forward, advanced, sent, rows):
    for i in range(part.shape[0] // (SPAN * WIDE)):
        x = beside(
            [
                p + o.astype(jnp.float32)
                for p, o in zip(spans_of(part, i, WIDE), spans_of(other, i, WIDE))
            ]
        )
        put(advanced, i, WIDE, x)
        high, low = split(x)
        put(rows, i, WIDE, product(forward, [high, low, high]))
    cols = part.shape[1]
    first = left_half(cols)
    for g in range(ROW_GROUPS):
        message = slice(g * cols, (g + 1) * cols)
        total = chosen(picks, rows, g, first) + far[message, :].astype(jnp.float32)
        sent[message, :] = (total.T + numbers[message, :].astype(jnp.float32)).astype(sent.dtype)


def kept_kernel(advanced, far, mask, forward, backward, kept):
    for i in range(kept.shape[0] // (SPAN * WIDE)):
        x = beside(
            [
                n + f.astype(jnp.float32)
                for n, f in zip(spans_of(advanced, i, WIDE), spans_of(far, i, WIDE))
            ]
        )
        high, low = split(chosen_rows(x, mask, forward, i))
        put(kept, i, WIDE, x - product(backward, [high, low, high]))


def total_kernel(pieces, unpack, backward, totals, placed):
    wide = pieces.shape[1]
    spans = totals.shape[1] // SPAN
    lane = lax.broadcasted_iota(jnp.int32, (BLK, wide), 0).astype(jnp.float32)
    lane = lane.astype(placed.dtype)
    for t in range(pieces.shape[0] // wide):
        values = pieces[t * wide : (t + 1) * wide, :].astype(jnp.float32).T.astype(placed.dtype)
        numbers = jnp.dot(
            values[wide - OWN_COLS :, :],
            unpack[...],
            preferred_element_type=jnp.float32,
        ).astype(placed.dtype)
        most = wide // (2 * spans)
        for a in range(spans):
            upper = jnp.zeros((BLK, wide), placed.dtype)
            lower = upper
            for k in range(most):
                at = a * most + k
                down, across = at % OWN_COLS, at // OWN_COLS * wide
                here = numbers[down : down + 1, across : across + wide] == lane
                upper = jnp.where(here, values[2 * at : 2 * at + 1, :], upper)
                lower = jnp.where(here, values[2 * at + 1 : 2 * at + 2, :], lower)
            across = slice(t * wide, (t + 1) * wide)
            placed[a * SPAN : a * SPAN + BLK, across] = upper
            placed[a * SPAN + BLK : (a + 1) * SPAN, across] = lower
    shape = (2 * OWN_COLS, placed.shape[1])
    column = lax.broadcasted_iota(jnp.int32, shape, 1) & (OWN_COLS - 1)
    row = lax.broadcasted_iota(jnp.int32, shape, 0) & (OWN_COLS - 1)
    total = lax.dot_general(
        (column == row).astype(jnp.float32).astype(placed.dtype),
        placed[...],
        (((1,), (1,)), ((), ())),
        preferred_element_type=jnp.float32,
    )
    pair = 2 * SPAN
    for i in range(totals.shape[1] // pair):
        high, low = split(total[:, i * pair : (i + 1) * pair])
        done = jnp.dot(
            jnp.concatenate([high, low, high], axis=1),
            backward[...],
            preferred_element_type=jnp.float32,
        ).astype(totals.dtype)
        for r in range(totals.shape[0] // shape[0]):
            totals[r * shape[0] : (r + 1) * shape[0], i * pair : (i + 1) * pair] = done


def turn_kernel(turned, update):
    cols, height = update.shape[1], turned.shape[1]
    for g in range(ROW_GROUPS):
        for i in range(height // cols):
            rows = g * height + i * cols
            block = turned[g * cols : (g + 1) * cols, i * cols : (i + 1) * cols]
            update[rows : rows + cols, :] = block.astype(jnp.float32).T.astype(update.dtype)


def gram(a, k):
    return lax.dot_general(a, k, (((0,), (0,)), ((), ())), preferred_element_type=jnp.float32)


VMEM, SMEM, HBM = (
    pl.BlockSpec(memory_space=space) for space in (pltpu.VMEM, pltpu.SMEM, pltpu.HBM)
)


def call(kernel, name, outs, *args, places=None, scratch=()):
    return pl.pallas_call(
        kernel,
        out_shape=outs,
        in_specs=places or [VMEM] * len(args),
        out_specs=(VMEM,) * len(outs),
        scratch_shapes=scratch,
        compiler_params=pltpu.CompilerParams(vmem_limit_bytes=10 << 20),
        cost_estimate=pl.CostEstimate(flops=0, bytes_accessed=0, transcendentals=0),
        name=name,
    )(*args)


def shards(activations, key_grad, momentum, block_ids, counts, *, replicas, group):
    tokens, features = activations.shape
    cols = key_grad.shape[1]

    def along(x, step):
        return lax.ppermute(x, "tensor", [(i, i ^ (2 * step)) for i in range(group)])

    def swap(x):
        return lax.ppermute(x, "tensor", [(i, i ^ 1) for i in range(group)])

    near_rows = jax.ShapeDtypeStruct((len(NEAR) * tokens, cols), jnp.bfloat16)
    far_rows = jax.ShapeDtypeStruct((2 * tokens + 16, cols), jnp.bfloat16)
    ids = jnp.transpose(block_ids[0], (2, 1, 0))
    (far_keys,) = call(
        functools.partial(far_keys_kernel, tokens),
        "far_keys",
        (far_rows,),
        pltpu.with_memory_space_constraint(key_grad, pltpu.HBM),
        pltpu.with_memory_space_constraint(ids, pltpu.HBM),
        places=[HBM, HBM],
        scratch=(pltpu.VMEM(ids.shape, jnp.int32), pltpu.SemaphoreType.DMA((2,))),
    )
    activations, key_grad, far_keys = lax.optimization_barrier(
        (activations, key_grad, far_keys)
    )
    far_keys = along(far_keys, FAR)
    first, second = (along(activations, step) for step in NEAR[1:])

    block_rows = jax.ShapeDtypeStruct((tokens, cols), jnp.bfloat16)
    far_own, far_theirs = call(
        functools.partial(pair_kernel, tokens), "pair", (block_rows, block_rows), far_keys
    )
    far_theirs = swap(far_theirs)
    far_other = swap(gram(activations, far_theirs).astype(jnp.bfloat16))
    far_part = gram(activations, far_own)
    own_keys, partner_keys = call(
        functools.partial(keys_kernel, tokens), "keys", (near_rows, near_rows), key_grad
    )
    their_keys = swap(partner_keys)

    flat = jax.ShapeDtypeStruct((features, cols), jnp.float32)
    flat_half = jax.ShapeDtypeStruct((features, cols), jnp.bfloat16)
    high, low = cosine_parts()
    forward = jnp.asarray(np.concatenate([high, high, low], axis=1))
    backward = jnp.asarray(np.concatenate([high.T, high.T, low.T], axis=1))
    height = features // ROW_GROUPS
    lines = np.arange(cols)
    base = SPAN * (lines // (2 * block_ids.shape[3])) + lines % 2
    base = jnp.asarray(np.repeat(base[:, None], cols, axis=1).astype(np.float32))
    picks_shape = (2 * ROW_GROUPS * cols, height)
    mask, picks, numbers = call(
        routes_kernel,
        "routes",
        (
            flat_half,
            jax.ShapeDtypeStruct(picks_shape, jnp.bfloat16),
            jax.ShapeDtypeStruct((ROW_GROUPS * cols, cols), jnp.bfloat16),
        ),
        ids,
        counts,
        base,
        places=[SMEM, SMEM, VMEM],
    )

    most = block_ids.shape[3]
    span = lines // (2 * most)
    each = features // SPAN // ROW_GROUPS
    span_table = np.concatenate(
        [(span[:, None] + g * each == lines) & (span[:, None] < each) for g in range(ROW_GROUPS)]
    )
    slot_table = np.where(span < each, lines % (2 * most) // 2, most)
    slot_table = np.repeat(slot_table[:, None], cols, axis=1)
    far_whole, far_sent = call(
        far_kernel,
        "far",
        (flat_half, jax.ShapeDtypeStruct((ROW_GROUPS * cols, cols), jnp.bfloat16)),
        far_keys[2 * tokens :],
        counts,
        jnp.asarray(span_table.astype(np.float32).astype(ml_dtypes.bfloat16)),
        jnp.asarray(slot_table.astype(np.float32)),
        base,
        far_part,
        far_other,
        forward,
        places=[VMEM, SMEM] + [VMEM] * 6,
        scratch=(
            pltpu.VMEM(picks_shape, jnp.bfloat16),
            pltpu.VMEM((features, cols), jnp.bfloat16),
        ),
    )
    far_sent = along(far_sent, FAR)

    keys = jnp.concatenate([own_keys, their_keys], axis=1)
    keys = lax.optimization_barrier(keys.reshape(len(NEAR), tokens, 2 * cols))
    first, second = lax.optimization_barrier((first, second))
    near = gram(activations, keys[0]) + gram(first, keys[1]) + gram(second, keys[2])
    other, far_whole = lax.optimization_barrier(
        (near[:, cols:].astype(jnp.bfloat16), far_whole)
    )
    other, far_whole = swap(other), along(far_whole, FAR)
    part = near[:, :cols] + 0.999 * momentum[0]

    order = np.concatenate([np.arange(0, SPAN, 2), np.arange(1, SPAN, 2)])
    both_high, both_low = (np.kron(np.eye(2, dtype=p.dtype), p[order]) for p in (high, low))
    backward_pair = jnp.asarray(np.concatenate([both_high, both_high, both_low], axis=0))

    message = jax.ShapeDtypeStruct((ROW_GROUPS * cols, cols), jnp.bfloat16)
    advanced, sent = call(
        spectrum_kernel,
        "spectrum",
        (flat, message),
        part,
        other,
        far_sent,
        picks,
        numbers,
        forward,
        scratch=(pltpu.VMEM((features, cols), jnp.bfloat16),),
    )

    def exchange(x):
        return lax.all_to_all(
            x.reshape(replicas, OWN_COLS, x.shape[1]), "dp", 0, 0, tiled=True
        ).reshape(x.shape)

    pieces = exchange(sent)
    unpack = np.concatenate(
        [
            np.kron(np.eye(cols // OWN_COLS), np.outer(np.eye(OWN_COLS)[c], np.ones(OWN_COLS)))
            for c in range(OWN_COLS)
        ],
        axis=1,
    )
    (totals,) = call(
        total_kernel,
        "total",
        (jax.ShapeDtypeStruct((replicas * OWN_COLS, height), jnp.bfloat16),),
        pieces,
        jnp.asarray(unpack.astype(ml_dtypes.bfloat16)),
        backward_pair,
        scratch=(pltpu.VMEM((height, replicas * OWN_COLS), jnp.bfloat16),),
    )
    totals, far_whole = lax.optimization_barrier((totals, far_whole))
    (kept,) = call(kept_kernel, "kept", (flat,), advanced, far_whole, mask, forward, backward)
    (update,) = call(turn_kernel, "turn", (flat_half,), exchange(totals))
    return kept[None], update


def solution(mesh):
    in_specs = (
        P(("dp", "tensor"), None),
        P("dp", "tensor"),
        P("dp", None, "tensor"),
        P("dp", None, "tensor", None),
        P("dp"),
    )
    out_specs = (P("dp", None, "tensor"), P(None, "tensor"))
    body = functools.partial(shards, replicas=mesh.shape["dp"], group=mesh.shape["tensor"])
    return jax.shard_map(body, mesh=mesh, in_specs=in_specs, out_specs=out_specs, check_vma=False)
```

```python
import functools

import jax
import jax.numpy as jnp
import ml_dtypes
import numpy as np
from jax import lax
from jax.experimental import pallas as pl
from jax.experimental.pallas import tpu as pltpu
from jax.sharding import PartitionSpec as P

BLK = 32
SPAN = 64
WIDE = 4
ROW_GROUPS = 4
OWN_COLS = 8
NEAR = (0, 3, 1)
FAR = 2


def cosine_parts():
    n = np.arange(SPAN, dtype=np.float64)
    table = np.cos(np.pi * (2.0 * n[None, :] + 1.0) * n[:, None] / 128.0) * np.sqrt(2.0 / SPAN)
    table[0] *= np.sqrt(0.5)
    high = table.astype(ml_dtypes.bfloat16)
    low = (table - high.astype(np.float64)).astype(ml_dtypes.bfloat16)
    return high, low


def split(x):
    high = x.astype(jnp.bfloat16)
    return high, (x - high.astype(jnp.float32)).astype(jnp.bfloat16)


def spans_of(ref, i, count):
    first = i * count * SPAN
    return [ref[first + s * SPAN : first + (s + 1) * SPAN, :] for s in range(count)]


def beside(parts):
    return jnp.concatenate(parts, axis=1)


def product(table, parts):
    return jnp.dot(table[...], jnp.concatenate(parts, axis=0), preferred_element_type=jnp.float32)


def put(ref, i, count, value):
    cols = ref.shape[1]
    for s in range(count):
        first = (i * count + s) * SPAN
        ref[first : first + SPAN, :] = value[:, s * cols : (s + 1) * cols].astype(ref.dtype)


def far_keys_kernel(tokens, keys, ids, far, numbers, done):
    chip = lax.shift_right_logical(lax.axis_index("tensor"), 1)
    first = 2 * lax.bitwise_xor(chip, FAR) * tokens
    rows = pltpu.make_async_copy(
        keys.at[pl.ds(pl.multiple_of(first, 16), 2 * tokens)],
        far.at[pl.ds(0, 2 * tokens)],
        done.at[0],
    )
    listed = pltpu.make_async_copy(ids, numbers, done.at[1])
    rows.start()
    listed.start()
    listed.wait()
    most, halves, spans = ids.shape
    lines = [numbers[k].astype(jnp.float32) for k in range(most)]
    lines.append(jnp.zeros((16 - most * halves, spans), jnp.float32))
    lines = jnp.concatenate(lines, axis=0)
    lines = jnp.concatenate([lines, jnp.zeros((16, far.shape[1] - spans), jnp.float32)], axis=1)
    far[2 * tokens :, :] = lines.astype(far.dtype)
    rows.wait()


def keys_kernel(tokens, keys, own, partner):
    spot = lax.axis_index("tensor")
    chip, core = lax.shift_right_logical(spot, 1), lax.bitwise_and(spot, 1)

    def block(step, which):
        first = (2 * lax.bitwise_xor(chip, step) + which) * tokens
        return keys[pl.ds(pl.multiple_of(first, 16), tokens), :]

    for place, step in enumerate(NEAR):
        here = slice(place * tokens, (place + 1) * tokens)
        own[here, :] = block(step, core)
        partner[here, :] = block(step, 1 - core)


def pair_kernel(tokens, far, mine, theirs):
    core = lax.bitwise_and(lax.axis_index("tensor"), 1)
    mine[...] = far[pl.ds(pl.multiple_of(core * tokens, 16), tokens), :]
    theirs[...] = far[pl.ds(pl.multiple_of((1 - core) * tokens, 16), tokens), :]


def routes_kernel(ids, count, base, mask, picks, numbers):
    cols = mask.shape[1]
    spans = mask.shape[0] // SPAN
    most = ids.shape[0]
    each = spans // ROW_GROUPS

    def number(a, b, k):
        return jnp.where(k < count[0], ids[k, b, a], -1)

    block = lax.shift_right_logical(lax.broadcasted_iota(jnp.int32, (SPAN, cols), 0), 1)
    first = lax.broadcasted_iota(jnp.int32, (SPAN, cols), 1) < SPAN

    def body(a, _):
        hit = jnp.zeros((SPAN, cols), jnp.bool_)
        for k in range(most):
            hit = hit | (jnp.where(first, number(a, 0, k), number(a, 1, k)) == block)
        rows = pl.ds(pl.multiple_of(a * SPAN, SPAN), SPAN)
        mask[rows, :] = hit.astype(jnp.float32).astype(mask.dtype)
        return 0

    lax.fori_loop(0, spans, body, 0)

    lane = lax.broadcasted_iota(jnp.int32, (SPAN, cols), 1)
    square = (cols, cols)
    column = lax.broadcasted_iota(jnp.int32, square, 1)
    slot = lax.shift_right_logical(lax.broadcasted_iota(jnp.int32, square, 0), 1)
    double = (column == slot).astype(jnp.float32).astype(jnp.bfloat16)
    place = column.astype(jnp.float32)
    row = lax.broadcasted_iota(jnp.int32, square, 0)
    spread = lax.shift_right_logical(column, 3) == (row & (OWN_COLS - 1))
    gather = (column == (row & (OWN_COLS - 1)) + cols - OWN_COLS).astype(jnp.float32)
    gather = gather.astype(jnp.bfloat16)
    for g in range(ROW_GROUPS):
        halves = []
        for b in range(2):
            line = jnp.full((SPAN, cols), -1, jnp.int32)
            for a in range(each):
                for k in range(most):
                    line = jnp.where(lane == a * most + k, number(g * each + a, b, k), line)
            halves.append(line)
        tile = jnp.concatenate(halves, axis=0).astype(jnp.float32)
        packed = jnp.dot(
            jnp.where(spread, tile, 0.0).astype(jnp.bfloat16),
            gather,
            preferred_element_type=jnp.float32,
        )
        numbers[g * cols : (g + 1) * cols, :] = packed.astype(numbers.dtype)
        twice = jnp.dot(
            double, tile.T.astype(jnp.bfloat16), preferred_element_type=jnp.float32
        )
        for b in range(2):
            own = jnp.broadcast_to(twice[:, b * SPAN : b * SPAN + 1], square)
            target = jnp.where(own < 0.0, -1.0, base[...] + 2.0 * own)
            for i in range(picks.shape[1] // cols):
                picks[(2 * g + b) * cols : (2 * g + b + 1) * cols, i * cols : (i + 1) * cols] = (
                    (target == place + float(i * cols)).astype(jnp.float32).astype(picks.dtype)
                )


def chosen_rows(x, mask, forward, i):
    high, low = split(x)
    keep = beside(spans_of(mask, i, WIDE)).astype(jnp.float32)
    return product(forward, [high, low, high]) * keep


def chosen(picks, rows, group, first):
    cols = rows.shape[1]
    height = picks.shape[1]
    band = rows[group * height : (group + 1) * height, :]
    one, two = (
        jnp.dot(
            picks[(2 * group + b) * cols : (2 * group + b + 1) * cols, :],
            band,
            preferred_element_type=jnp.float32,
        )
        for b in range(2)
    )
    return jnp.where(first, one, two)


def left_half(cols):
    return lax.broadcasted_iota(jnp.int32, (cols, cols), 1) < SPAN


def far_kernel(
    numbers, count, spans, slots, base, part, other, forward, whole, sent, picks, rows
):
    cols = part.shape[1]
    height = picks.shape[1]
    square = (cols, cols)
    known = numbers[...].astype(jnp.float32)
    known = jnp.concatenate(
        [known, jnp.zeros((cols - known.shape[0], cols), jnp.float32)], axis=0
    ).T.astype(jnp.bfloat16)
    place = lax.broadcasted_iota(jnp.int32, square, 1).astype(jnp.float32)
    ones = jnp.ones(square, jnp.bfloat16)
    slot = slots[...]
    active = slot < count[0].astype(jnp.float32)
    for g in range(ROW_GROUPS):
        by_span = jnp.dot(
            spans[g * cols : (g + 1) * cols, :], known, preferred_element_type=jnp.float32
        )
        for b in range(2):
            single = jnp.where(place == 2.0 * slot + float(b), by_span, 0.0)
            own = jnp.dot(
                single.astype(jnp.bfloat16), ones, preferred_element_type=jnp.float32
            )
            target = jnp.where(active, base[...] + 2.0 * own, -1.0)
            for i in range(height // cols):
                picks[(2 * g + b) * cols : (2 * g + b + 1) * cols, i * cols : (i + 1) * cols] = (
                    (target == place + float(i * cols)).astype(jnp.float32).astype(picks.dtype)
                )
    for i in range(part.shape[0] // (SPAN * WIDE)):
        x = beside(
            [
                p + o.astype(jnp.float32)
                for p, o in zip(spans_of(part, i, WIDE), spans_of(other, i, WIDE))
            ]
        )
        put(whole, i, WIDE, x)
        high, low = split(x)
        put(rows, i, WIDE, product(forward, [high, low, high]))
    first = left_half(cols)
    for g in range(ROW_GROUPS):
        sent[g * cols : (g + 1) * cols, :] = chosen(picks, rows, g, first).astype(sent.dtype)


def spectrum_kernel(part, other, far, picks, numbers, forward, advanced, sent, rows):
    for i in range(part.shape[0] // (SPAN * WIDE)):
        x = beside(
            [
                p + o.astype(jnp.float32)
                for p, o in zip(spans_of(part, i, WIDE), spans_of(other, i, WIDE))
            ]
        )
        put(advanced, i, WIDE, x)
        high, low = split(x)
        put(rows, i, WIDE, product(forward, [high, low, high]))
    cols = part.shape[1]
    first = left_half(cols)
    for g in range(ROW_GROUPS):
        message = slice(g * cols, (g + 1) * cols)
        total = chosen(picks, rows, g, first) + far[message, :].astype(jnp.float32)
        sent[message, :] = (total.T + numbers[message, :].astype(jnp.float32)).astype(sent.dtype)


def kept_kernel(advanced, far, mask, forward, backward, kept):
    for i in range(kept.shape[0] // (SPAN * WIDE)):
        x = beside(
            [
                n + f.astype(jnp.float32)
                for n, f in zip(spans_of(advanced, i, WIDE), spans_of(far, i, WIDE))
            ]
        )
        high, low = split(chosen_rows(x, mask, forward, i))
        put(kept, i, WIDE, x - product(backward, [high, low, high]))


def total_kernel(pieces, unpack, backward, totals, placed):
    wide = pieces.shape[1]
    spans = totals.shape[1] // SPAN
    lane = lax.broadcasted_iota(jnp.int32, (BLK, wide), 0).astype(jnp.float32)
    lane = lane.astype(placed.dtype)
    for t in range(pieces.shape[0] // wide):
        values = pieces[t * wide : (t + 1) * wide, :].astype(jnp.float32).T.astype(placed.dtype)
        numbers = jnp.dot(
            values[wide - OWN_COLS :, :],
            unpack[...],
            preferred_element_type=jnp.float32,
        ).astype(placed.dtype)
        most = wide // (2 * spans)
        for a in range(spans):
            upper = jnp.zeros((BLK, wide), placed.dtype)
            lower = upper
            for k in range(most):
                at = a * most + k
                down, across = at % OWN_COLS, at // OWN_COLS * wide
                here = numbers[down : down + 1, across : across + wide] == lane
                upper = jnp.where(here, values[2 * at : 2 * at + 1, :], upper)
                lower = jnp.where(here, values[2 * at + 1 : 2 * at + 2, :], lower)
            across = slice(t * wide, (t + 1) * wide)
            placed[a * SPAN : a * SPAN + BLK, across] = upper
            placed[a * SPAN + BLK : (a + 1) * SPAN, across] = lower
    shape = (2 * OWN_COLS, placed.shape[1])
    column = lax.broadcasted_iota(jnp.int32, shape, 1) & (OWN_COLS - 1)
    row = lax.broadcasted_iota(jnp.int32, shape, 0) & (OWN_COLS - 1)
    total = lax.dot_general(
        (column == row).astype(jnp.float32).astype(placed.dtype),
        placed[...],
        (((1,), (1,)), ((), ())),
        preferred_element_type=jnp.float32,
    )
    pair = 2 * SPAN
    for i in range(totals.shape[1] // pair):
        high, low = split(total[:, i * pair : (i + 1) * pair])
        done = jnp.dot(
            jnp.concatenate([high, low, high], axis=1),
            backward[...],
            preferred_element_type=jnp.float32,
        ).astype(totals.dtype)
        for r in range(totals.shape[0] // shape[0]):
            totals[r * shape[0] : (r + 1) * shape[0], i * pair : (i + 1) * pair] = done


def turn_kernel(turned, update):
    cols, height = update.shape[1], turned.shape[1]
    for g in range(ROW_GROUPS):
        for i in range(height // cols):
            rows = g * height + i * cols
            block = turned[g * cols : (g + 1) * cols, i * cols : (i + 1) * cols]
            update[rows : rows + cols, :] = block.astype(jnp.float32).T.astype(update.dtype)


def gram(a, k):
    return lax.dot_general(a, k, (((0,), (0,)), ((), ())), preferred_element_type=jnp.float32)


VMEM, SMEM, HBM = (
    pl.BlockSpec(memory_space=space) for space in (pltpu.VMEM, pltpu.SMEM, pltpu.HBM)
)


def call(kernel, name, outs, *args, places=None, scratch=()):
    return pl.pallas_call(
        kernel,
        out_shape=outs,
        in_specs=places or [VMEM] * len(args),
        out_specs=(VMEM,) * len(outs),
        scratch_shapes=scratch,
        compiler_params=pltpu.CompilerParams(vmem_limit_bytes=10 << 20),
        cost_estimate=pl.CostEstimate(flops=0, bytes_accessed=0, transcendentals=0),
        name=name,
    )(*args)


def shards(activations, key_grad, momentum, block_ids, counts, *, replicas, group):
    tokens, features = activations.shape
    cols = key_grad.shape[1]

    def along(x, step):
        return lax.ppermute(x, "tensor", [(i, i ^ (2 * step)) for i in range(group)])

    def swap(x):
        return lax.ppermute(x, "tensor", [(i, i ^ 1) for i in range(group)])

    near_rows = jax.ShapeDtypeStruct((len(NEAR) * tokens, cols), jnp.bfloat16)
    far_rows = jax.ShapeDtypeStruct((2 * tokens + 16, cols), jnp.bfloat16)
    ids = jnp.transpose(block_ids[0], (2, 1, 0))
    (far_keys,) = call(
        functools.partial(far_keys_kernel, tokens),
        "far_keys",
        (far_rows,),
        pltpu.with_memory_space_constraint(key_grad, pltpu.HBM),
        pltpu.with_memory_space_constraint(ids, pltpu.HBM),
        places=[HBM, HBM],
        scratch=(pltpu.VMEM(ids.shape, jnp.int32), pltpu.SemaphoreType.DMA((2,))),
    )
    activations, key_grad, far_keys = lax.optimization_barrier(
        (activations, key_grad, far_keys)
    )
    far_keys = along(far_keys, FAR)
    first, second = (along(activations, step) for step in NEAR[1:])

    block_rows = jax.ShapeDtypeStruct((tokens, cols), jnp.bfloat16)
    far_own, far_theirs = call(
        functools.partial(pair_kernel, tokens), "pair", (block_rows, block_rows), far_keys
    )
    far_theirs = swap(far_theirs)
    far_other = swap(gram(activations, far_theirs).astype(jnp.bfloat16))
    far_part = gram(activations, far_own)
    own_keys, partner_keys = call(
        functools.partial(keys_kernel, tokens), "keys", (near_rows, near_rows), key_grad
    )
    their_keys = swap(partner_keys)

    flat = jax.ShapeDtypeStruct((features, cols), jnp.float32)
    flat_half = jax.ShapeDtypeStruct((features, cols), jnp.bfloat16)
    high, low = cosine_parts()
    forward = jnp.asarray(np.concatenate([high, high, low], axis=1))
    backward = jnp.asarray(np.concatenate([high.T, high.T, low.T], axis=1))
    height = features // ROW_GROUPS
    lines = np.arange(cols)
    base = SPAN * (lines // (2 * block_ids.shape[3])) + lines % 2
    base = jnp.asarray(np.repeat(base[:, None], cols, axis=1).astype(np.float32))
    picks_shape = (2 * ROW_GROUPS * cols, height)
    mask, picks, numbers = call(
        routes_kernel,
        "routes",
        (
            flat_half,
            jax.ShapeDtypeStruct(picks_shape, jnp.bfloat16),
            jax.ShapeDtypeStruct((ROW_GROUPS * cols, cols), jnp.bfloat16),
        ),
        ids,
        counts,
        base,
        places=[SMEM, SMEM, VMEM],
    )

    most = block_ids.shape[3]
    span = lines // (2 * most)
    each = features // SPAN // ROW_GROUPS
    span_table = np.concatenate(
        [(span[:, None] + g * each == lines) & (span[:, None] < each) for g in range(ROW_GROUPS)]
    )
    slot_table = np.where(span < each, lines % (2 * most) // 2, most)
    slot_table = np.repeat(slot_table[:, None], cols, axis=1)
    far_whole, far_sent = call(
        far_kernel,
        "far",
        (flat_half, jax.ShapeDtypeStruct((ROW_GROUPS * cols, cols), jnp.bfloat16)),
        far_keys[2 * tokens :],
        counts,
        jnp.asarray(span_table.astype(np.float32).astype(ml_dtypes.bfloat16)),
        jnp.asarray(slot_table.astype(np.float32)),
        base,
        far_part,
        far_other,
        forward,
        places=[VMEM, SMEM] + [VMEM] * 6,
        scratch=(
            pltpu.VMEM(picks_shape, jnp.bfloat16),
            pltpu.VMEM((features, cols), jnp.bfloat16),
        ),
    )
    far_sent = along(far_sent, FAR)

    keys = jnp.concatenate([own_keys, their_keys], axis=1)
    keys = lax.optimization_barrier(keys.reshape(len(NEAR), tokens, 2 * cols))
    first, second = lax.optimization_barrier((first, second))
    near = gram(activations, keys[0]) + gram(first, keys[1]) + gram(second, keys[2])
    other = swap(near[:, cols:].astype(jnp.bfloat16))
    part = near[:, :cols] + 0.999 * momentum[0]

    order = np.concatenate([np.arange(0, SPAN, 2), np.arange(1, SPAN, 2)])
    both_high, both_low = (np.kron(np.eye(2, dtype=p.dtype), p[order]) for p in (high, low))
    backward_pair = jnp.asarray(np.concatenate([both_high, both_high, both_low], axis=0))

    message = jax.ShapeDtypeStruct((ROW_GROUPS * cols, cols), jnp.bfloat16)
    advanced, sent = call(
        spectrum_kernel,
        "spectrum",
        (flat, message),
        part,
        other,
        far_sent,
        picks,
        numbers,
        forward,
        scratch=(pltpu.VMEM((features, cols), jnp.bfloat16),),
    )

    def exchange(x):
        return lax.all_to_all(
            x.reshape(replicas, OWN_COLS, x.shape[1]), "dp", 0, 0, tiled=True
        ).reshape(x.shape)

    sent, far_whole = lax.optimization_barrier((sent, far_whole))
    pieces, far_whole = exchange(sent), along(far_whole, FAR)
    unpack = np.concatenate(
        [
            np.kron(np.eye(cols // OWN_COLS), np.outer(np.eye(OWN_COLS)[c], np.ones(OWN_COLS)))
            for c in range(OWN_COLS)
        ],
        axis=1,
    )
    (totals,) = call(
        total_kernel,
        "total",
        (jax.ShapeDtypeStruct((replicas * OWN_COLS, height), jnp.bfloat16),),
        pieces,
        jnp.asarray(unpack.astype(ml_dtypes.bfloat16)),
        backward_pair,
        scratch=(pltpu.VMEM((height, replicas * OWN_COLS), jnp.bfloat16),),
    )
    totals, far_whole = lax.optimization_barrier((totals, far_whole))
    (kept,) = call(kept_kernel, "kept", (flat,), advanced, far_whole, mask, forward, backward)
    (update,) = call(turn_kernel, "turn", (flat_half,), exchange(totals))
    return kept[None], update


def solution(mesh):
    in_specs = (
        P(("dp", "tensor"), None),
        P("dp", "tensor"),
        P("dp", None, "tensor"),
        P("dp", None, "tensor", None),
        P("dp"),
    )
    out_specs = (P("dp", None, "tensor"), P(None, "tensor"))
    body = functools.partial(shards, replicas=mesh.shape["dp"], group=mesh.shape["tensor"])
    return jax.shard_map(body, mesh=mesh, in_specs=in_specs, out_specs=out_specs, check_vma=False)
```

```python
import functools

import jax
import jax.numpy as jnp
import ml_dtypes
import numpy as np
from jax import lax
from jax.experimental import pallas as pl
from jax.experimental.pallas import tpu as pltpu
from jax.sharding import PartitionSpec as P

BLK = 32
SPAN = 64
WIDE = 4
ROW_GROUPS = 4
OWN_COLS = 8
NEAR = (0, 3, 1)
FAR = 2


def cosine_parts():
    n = np.arange(SPAN, dtype=np.float64)
    table = np.cos(np.pi * (2.0 * n[None, :] + 1.0) * n[:, None] / 128.0) * np.sqrt(2.0 / SPAN)
    table[0] *= np.sqrt(0.5)
    high = table.astype(ml_dtypes.bfloat16)
    low = (table - high.astype(np.float64)).astype(ml_dtypes.bfloat16)
    return high, low


def split(x):
    high = x.astype(jnp.bfloat16)
    return high, (x - high.astype(jnp.float32)).astype(jnp.bfloat16)


def spans_of(ref, i, count):
    first = i * count * SPAN
    return [ref[first + s * SPAN : first + (s + 1) * SPAN, :] for s in range(count)]


def beside(parts):
    return jnp.concatenate(parts, axis=1)


def product(table, parts):
    return jnp.dot(table[...], jnp.concatenate(parts, axis=0), preferred_element_type=jnp.float32)


def put(ref, i, count, value):
    cols = ref.shape[1]
    for s in range(count):
        first = (i * count + s) * SPAN
        ref[first : first + SPAN, :] = value[:, s * cols : (s + 1) * cols].astype(ref.dtype)


def far_keys_kernel(tokens, keys, ids, far, numbers, done):
    chip = lax.shift_right_logical(lax.axis_index("tensor"), 1)
    first = 2 * lax.bitwise_xor(chip, FAR) * tokens
    rows = pltpu.make_async_copy(
        keys.at[pl.ds(pl.multiple_of(first, 16), 2 * tokens)],
        far.at[pl.ds(0, 2 * tokens)],
        done.at[0],
    )
    listed = pltpu.make_async_copy(ids, numbers, done.at[1])
    rows.start()
    listed.start()
    listed.wait()
    most, halves, spans = ids.shape
    lines = [numbers[k].astype(jnp.float32) for k in range(most)]
    lines.append(jnp.zeros((16 - most * halves, spans), jnp.float32))
    lines = jnp.concatenate(lines, axis=0)
    lines = jnp.concatenate([lines, jnp.zeros((16, far.shape[1] - spans), jnp.float32)], axis=1)
    far[2 * tokens :, :] = lines.astype(far.dtype)
    rows.wait()


def keys_kernel(tokens, keys, own, partner):
    spot = lax.axis_index("tensor")
    chip, core = lax.shift_right_logical(spot, 1), lax.bitwise_and(spot, 1)

    def block(step, which):
        first = (2 * lax.bitwise_xor(chip, step) + which) * tokens
        return keys[pl.ds(pl.multiple_of(first, 16), tokens), :]

    for place, step in enumerate(NEAR):
        here = slice(place * tokens, (place + 1) * tokens)
        own[here, :] = block(step, core)
        partner[here, :] = block(step, 1 - core)


def pair_kernel(tokens, far, mine, theirs):
    core = lax.bitwise_and(lax.axis_index("tensor"), 1)
    mine[...] = far[pl.ds(pl.multiple_of(core * tokens, 16), tokens), :]
    theirs[...] = far[pl.ds(pl.multiple_of((1 - core) * tokens, 16), tokens), :]


def routes_kernel(ids, count, base, mask, picks, numbers):
    cols = mask.shape[1]
    spans = mask.shape[0] // SPAN
    most = ids.shape[0]
    each = spans // ROW_GROUPS

    def number(a, b, k):
        return jnp.where(k < count[0], ids[k, b, a], -1)

    block = lax.shift_right_logical(lax.broadcasted_iota(jnp.int32, (SPAN, cols), 0), 1)
    first = lax.broadcasted_iota(jnp.int32, (SPAN, cols), 1) < SPAN

    def body(a, _):
        hit = jnp.zeros((SPAN, cols), jnp.bool_)
        for k in range(most):
            hit = hit | (jnp.where(first, number(a, 0, k), number(a, 1, k)) == block)
        rows = pl.ds(pl.multiple_of(a * SPAN, SPAN), SPAN)
        mask[rows, :] = hit.astype(jnp.float32).astype(mask.dtype)
        return 0

    lax.fori_loop(0, spans, body, 0)

    lane = lax.broadcasted_iota(jnp.int32, (SPAN, cols), 1)
    square = (cols, cols)
    column = lax.broadcasted_iota(jnp.int32, square, 1)
    slot = lax.shift_right_logical(lax.broadcasted_iota(jnp.int32, square, 0), 1)
    double = (column == slot).astype(jnp.float32).astype(jnp.bfloat16)
    place = column.astype(jnp.float32)
    row = lax.broadcasted_iota(jnp.int32, square, 0)
    spread = lax.shift_right_logical(column, 3) == (row & (OWN_COLS - 1))
    gather = (column == (row & (OWN_COLS - 1)) + cols - OWN_COLS).astype(jnp.float32)
    gather = gather.astype(jnp.bfloat16)
    for g in range(ROW_GROUPS):
        halves = []
        for b in range(2):
            line = jnp.full((SPAN, cols), -1, jnp.int32)
            for a in range(each):
                for k in range(most):
                    line = jnp.where(lane == a * most + k, number(g * each + a, b, k), line)
            halves.append(line)
        tile = jnp.concatenate(halves, axis=0).astype(jnp.float32)
        packed = jnp.dot(
            jnp.where(spread, tile, 0.0).astype(jnp.bfloat16),
            gather,
            preferred_element_type=jnp.float32,
        )
        numbers[g * cols : (g + 1) * cols, :] = packed.astype(numbers.dtype)
        twice = jnp.dot(
            double, tile.T.astype(jnp.bfloat16), preferred_element_type=jnp.float32
        )
        for b in range(2):
            own = jnp.broadcast_to(twice[:, b * SPAN : b * SPAN + 1], square)
            target = jnp.where(own < 0.0, -1.0, base[...] + 2.0 * own)
            for i in range(picks.shape[1] // cols):
                picks[(2 * g + b) * cols : (2 * g + b + 1) * cols, i * cols : (i + 1) * cols] = (
                    (target == place + float(i * cols)).astype(jnp.float32).astype(picks.dtype)
                )


def chosen_rows(x, mask, forward, i):
    high, low = split(x)
    keep = beside(spans_of(mask, i, WIDE)).astype(jnp.float32)
    return product(forward, [high, low, high]) * keep


def chosen(picks, rows, group, first):
    cols = rows.shape[1]
    height = picks.shape[1]
    band = rows[group * height : (group + 1) * height, :]
    one, two = (
        jnp.dot(
            picks[(2 * group + b) * cols : (2 * group + b + 1) * cols, :],
            band,
            preferred_element_type=jnp.float32,
        )
        for b in range(2)
    )
    return jnp.where(first, one, two)


def left_half(cols):
    return lax.broadcasted_iota(jnp.int32, (cols, cols), 1) < SPAN


def far_kernel(
    numbers, count, spans, slots, base, part, other, forward, whole, sent, picks, rows
):
    cols = part.shape[1]
    height = picks.shape[1]
    square = (cols, cols)
    known = numbers[...].astype(jnp.float32)
    known = jnp.concatenate(
        [known, jnp.zeros((cols - known.shape[0], cols), jnp.float32)], axis=0
    ).T.astype(jnp.bfloat16)
    place = lax.broadcasted_iota(jnp.int32, square, 1).astype(jnp.float32)
    ones = jnp.ones(square, jnp.bfloat16)
    slot = slots[...]
    active = slot < count[0].astype(jnp.float32)
    for g in range(ROW_GROUPS):
        by_span = jnp.dot(
            spans[g * cols : (g + 1) * cols, :], known, preferred_element_type=jnp.float32
        )
        for b in range(2):
            single = jnp.where(place == 2.0 * slot + float(b), by_span, 0.0)
            own = jnp.dot(
                single.astype(jnp.bfloat16), ones, preferred_element_type=jnp.float32
            )
            target = jnp.where(active, base[...] + 2.0 * own, -1.0)
            for i in range(height // cols):
                picks[(2 * g + b) * cols : (2 * g + b + 1) * cols, i * cols : (i + 1) * cols] = (
                    (target == place + float(i * cols)).astype(jnp.float32).astype(picks.dtype)
                )
    for i in range(part.shape[0] // (SPAN * WIDE)):
        x = beside(
            [
                p + o.astype(jnp.float32)
                for p, o in zip(spans_of(part, i, WIDE), spans_of(other, i, WIDE))
            ]
        )
        put(whole, i, WIDE, x)
        high, low = split(x)
        put(rows, i, WIDE, product(forward, [high, low, high]))
    first = left_half(cols)
    for g in range(ROW_GROUPS):
        sent[g * cols : (g + 1) * cols, :] = chosen(picks, rows, g, first).astype(sent.dtype)


def spectrum_kernel(part, other, far, picks, numbers, forward, advanced, sent, rows):
    for i in range(part.shape[0] // (SPAN * WIDE)):
        x = beside(
            [
                p + o.astype(jnp.float32)
                for p, o in zip(spans_of(part, i, WIDE), spans_of(other, i, WIDE))
            ]
        )
        put(advanced, i, WIDE, x)
        high, low = split(x)
        put(rows, i, WIDE, product(forward, [high, low, high]))
    cols = part.shape[1]
    first = left_half(cols)
    for g in range(ROW_GROUPS):
        message = slice(g * cols, (g + 1) * cols)
        total = chosen(picks, rows, g, first) + far[message, :].astype(jnp.float32)
        sent[message, :] = (total.T + numbers[message, :].astype(jnp.float32)).astype(sent.dtype)


def kept_kernel(advanced, far, mask, forward, backward, kept):
    for i in range(kept.shape[0] // (SPAN * WIDE)):
        x = beside(
            [
                n + f.astype(jnp.float32)
                for n, f in zip(spans_of(advanced, i, WIDE), spans_of(far, i, WIDE))
            ]
        )
        high, low = split(chosen_rows(x, mask, forward, i))
        put(kept, i, WIDE, x - product(backward, [high, low, high]))


def total_kernel(pieces, unpack, backward, totals, placed):
    wide = pieces.shape[1]
    spans = totals.shape[1] // SPAN
    lane = lax.broadcasted_iota(jnp.int32, (BLK, wide), 0).astype(jnp.float32)
    lane = lane.astype(placed.dtype)
    for t in range(pieces.shape[0] // wide):
        values = pieces[t * wide : (t + 1) * wide, :].astype(jnp.float32).T.astype(placed.dtype)
        numbers = jnp.dot(
            values[wide - OWN_COLS :, :],
            unpack[...],
            preferred_element_type=jnp.float32,
        ).astype(placed.dtype)
        most = wide // (2 * spans)
        for a in range(spans):
            upper = jnp.zeros((BLK, wide), placed.dtype)
            lower = upper
            for k in range(most):
                at = a * most + k
                down, across = at % OWN_COLS, at // OWN_COLS * wide
                here = numbers[down : down + 1, across : across + wide] == lane
                upper = jnp.where(here, values[2 * at : 2 * at + 1, :], upper)
                lower = jnp.where(here, values[2 * at + 1 : 2 * at + 2, :], lower)
            across = slice(t * wide, (t + 1) * wide)
            placed[a * SPAN : a * SPAN + BLK, across] = upper
            placed[a * SPAN + BLK : (a + 1) * SPAN, across] = lower
    shape = (2 * OWN_COLS, placed.shape[1])
    column = lax.broadcasted_iota(jnp.int32, shape, 1) & (OWN_COLS - 1)
    row = lax.broadcasted_iota(jnp.int32, shape, 0) & (OWN_COLS - 1)
    total = lax.dot_general(
        (column == row).astype(jnp.float32).astype(placed.dtype),
        placed[...],
        (((1,), (1,)), ((), ())),
        preferred_element_type=jnp.float32,
    )
    pair = 2 * SPAN
    for i in range(totals.shape[1] // pair):
        high, low = split(total[:, i * pair : (i + 1) * pair])
        done = jnp.dot(
            jnp.concatenate([high, low, high], axis=1),
            backward[...],
            preferred_element_type=jnp.float32,
        ).astype(totals.dtype)
        for r in range(totals.shape[0] // shape[0]):
            totals[r * shape[0] : (r + 1) * shape[0], i * pair : (i + 1) * pair] = done


def turn_kernel(turned, update):
    cols, height = update.shape[1], turned.shape[1]
    for g in range(ROW_GROUPS):
        for i in range(height // cols):
            rows = g * height + i * cols
            block = turned[g * cols : (g + 1) * cols, i * cols : (i + 1) * cols]
            update[rows : rows + cols, :] = block.T


def gram(a, k):
    return lax.dot_general(a, k, (((0,), (0,)), ((), ())), preferred_element_type=jnp.float32)


VMEM, SMEM, HBM = (
    pl.BlockSpec(memory_space=space) for space in (pltpu.VMEM, pltpu.SMEM, pltpu.HBM)
)


def call(kernel, name, outs, *args, places=None, scratch=()):
    return pl.pallas_call(
        kernel,
        out_shape=outs,
        in_specs=places or [VMEM] * len(args),
        out_specs=(VMEM,) * len(outs),
        scratch_shapes=scratch,
        compiler_params=pltpu.CompilerParams(vmem_limit_bytes=10 << 20),
        cost_estimate=pl.CostEstimate(flops=0, bytes_accessed=0, transcendentals=0),
        name=name,
    )(*args)


def shards(activations, key_grad, momentum, block_ids, counts, *, replicas, group):
    tokens, features = activations.shape
    cols = key_grad.shape[1]

    def along(x, step):
        return lax.ppermute(x, "tensor", [(i, i ^ (2 * step)) for i in range(group)])

    def swap(x):
        return lax.ppermute(x, "tensor", [(i, i ^ 1) for i in range(group)])

    near_rows = jax.ShapeDtypeStruct((len(NEAR) * tokens, cols), jnp.bfloat16)
    far_rows = jax.ShapeDtypeStruct((2 * tokens + 16, cols), jnp.bfloat16)
    ids = jnp.transpose(block_ids[0], (2, 1, 0))
    (far_keys,) = call(
        functools.partial(far_keys_kernel, tokens),
        "far_keys",
        (far_rows,),
        pltpu.with_memory_space_constraint(key_grad, pltpu.HBM),
        pltpu.with_memory_space_constraint(ids, pltpu.HBM),
        places=[HBM, HBM],
        scratch=(pltpu.VMEM(ids.shape, jnp.int32), pltpu.SemaphoreType.DMA((2,))),
    )
    activations, key_grad, far_keys = lax.optimization_barrier(
        (activations, key_grad, far_keys)
    )
    far_keys = along(far_keys, FAR)
    first, second = (along(activations, step) for step in NEAR[1:])

    block_rows = jax.ShapeDtypeStruct((tokens, cols), jnp.bfloat16)
    far_own, far_theirs = call(
        functools.partial(pair_kernel, tokens), "pair", (block_rows, block_rows), far_keys
    )
    far_theirs = swap(far_theirs)
    far_other = swap(gram(activations, far_theirs).astype(jnp.bfloat16))
    far_part = gram(activations, far_own)
    own_keys, partner_keys = call(
        functools.partial(keys_kernel, tokens), "keys", (near_rows, near_rows), key_grad
    )
    their_keys = swap(partner_keys)

    flat = jax.ShapeDtypeStruct((features, cols), jnp.float32)
    flat_half = jax.ShapeDtypeStruct((features, cols), jnp.bfloat16)
    high, low = cosine_parts()
    forward = jnp.asarray(np.concatenate([high, high, low], axis=1))
    backward = jnp.asarray(np.concatenate([high.T, high.T, low.T], axis=1))
    height = features // ROW_GROUPS
    lines = np.arange(cols)
    base = SPAN * (lines // (2 * block_ids.shape[3])) + lines % 2
    base = jnp.asarray(np.repeat(base[:, None], cols, axis=1).astype(np.float32))
    picks_shape = (2 * ROW_GROUPS * cols, height)
    mask, picks, numbers = call(
        routes_kernel,
        "routes",
        (
            flat_half,
            jax.ShapeDtypeStruct(picks_shape, jnp.bfloat16),
            jax.ShapeDtypeStruct((ROW_GROUPS * cols, cols), jnp.bfloat16),
        ),
        ids,
        counts,
        base,
        places=[SMEM, SMEM, VMEM],
    )

    most = block_ids.shape[3]
    span = lines // (2 * most)
    each = features // SPAN // ROW_GROUPS
    span_table = np.concatenate(
        [(span[:, None] + g * each == lines) & (span[:, None] < each) for g in range(ROW_GROUPS)]
    )
    slot_table = np.where(span < each, lines % (2 * most) // 2, most)
    slot_table = np.repeat(slot_table[:, None], cols, axis=1)
    far_whole, far_sent = call(
        far_kernel,
        "far",
        (flat_half, jax.ShapeDtypeStruct((ROW_GROUPS * cols, cols), jnp.bfloat16)),
        far_keys[2 * tokens :],
        counts,
        jnp.asarray(span_table.astype(np.float32).astype(ml_dtypes.bfloat16)),
        jnp.asarray(slot_table.astype(np.float32)),
        base,
        far_part,
        far_other,
        forward,
        places=[VMEM, SMEM] + [VMEM] * 6,
        scratch=(
            pltpu.VMEM(picks_shape, jnp.bfloat16),
            pltpu.VMEM((features, cols), jnp.bfloat16),
        ),
    )
    far_sent = along(far_sent, FAR)

    keys = jnp.concatenate([own_keys, their_keys], axis=1)
    keys = lax.optimization_barrier(keys.reshape(len(NEAR), tokens, 2 * cols))
    first, second = lax.optimization_barrier((first, second))
    near = gram(activations, keys[0]) + gram(first, keys[1]) + gram(second, keys[2])
    other, far_whole = lax.optimization_barrier(
        (near[:, cols:].astype(jnp.bfloat16), far_whole)
    )
    other, far_whole = swap(other), along(far_whole, FAR)
    part = near[:, :cols] + 0.999 * momentum[0]

    order = np.concatenate([np.arange(0, SPAN, 2), np.arange(1, SPAN, 2)])
    both_high, both_low = (np.kron(np.eye(2, dtype=p.dtype), p[order]) for p in (high, low))
    backward_pair = jnp.asarray(np.concatenate([both_high, both_high, both_low], axis=0))

    message = jax.ShapeDtypeStruct((ROW_GROUPS * cols, cols), jnp.bfloat16)
    advanced, sent = call(
        spectrum_kernel,
        "spectrum",
        (flat, message),
        part,
        other,
        far_sent,
        picks,
        numbers,
        forward,
        scratch=(pltpu.VMEM((features, cols), jnp.bfloat16),),
    )

    def exchange(x):
        return lax.all_to_all(
            x.reshape(replicas, OWN_COLS, x.shape[1]), "dp", 0, 0, tiled=True
        ).reshape(x.shape)

    pieces = exchange(sent)
    unpack = np.concatenate(
        [
            np.kron(np.eye(cols // OWN_COLS), np.outer(np.eye(OWN_COLS)[c], np.ones(OWN_COLS)))
            for c in range(OWN_COLS)
        ],
        axis=1,
    )
    (totals,) = call(
        total_kernel,
        "total",
        (jax.ShapeDtypeStruct((replicas * OWN_COLS, height), jnp.bfloat16),),
        pieces,
        jnp.asarray(unpack.astype(ml_dtypes.bfloat16)),
        backward_pair,
        scratch=(pltpu.VMEM((height, replicas * OWN_COLS), jnp.bfloat16),),
    )
    totals, far_whole = lax.optimization_barrier((totals, far_whole))
    (kept,) = call(kept_kernel, "kept", (flat,), advanced, far_whole, mask, forward, backward)
    (update,) = call(turn_kernel, "turn", (flat_half,), exchange(totals))
    return kept[None], update


def solution(mesh):
    in_specs = (
        P(("dp", "tensor"), None),
        P("dp", "tensor"),
        P("dp", None, "tensor"),
        P("dp", None, "tensor", None),
        P("dp"),
    )
    out_specs = (P("dp", None, "tensor"), P(None, "tensor"))
    body = functools.partial(shards, replicas=mesh.shape["dp"], group=mesh.shape["tensor"])
    return jax.shard_map(body, mesh=mesh, in_specs=in_specs, out_specs=out_specs, check_vma=False)
```
